256 devices in a mesh: freq: 32 (over y_lo, z, core), rcv: 8 (over x, y_hi).
Axes of the slice: x: 4, y: 4 (y_hi: 2, y_lo: 2; y = y_hi * 2 + y_lo), z: 8, core: 2. Of those that a mesh axis runs over, the one named last changes fastest.
Arguments:
- reflection: bfloat16 [2, 1024, 256, 1024], P(None, 'freq', 'rcv'), may hold values from -0.25 to 0.25
- plus_init: float32 [2, 1024, 12288], P(None, 'freq', 'rcv'), may hold values from -6 to 6
- onset_receiver: int32 [256, 12], P('rcv'), may hold values from 128 to 768
- onset_source: int32 [1024, 12], P('rcv'), may hold values from 128 to 768
Outputs:
- focus_minus: float32 [2, 1024, 3072], P(None, 'freq', 'rcv')
- focus_plus: float32 [2, 1024, 12288], P(None, 'freq', 'rcv')
The draws below stay inside these ranges and needn't reach their ends.
All inputs are finite; a program needn't handle non-finite values.
Results may differ from the reference program's by a relative error of at most 0.017.
Values may be sent and summed in bfloat16 or wider, within the bound.
A program may use at most 128 MiB of HBM per device.

```python
import jax
import jax.numpy as jnp
from jax import lax

NF = 1024
S = 1024
P_SIZE = 12
ITERS = 2
NT = 2048
M = 256


def touch_ends(entries, stream_key, least, high):
    extent = entries.shape
    spot = [jax.random.randint(jax.random.fold_in(stream_key, axis), (), 0, extent[axis]) for axis in range(len(extent))]
    entries = entries.at[tuple(spot)].set(least)
    longest = extent.index(max(extent))
    spot[longest] = (spot[longest] + 1) % extent[longest]
    return entries.at[tuple(spot)].set(high)


def steps_of(own_key, shape, cuts, least, high):
    loudness, own = 1.0, jax.random.fold_in(own_key, 6)
    for axis_at, blocks in cuts:
        steps = jnp.exp(jax.random.uniform(jax.random.fold_in(own, axis_at), (blocks,), jnp.float32, least / len(cuts), high / len(cuts)))
        loudness = loudness * jnp.repeat(steps, shape[axis_at] // blocks).reshape([-1 if axis == axis_at else 1 for axis in range(len(shape))])
    return loudness


def noise(own_key, shape, width, limit, cuts=(), kind=jnp.bfloat16):
    level = steps_of(own_key, shape, cuts, -0.22, 0.18) if cuts else 1.0
    values = jax.random.normal(own_key, shape, jnp.float32) * width * level
    return jnp.minimum(jnp.maximum(values, -limit), limit).astype(kind)


def setup_inputs(seed: int = 0) -> dict:
    keys = jax.random.split(jax.random.key(seed), 5)
    reflection = noise(keys[0], (2, NF, M, S), (0.9 * (S * M) ** -0.25), 0.25, ((1, 32), (2, 8)))
    plus_init = noise(keys[1], (2, NF, S * P_SIZE), 1.0, 6.0, ((1, 32), (2, 8)), jnp.float32)
    onset_receiver = touch_ends(jax.random.randint(keys[2], (M, P_SIZE), NT // 16, 3 * NT // 8 + 1), jax.random.fold_in(keys[2], 1), NT // 16, (3 * NT // 8 + 1) - 1).astype(jnp.int32)
    onset_source = touch_ends(jax.random.randint(keys[3], (S, P_SIZE), NT // 16, 3 * NT // 8 + 1), jax.random.fold_in(keys[3], 1), NT // 16, (3 * NT // 8 + 1) - 1).astype(jnp.int32)
    return {"reflection": reflection, "plus_init": plus_init, "onset_receiver": onset_receiver, "onset_source": onset_source}


def window_traces(spectrum, onsets):
    complex_part = spectrum[0] + 1j * spectrum[1]
    padded = jnp.concatenate([complex_part, jnp.zeros((1, complex_part.shape[1]), complex_part.dtype)], axis=0)
    signal = jnp.fft.irfft(padded, n=NT, axis=0)
    times = jnp.arange(NT, dtype=jnp.int32)[:, None]
    inside = (times < onsets[None, :]) | (times > NT - onsets[None, :])
    signal = jnp.where(inside, signal, jnp.zeros_like(signal))
    result = jnp.fft.rfft(signal, axis=0)[:NF]
    return jnp.stack([jnp.real(result), jnp.imag(result)]).astype(jnp.float32)


def apply_forward(reflection, plus_half):
    def one_freq(index):
        block = lax.dynamic_index_in_dim(reflection, index, 1, keepdims=False)
        sources = lax.dynamic_index_in_dim(plus_half, index, 1, keepdims=False).reshape(2, S, P_SIZE)
        stacked = jnp.concatenate([sources[0], sources[1]], axis=1)
        first_term = jnp.dot(block[0], stacked, preferred_element_type=jnp.float32)
        second_term = jnp.dot(block[1], stacked, preferred_element_type=jnp.float32)
        real_part = first_term[:, :P_SIZE] - second_term[:, P_SIZE:]
        imag_part = first_term[:, P_SIZE:] + second_term[:, :P_SIZE]
        return jnp.stack([real_part, imag_part]).reshape(2, M * P_SIZE)

    stacked_all = lax.map(one_freq, jnp.arange(NF, dtype=jnp.int32))
    return jnp.transpose(stacked_all, (1, 0, 2))


def apply_adjoint(reflection, minus_half):
    def one_freq(index):
        block = lax.dynamic_index_in_dim(reflection, index, 1, keepdims=False)
        traces = lax.dynamic_index_in_dim(minus_half, index, 1, keepdims=False).reshape(2, M, P_SIZE)
        stacked = jnp.concatenate([traces[0], traces[1]], axis=1)
        numbers = (((0,), (0,)), ((), ()))
        first_term = lax.dot_general(block[0], stacked, numbers, preferred_element_type=jnp.float32)
        second_term = lax.dot_general(block[1], stacked, numbers, preferred_element_type=jnp.float32)
        real_part = first_term[:, :P_SIZE] + second_term[:, P_SIZE:]
        imag_part = first_term[:, P_SIZE:] - second_term[:, :P_SIZE]
        return jnp.stack([real_part, imag_part]).reshape(2, S * P_SIZE)

    stacked_all = lax.map(one_freq, jnp.arange(NF, dtype=jnp.int32))
    return jnp.transpose(stacked_all, (1, 0, 2))


def reference(reflection, plus_init, onset_receiver, onset_source):
    flat_receiver = onset_receiver.reshape(M * P_SIZE)
    flat_source = onset_source.reshape(S * P_SIZE)
    plus = plus_init
    focus_minus = jnp.zeros((2, NF, M * P_SIZE), jnp.float32)
    for iteration in range(ITERS):
        plus_half = plus.astype(jnp.bfloat16)
        raw_minus = apply_forward(reflection, plus_half)
        focus_minus = window_traces(raw_minus, flat_receiver)
        minus_half = focus_minus.astype(jnp.bfloat16)
        backward = apply_adjoint(reflection, minus_half)
        plus = plus_init + window_traces(backward, flat_source)
    return focus_minus, plus
```

```python
import math

import jax
import jax.numpy as jnp
import numpy as np
from jax import lax
from jax.experimental import pallas as pl
from jax.experimental.pallas import tpu as pltpu
from jax.sharding import PartitionSpec as P

MESH = pl.DeviceIdType.MESH
PS = 12
ITERS = 2
FB = 32
NB = 32
NR = 8
GF = 8
NG = FB // GF
ROWS = 2 * PS * GF
ML = 32
SL = 128
NK = FB * NB
TW = 768
NQ = 3
WM = 2 * NQ
WP = 2 * PS
F32 = jnp.float32
BF16 = jnp.bfloat16


def tables():
    index = np.arange(NK)
    phases = (index[:, None] * index[None, :]) % (2 * NK)
    angles = phases * (2.0 * math.pi / (2 * NK))
    return np.stack([np.cos(angles), np.sin(angles)]).astype(np.float32)


def reorder_rows(start, rows, count):
    index = start + lax.broadcasted_iota(jnp.int32, (rows, 1), 0)
    item = (index * 43691) >> 19
    target = (index - PS * item) * count + item
    lane = lax.broadcasted_iota(jnp.int32, (rows, PS * count), 1)
    return jnp.where(lane == target, 1.0, 0.0).astype(BF16)


def spreading():
    row = lax.broadcasted_iota(jnp.int32, (4 * ML, 4 * GF * ML), 0)
    lane = lax.broadcasted_iota(jnp.int32, (4 * ML, 4 * GF * ML), 1)
    hit = (lane // (GF * ML) == row // ML) & (lax.rem(lane, ML) == lax.rem(row, ML))
    return jnp.where(hit, 1.0, 0.0).astype(BF16)


MINUS_AT = (0, 10, 20, 5, 26, 30)


def minus_device(w):
    at = jnp.int32(MINUS_AT[0])
    for role in range(1, WM):
        at = jnp.where(w == role, MINUS_AT[role], at)
    return at


def plus_device(w):
    return jnp.where(w < 16, 2 * w, 4 * (w - 16) + 1)


def kernel(
    refl_hbm, tab_hbm, plus_ref, onm_ref, onp_ref,
    out_minus, out_plus,
    refl, tab_full, tab, perm, perm_m, spread, pinit, psnd, gath, mraw, msnd, xm, ymsnd, ym, spread_out, psum_snd, psum_rcv, total,
    xsnd, xp, ypsnd, wp, eo,
    load_sem, gath_send, gath_recv, xm_send, xm_recv, ym_send, ym_recv, rs_send, rs_recv, xp_send, xp_recv,
    wp_send, wp_recv,
):
    me_f = lax.axis_index("freq")
    me_r = lax.axis_index("rcv")

    chip = me_f // 2
    core = lax.rem(me_f, 2)
    w_minus = jnp.int32(0)
    is_minus = me_f == MINUS_AT[0]
    for role in range(1, WM):
        w_minus = jnp.where(me_f == MINUS_AT[role], role, w_minus)
        is_minus = is_minus | (me_f == MINUS_AT[role])
    w_plus = jnp.where(core == 0, chip, 16 + chip // 2)
    is_plus = (core == 0) | (lax.rem(chip, 2) == 0)
    part = jnp.minimum(w_plus, WP - 1) // PS

    load_refl = pltpu.make_async_copy(refl_hbm, refl, load_sem.at[0])
    load_tab = pltpu.make_async_copy(tab_hbm.at[part], tab_full, load_sem.at[1])
    load_refl.start()
    load_tab.start()

    barrier = pltpu.get_barrier_semaphore()

    def greet_f(i, _):
        pl.semaphore_signal(
            barrier, inc=1, device_id={"freq": lax.rem(me_f + i, NB), "rcv": me_r}, device_id_type=MESH
        )
        return 0

    def greet_r(i, _):
        pl.semaphore_signal(
            barrier, inc=1, device_id={"freq": me_f, "rcv": lax.rem(me_r + i, NR)}, device_id_type=MESH
        )
        return 0

    lax.fori_loop(1, NB, greet_f, 0)
    lax.fori_loop(1, NR, greet_r, 0)

    row32 = lax.broadcasted_iota(jnp.int32, (FB, 128), 0)
    k_scale = jnp.where((row32 == 0) & (me_f == 0), 0.5, 1.0).astype(F32)

    def remote_f(src, dst, send, recv, to):
        return pltpu.make_async_remote_copy(
            src_ref=src, dst_ref=dst, send_sem=send, recv_sem=recv,
            device_id={"freq": to, "rcv": me_r}, device_id_type=MESH,
        )

    def remote_r(src, dst, send, recv, to):
        return pltpu.make_async_remote_copy(
            src_ref=src, dst_ref=dst, send_sem=send, recv_sem=recv,
            device_id={"freq": me_f, "rcv": to}, device_id_type=MESH,
        )

    def await_bytes(ref, sem):
        pltpu.make_async_copy(ref, ref, sem).wait()

    def send_plus(it, g):
        rows = pl.ds(pl.multiple_of(g * ROWS, ROWS), ROWS)
        gath[it, me_r, rows, :] = psnd[it, rows, :]

        def one(i, _):
            to = lax.rem(me_r + i, NR)
            remote_r(
                psnd.at[it, rows], gath.at[it, me_r, rows], gath_send.at[it], gath_recv.at[it, g], to
            ).start()
            return 0

        lax.fori_loop(1, NR, one, 0)

    def fill_perm(i, _):
        perm[pl.ds(pl.multiple_of(i * 128, 128), 128), :] = reorder_rows(i * 128, 128, SL)
        return 0

    lax.fori_loop(0, PS, fill_perm, 0)
    first = jnp.dot(plus_ref[...].astype(BF16), perm[...], preferred_element_type=F32)
    pl.semaphore_wait(barrier, NB - 1 + NR - 1)
    for g in range(NG):
        parts = [
            first[c * FB + g * GF : c * FB + (g + 1) * GF, p * SL : (p + 1) * SL]
            for c in range(2)
            for p in range(PS)
        ]
        psnd[0, g * ROWS : (g + 1) * ROWS, :] = jnp.concatenate(parts, axis=0).astype(BF16)
        send_plus(0, g)

    left = plus_ref[...] - plus_ref[...].astype(BF16).astype(F32)
    middle = left.astype(BF16)
    small = (left - middle.astype(F32)).astype(BF16)
    rest = jnp.dot(jnp.concatenate([middle, small], axis=0), perm[...], preferred_element_type=F32)
    exact = first + (rest[: 2 * FB] + rest[2 * FB :])
    for c in range(2):
        for p in range(PS):
            pinit[c * PS + p] = exact[c * FB : (c + 1) * FB, p * SL : (p + 1) * SL]

    spread[...] = spreading()
    perm_m[...] = reorder_rows(0, ML * PS, ML)
    load_tab.wait()

    def split_tab(i, _):
        rows = pl.ds(pl.multiple_of(i * 128, 128), 128)
        values = tab_full[rows, :]
        high = values.astype(BF16)
        tab[0, rows, :] = high
        tab[1, rows, :] = (values - high.astype(F32)).astype(BF16)
        return 0

    lax.fori_loop(0, NK // 128, split_tab, 0)
    load_refl.wait()

    def window(x, onsets, y, send_rows):
        step_t = 256

        def forward(i, _):
            rows = pl.ds(pl.multiple_of(i * step_t, step_t), step_t)
            values = x[...]
            in_time = jnp.dot(tab[0, rows, :], values, preferred_element_type=F32)
            in_time += jnp.dot(tab[1, rows, :], values, preferred_element_type=F32)
            time = i * step_t + lax.broadcasted_iota(jnp.int32, (step_t, 128), 0)
            factor = jnp.where(time == 0, 1.0 / NK, 2.0 / NK).astype(F32)
            in_time = jnp.where(time < onsets, in_time * factor, 0.0)
            high = in_time.astype(BF16)
            eo[rows, :128] = high
            eo[rows, 128:] = (in_time - high.astype(F32)).astype(BF16)
            return 0

        lax.fori_loop(0, TW // step_t, forward, 0)

        def back(i, _):
            rows = pl.ds(pl.multiple_of(i * step_t, step_t), step_t)
            both = jnp.dot(tab[0, rows, :TW], eo[...], preferred_element_type=F32)
            small = jnp.dot(tab[1, rows, :TW], eo[:, :128], preferred_element_type=F32)
            y[rows, :] = (both[:, :128] + (both[:, 128:] + small)).astype(BF16)
            send_rows(i, step_t // FB)
            return 0

        lax.fori_loop(0, NK // step_t, back, 0)

    def iteration(it, _):
        lane = lax.broadcasted_iota(jnp.int32, (ROWS // 2, 256), 1)
        row = lax.broadcasted_iota(jnp.int32, (ROWS // 2, 256), 0)
        same = lax.rem(row, GF) == lane // ML
        quad_lane = lax.broadcasted_iota(jnp.int32, (GF, 128), 1) // ML

        def forward(g, _):
            await_bytes(gath.at[it, pl.ds(0, NR - 1), pl.ds(0, ROWS)], gath_recv.at[it, g])
            rows = pl.ds(pl.multiple_of(g * ROWS, ROWS), ROWS)
            values = jnp.concatenate([gath[it, r, rows, :] for r in range(NR)], axis=1)
            dims = (((1,), (1,)), ((), ()))
            rows_re = pl.ds(pl.multiple_of(g * (GF * ML), GF * ML), GF * ML)
            rows_im = pl.ds(pl.multiple_of(FB * ML + g * (GF * ML), GF * ML), GF * ML)
            a = lax.dot_general(values, refl[rows_re, :], dims, preferred_element_type=F32)
            b = lax.dot_general(values, refl[rows_im, :], dims, preferred_element_type=F32)
            half = ROWS // 2
            parts = (a[:half] - b[half:], b[:half] + a[half:])
            for c in range(2):
                own = jnp.where(same, parts[c], 0.0)
                own = own[:, :128] + own[:, 128:]
                own = own + pltpu.roll(own, 64, 1)
                own = own + pltpu.roll(own, 32, 1)
                for q in range(NQ):
                    block = jnp.zeros((GF, 128), F32)
                    for i in range(4):
                        p = 4 * q + i
                        block = jnp.where(quad_lane == i, own[p * GF : (p + 1) * GF], block)
                    mraw[c * NQ + q, pl.ds(pl.multiple_of(g * GF, GF), GF), :] = block
            return 0

        lax.fori_loop(0, NG, forward, 0)

        my_rows = pl.ds(pl.multiple_of(me_f * FB, FB), FB)

        def send_minus(w, _):
            to = minus_device(w)
            msnd[it, w] = (mraw[w] * k_scale).astype(BF16)

            @pl.when(to == me_f)
            def _():
                xm[it, my_rows, :] = msnd[it, w]

            @pl.when(to != me_f)
            def _():
                remote_f(
                    msnd.at[it, w], xm.at[it, my_rows], xm_send.at[it], xm_recv.at[it], to
                ).start()

            return 0

        lax.fori_loop(0, WM, send_minus, 0)

        @pl.when(is_minus)
        def _():
            await_bytes(xm.at[it, pl.ds(0, NK - FB)], xm_recv.at[it])
            onsets = onm_ref[pl.ds(lax.rem(w_minus, NQ), 1), :]

            def send_rows(chunk, count):
                def one(i, _):
                    to = chunk * count + i
                    rows = pl.ds(pl.multiple_of(to * FB, FB), FB)

                    @pl.when(to == me_f)
                    def _():
                        ym[it, w_minus] = ymsnd[it, rows, :]

                    @pl.when(to != me_f)
                    def _():
                        remote_f(
                            ymsnd.at[it, rows], ym.at[it, w_minus], ym_send.at[it], ym_recv.at[it], to
                        ).start()

                    return 0

                lax.fori_loop(0, count, one, 0)

            window(xm.at[it], onsets, ymsnd.at[it], send_rows)

        @pl.when(is_minus)
        def _():
            await_bytes(ym.at[it, pl.ds(0, WM - 1)], ym_recv.at[it])

        @pl.when(jnp.logical_not(is_minus))
        def _():
            await_bytes(ym.at[it], ym_recv.at[it])

        wide = jnp.dot(ym[it].reshape(WM * FB, 128), spread[...], preferred_element_type=F32)
        row_s = lax.broadcasted_iota(jnp.int32, (WM * FB, 1024), 0)
        lane_s = lax.broadcasted_iota(jnp.int32, (WM * FB, 1024), 1)
        wide = jnp.where(lax.rem(row_s, GF) == lax.rem(lane_s // ML, GF), wide, 0.0)
        spread_out[...] = wide.reshape(WM, FB, 1024)

        def adjoint(g, _):
            frows = pl.ds(pl.multiple_of(g * GF, GF), GF)
            blocks = [spread_out[w, frows, :] for w in range(WM)]
            re = jnp.concatenate(
                [blocks[p // 4][:, (p % 4) * 256 : (p % 4 + 1) * 256] for p in range(PS)], axis=0
            )
            im = jnp.concatenate(
                [blocks[NQ + p // 4][:, (p % 4) * 256 : (p % 4 + 1) * 256] for p in range(PS)], axis=0
            )
            left = jnp.concatenate([re, im], axis=0).astype(BF16)
            right = jnp.concatenate([im, -re], axis=0).astype(BF16)
            rows_re = pl.ds(pl.multiple_of(g * (GF * ML), GF * ML), GF * ML)
            rows_im = pl.ds(pl.multiple_of(FB * ML + g * (GF * ML), GF * ML), GF * ML)
            rows = pl.ds(pl.multiple_of(g * ROWS, ROWS), ROWS)
            for n in range(4):
                cols = slice(n * 256, (n + 1) * 256)
                out = jnp.dot(left, refl[rows_re, cols], preferred_element_type=F32)
                out += jnp.dot(right, refl[rows_im, cols], preferred_element_type=F32)
                out = out.astype(BF16)
                psum_snd[it, 2 * n, rows, :] = out[:, :128]
                psum_snd[it, 2 * n + 1, rows, :] = out[:, 128:]
            psum_rcv[it, me_r, rows, :] = psum_snd[it, me_r, rows, :]

            def one(i, _):
                to = lax.rem(me_r + i, NR)
                remote_r(
                    psum_snd.at[it, to, rows], psum_rcv.at[it, me_r, rows], rs_send.at[it], rs_recv.at[it, g], to
                ).start()
                return 0

            lax.fori_loop(1, NR, one, 0)
            return 0

        lax.fori_loop(0, NG, adjoint, 0)

        def add_up(g, _):
            await_bytes(psum_rcv.at[it, pl.ds(0, NR - 1), pl.ds(0, ROWS)], rs_recv.at[it, g])
            rows = pl.ds(pl.multiple_of(g * ROWS, ROWS), ROWS)
            acc = psum_rcv[it, 0, rows, :].astype(F32)
            for r in range(1, NR):
                acc += psum_rcv[it, r, rows, :].astype(F32)
            total[:, pl.ds(pl.multiple_of(g * GF, GF), GF), :] = acc.reshape(WP, GF, SL)
            return 0

        lax.fori_loop(0, NG, add_up, 0)

        def send_total(w, _):
            to = plus_device(w)
            xsnd[it, w] = (total[w] * k_scale).astype(BF16)

            @pl.when(to == me_f)
            def _():
                xp[it, my_rows, :] = xsnd[it, w]

            @pl.when(to != me_f)
            def _():
                remote_f(
                    xsnd.at[it, w], xp.at[it, my_rows], xp_send.at[it], xp_recv.at[it], to
                ).start()

            return 0

        lax.fori_loop(0, WP, send_total, 0)

        @pl.when(is_plus)
        def _():
            await_bytes(xp.at[it, pl.ds(0, NK - FB)], xp_recv.at[it])
            onsets = onp_ref[pl.ds(lax.rem(w_plus, PS), 1), :]

            def send_rows(chunk, count):
                def one(i, _):
                    to = chunk * count + i
                    rows = pl.ds(pl.multiple_of(to * FB, FB), FB)

                    @pl.when(to == me_f)
                    def _():
                        wp[it, w_plus] = ypsnd[it, rows, :]

                    @pl.when(to != me_f)
                    def _():
                        remote_f(
                            ypsnd.at[it, rows], wp.at[it, w_plus], wp_send.at[it], wp_recv.at[it], to
                        ).start()

                    return 0

                lax.fori_loop(0, count, one, 0)

            window(xp.at[it], onsets, ypsnd.at[it], send_rows)

        @pl.when(is_plus)
        def _():
            await_bytes(wp.at[it, pl.ds(0, WP - 1)], wp_recv.at[it])

        @pl.when(jnp.logical_not(is_plus))
        def _():
            await_bytes(wp.at[it], wp_recv.at[it])

        @pl.when(it < ITERS - 1)
        def _():
            def update(g, _):
                frows = pl.ds(pl.multiple_of(g * GF, GF), GF)
                rows = pl.ds(pl.multiple_of(g * ROWS, ROWS), ROWS)
                total[...] = wp[it].astype(F32)
                new = pinit[:, frows, :] + total[:, frows, :]
                psnd[it + 1, rows, :] = new.reshape(ROWS, SL).astype(BF16)
                send_plus(it + 1, g)
                return 0

            lax.fori_loop(0, NG, update, 0)

        return 0

    lax.fori_loop(0, ITERS, iteration, 0)

    last = ITERS - 1
    dims = (((1,), (1,)), ((), ()))
    minus = jnp.concatenate(
        [jnp.concatenate([ym[last, c * NQ + q] for q in range(NQ)], axis=1) for c in range(2)], axis=0
    )
    out_minus[...] = lax.dot_general(minus, perm_m[...], dims, preferred_element_type=F32)
    change = jnp.concatenate(
        [jnp.concatenate([wp[last, c * PS + p] for p in range(PS)], axis=1) for c in range(2)], axis=0
    )
    out_plus[...] = plus_ref[...] + lax.dot_general(change, perm[...], dims, preferred_element_type=F32)

    def drain(it, _):
        await_bytes(gath.at[it, pl.ds(0, NR - 1)], gath_send.at[it])
        await_bytes(gath.at[it, pl.ds(0, NR - 1)], rs_send.at[it])

        @pl.when(is_minus)
        def _():
            await_bytes(msnd.at[it, pl.ds(0, WM - 1)], xm_send.at[it])
            await_bytes(ymsnd.at[it, pl.ds(0, NK - FB)], ym_send.at[it])

        @pl.when(jnp.logical_not(is_minus))
        def _():
            await_bytes(msnd.at[it], xm_send.at[it])

        @pl.when(is_plus)
        def _():
            await_bytes(xsnd.at[it, pl.ds(0, WP - 1)], xp_send.at[it])
            await_bytes(ypsnd.at[it, pl.ds(0, NK - FB)], wp_send.at[it])

        @pl.when(jnp.logical_not(is_plus))
        def _():
            await_bytes(xsnd.at[it], xp_send.at[it])

        return 0

    lax.fori_loop(0, ITERS, drain, 0)


def local(reflection, plus_init, onset_receiver, onset_source):
    onm = jnp.transpose(onset_receiver).reshape(NQ, 4 * ML)
    onp = jnp.transpose(onset_source)
    vmem = pl.BlockSpec(memory_space=pltpu.VMEM)
    hbm = pl.BlockSpec(memory_space=pl.ANY)
    dma = pltpu.SemaphoreType.DMA
    out_minus, out_plus = pl.pallas_call(
        kernel,
        out_shape=(
            jax.ShapeDtypeStruct((2 * FB, ML * PS), F32),
            jax.ShapeDtypeStruct((2 * FB, SL * PS), F32),
        ),
        in_specs=[hbm, hbm, vmem, vmem, vmem],
        out_specs=(vmem, vmem),
        scratch_shapes=[
            pltpu.VMEM((2 * FB * ML, 1024), BF16),
            pltpu.VMEM((NK, NK), F32),
            pltpu.VMEM((2, NK, NK), BF16),
            pltpu.VMEM((SL * PS, SL * PS), BF16),
            pltpu.VMEM((ML * PS, ML * PS), BF16),
            pltpu.VMEM((4 * ML, 4 * GF * ML), BF16),
            pltpu.VMEM((WP, FB, SL), F32),
            pltpu.VMEM((ITERS, NG * ROWS, SL), BF16),
            pltpu.VMEM((ITERS, NR, NG * ROWS, SL), BF16),
            pltpu.VMEM((WM, FB, 128), F32),
            pltpu.VMEM((ITERS, WM, FB, 128), BF16),
            pltpu.VMEM((ITERS, NK, 128), BF16),
            pltpu.VMEM((ITERS, NK, 128), BF16),
            pltpu.VMEM((ITERS, WM, FB, 128), BF16),
            pltpu.VMEM((WM, FB, 1024), F32),
            pltpu.VMEM((ITERS, NR, NG * ROWS, SL), BF16),
            pltpu.VMEM((ITERS, NR, NG * ROWS, SL), BF16),
            pltpu.VMEM((WP, FB, SL), F32),
            pltpu.VMEM((ITERS, WP, FB, SL), BF16),
            pltpu.VMEM((ITERS, NK, SL), BF16),
            pltpu.VMEM((ITERS, NK, SL), BF16),
            pltpu.VMEM((ITERS, WP, FB, SL), BF16),
            pltpu.VMEM((TW, 256), BF16),
            dma((2,)),
            dma((ITERS,)), dma((ITERS, NG)),
            dma((ITERS,)), dma((ITERS,)),
            dma((ITERS,)), dma((ITERS,)),
            dma((ITERS,)), dma((ITERS, NG)),
            dma((ITERS,)), dma((ITERS,)),
            dma((ITERS,)), dma((ITERS,)),
        ],
        compiler_params=pltpu.CompilerParams(
            collective_id=0, has_side_effects=True, vmem_limit_bytes=56 * 1024 * 1024
        ),
    )(
        reflection.reshape(2 * FB * ML, 1024),
        jnp.asarray(tables()),
        plus_init.reshape(2 * FB, SL * PS),
        onm,
        onp,
    )
    return out_minus.reshape(2, FB, ML * PS), out_plus.reshape(2, FB, SL * PS)


def solution(mesh):
    return jax.shard_map(
        local,
        mesh=mesh,
        in_specs=(
            P(None, "freq", "rcv", None),
            P(None, "freq", "rcv"),
            P("rcv", None),
            P("rcv", None),
        ),
        out_specs=(P(None, "freq", "rcv"), P(None, "freq", "rcv")),
        check_vma=False,
    )
```

```python
import math

import jax
import jax.numpy as jnp
import numpy as np
from jax import lax
from jax.experimental import pallas as pl
from jax.experimental.pallas import tpu as pltpu
from jax.sharding import PartitionSpec as P

MESH = pl.DeviceIdType.MESH
PS = 12
ITERS = 2
FB = 32
NB = 32
NR = 8
GF = 8
NG = FB // GF
ROWS = 2 * 4 * GF
ML = 32
SL = 128
NK = FB * NB
TW = 768
NQ = 3
WM = 2 * NQ
WP = 2 * PS
F32 = jnp.float32
BF16 = jnp.bfloat16


def tables():
    index = np.arange(NK)
    phases = (index[:, None] * index[None, :]) % (2 * NK)
    angles = phases * (2.0 * math.pi / (2 * NK))
    return np.stack([np.cos(angles), np.sin(angles)]).astype(np.float32)


def reorder_rows(start, rows, count):
    index = start + lax.broadcasted_iota(jnp.int32, (rows, 1), 0)
    item = (index * 43691) >> 19
    target = (index - PS * item) * count + item
    lane = lax.broadcasted_iota(jnp.int32, (rows, PS * count), 1)
    return jnp.where(lane == target, 1.0, 0.0).astype(BF16)


def spreading():
    row = lax.broadcasted_iota(jnp.int32, (4 * ML, 4 * GF * ML), 0)
    lane = lax.broadcasted_iota(jnp.int32, (4 * ML, 4 * GF * ML), 1)
    hit = (lane // (GF * ML) == row // ML) & (lax.rem(lane, ML) == lax.rem(row, ML))
    return jnp.where(hit, 1.0, 0.0).astype(BF16)


MINUS_AT = ((3, 11, 5), (25, 17, 31))
PLUS_AT = (
    (0, 4, 8, 12, 2, 6, 10, 14, 1, 7, 9, 15),
    (18, 22, 26, 30, 16, 20, 24, 28, 19, 21, 27, 29),
)


def kernel(
    refl_hbm, tab_hbm, plus_ref, onm_ref, onp_ref,
    out_minus, out_plus,
    refl, tab_full, tab, perm, perm_m, spread, pinit, psnd, gath, msnd, xm, ymsnd, ym, wide, psum_snd, psum_rcv,
    xsnd, xp, ypsnd, wp, eo,
    load_sem, gath_send, gath_recv, xm_send, xm_recv, ym_send, ym_recv, rs_send, rs_recv, xp_send, xp_recv,
    wp_send, wp_recv,
):
    me_f = lax.axis_index("freq")
    me_r = lax.axis_index("rcv")
    part = me_f // (NB // 2)

    load_refl = pltpu.make_async_copy(refl_hbm, refl, load_sem.at[0])
    load_tab = pltpu.make_async_copy(tab_hbm.at[part], tab_full, load_sem.at[1])
    load_refl.start()
    load_tab.start()

    barrier = pltpu.get_barrier_semaphore()

    def greet_f(i, _):
        pl.semaphore_signal(
            barrier, inc=1, device_id={"freq": lax.rem(me_f + i, NB), "rcv": me_r}, device_id_type=MESH
        )
        return 0

    def greet_r(i, _):
        pl.semaphore_signal(
            barrier, inc=1, device_id={"freq": me_f, "rcv": lax.rem(me_r + i, NR)}, device_id_type=MESH
        )
        return 0

    lax.fori_loop(1, NB, greet_f, 0)
    lax.fori_loop(1, NR, greet_r, 0)

    row32 = lax.broadcasted_iota(jnp.int32, (FB, 128), 0)
    k_scale = jnp.where((row32 == 0) & (me_f == 0), 0.5, 1.0).astype(F32)
    my_rows = pl.ds(pl.multiple_of(me_f * FB, FB), FB)

    def remote_f(src, dst, send, recv, to):
        return pltpu.make_async_remote_copy(
            src_ref=src, dst_ref=dst, send_sem=send, recv_sem=recv,
            device_id={"freq": to, "rcv": me_r}, device_id_type=MESH,
        )

    def remote_r(src, dst, send, recv, to):
        return pltpu.make_async_remote_copy(
            src_ref=src, dst_ref=dst, send_sem=send, recv_sem=recv,
            device_id={"freq": me_f, "rcv": to}, device_id_type=MESH,
        )

    def await_bytes(ref, sem):
        pltpu.make_async_copy(ref, ref, sem).wait()

    def any_of(places):
        found = me_f == places[0]
        for place in places[1:]:
            found = found | (me_f == place)
        return found

    def minus_places(q):
        return [MINUS_AT[c][q] for c in range(2)]

    def plus_places(q):
        return [PLUS_AT[c][4 * q + i] for c in range(2) for i in range(4)]

    def send_plus(it, q):
        gath[it, q, me_r] = psnd[it, q]

        def one(i, _):
            to = lax.rem(me_r + i, NR)
            remote_r(psnd.at[it, q], gath.at[it, q, me_r], gath_send.at[it], gath_recv.at[it, q], to).start()
            return 0

        lax.fori_loop(1, NR, one, 0)

    def fill_perm(i, _):
        perm[pl.ds(pl.multiple_of(i * 128, 128), 128), :] = reorder_rows(i * 128, 128, SL)
        return 0

    lax.fori_loop(0, PS, fill_perm, 0)
    high = plus_ref[...].astype(BF16)
    left = plus_ref[...] - high.astype(F32)
    middle = left.astype(BF16)
    small = (left - middle.astype(F32)).astype(BF16)
    split = jnp.dot(jnp.concatenate([high, middle, small], axis=0), perm[...], preferred_element_type=F32)
    first = split[: 2 * FB]
    for q in range(NQ):
        for g in range(NG):
            parts = [
                first[c * FB + g * GF : c * FB + (g + 1) * GF, p * SL : (p + 1) * SL]
                for c in range(2)
                for p in range(4 * q, 4 * q + 4)
            ]
            psnd[0, q, g * ROWS : (g + 1) * ROWS, :] = jnp.concatenate(parts, axis=0).astype(BF16)
    pl.semaphore_wait(barrier, NB - 1 + NR - 1)
    for q in range(NQ):
        send_plus(0, q)

    exact = first + (split[2 * FB : 4 * FB] + split[4 * FB :])
    for c in range(2):
        for p in range(PS):
            pinit[p // 4, c * 4 + p % 4] = exact[c * FB : (c + 1) * FB, p * SL : (p + 1) * SL]

    spread[...] = spreading()
    perm_m[...] = reorder_rows(0, ML * PS, ML)
    load_tab.wait()

    def split_tab(i, _):
        rows = pl.ds(pl.multiple_of(i * 128, 128), 128)
        values = tab_full[rows, :]
        top = values.astype(BF16)
        tab[0, rows, :] = top
        tab[1, rows, :] = (values - top.astype(F32)).astype(BF16)
        return 0

    lax.fori_loop(0, NK // 128, split_tab, 0)
    load_refl.wait()

    def window(x, onsets, y, send_chunk):
        until = jnp.transpose(jnp.broadcast_to(onsets, (128, 128)))
        until = jnp.concatenate([until, until], axis=1)
        traces = jnp.transpose(x[...])
        for n in range(TW // 256):
            cols = slice(n * 256, (n + 1) * 256)
            in_time = jnp.dot(traces, tab[0, :, cols], preferred_element_type=F32)
            in_time += jnp.dot(traces, tab[1, :, cols], preferred_element_type=F32)
            time = n * 256 + lax.broadcasted_iota(jnp.int32, (128, 256), 1)
            factor = jnp.where(time == 0, 1.0 / NK, 2.0 / NK).astype(F32)
            in_time = jnp.where(time < until, in_time * factor, 0.0)
            top = in_time.astype(BF16)
            eo[:128, cols] = top
            eo[128:, cols] = (in_time - top.astype(F32)).astype(BF16)
        for n in range(NK // 256):
            cols = slice(n * 256, (n + 1) * 256)
            both = jnp.dot(eo[...], tab[0, :TW, cols], preferred_element_type=F32)
            small = jnp.dot(eo[:128, :], tab[1, :TW, cols], preferred_element_type=F32)
            y[cols, :] = jnp.transpose(both[:128] + (both[128:] + small)).astype(BF16)
            send_chunk(n * (256 // FB), 256 // FB)

    half = ROWS // 2
    lane = lax.broadcasted_iota(jnp.int32, (half, GF * ML), 1)
    row = lax.broadcasted_iota(jnp.int32, (half, GF * ML), 0)
    same = lax.rem(row, GF) == lane // ML
    quad_lane = lax.broadcasted_iota(jnp.int32, (GF, 128), 1) // ML

    def refl_rows(c, g):
        return slice(c * FB * ML + g * GF * ML, c * FB * ML + (g + 1) * GF * ML)

    def forward(it, q):
        await_bytes(gath.at[it, q, pl.ds(0, NR - 1)], gath_recv.at[it, q])
        dims = (((1,), (1,)), ((), ()))
        blocks = ([], [])
        for g in range(NG):
            rows = slice(g * ROWS, (g + 1) * ROWS)
            values = jnp.concatenate([gath[it, q, r, rows, :] for r in range(NR)], axis=1)
            a = lax.dot_general(values, refl[refl_rows(0, g), :], dims, preferred_element_type=F32)
            b = lax.dot_general(values, refl[refl_rows(1, g), :], dims, preferred_element_type=F32)
            parts = (a[:half] - b[half:], b[:half] + a[half:])
            for c in range(2):
                own = jnp.where(same, parts[c], 0.0)
                own = own[:, :128] + own[:, 128:]
                own = own + pltpu.roll(own, 64, 1)
                own = own + pltpu.roll(own, 32, 1)
                block = jnp.zeros((GF, 128), F32)
                for i in range(4):
                    block = jnp.where(quad_lane == i, own[i * GF : (i + 1) * GF], block)
                blocks[c].append(block)
        for c in range(2):
            to = MINUS_AT[c][q]
            msnd[it, q, c] = (jnp.concatenate(blocks[c], axis=0) * k_scale).astype(BF16)

            @pl.when(me_f == to)
            def _():
                xm[it, my_rows, :] = msnd[it, q, c]

            @pl.when(me_f != to)
            def _():
                remote_f(msnd.at[it, q, c], xm.at[it, my_rows], xm_send.at[it], xm_recv.at[it], to).start()

    def scatter(it, buffer, dst, send, recv):
        def send_chunk(begin, count):
            def one(i, _):
                to = begin + i
                rows = pl.ds(pl.multiple_of(to * FB, FB), FB)

                @pl.when(to == me_f)
                def _():
                    dst[...] = buffer[it, rows, :]

                @pl.when(to != me_f)
                def _():
                    remote_f(buffer.at[it, rows], dst, send, recv, to).start()

                return 0

            lax.fori_loop(0, count, one, 0)

        return send_chunk

    def window_minus(it, q):
        @pl.when(any_of(minus_places(q)))
        def _():
            await_bytes(xm.at[it, pl.ds(0, NK - FB)], xm_recv.at[it])
            onsets = jnp.concatenate([onm_ref[4 * q + i : 4 * q + i + 1, :] for i in range(4)], axis=1)
            send_chunk = scatter(it, ymsnd, ym.at[it, q, part], ym_send.at[it], ym_recv.at[it, q])
            window(xm.at[it], onsets, ymsnd.at[it], send_chunk)

    def adjoint(it, q):
        here = any_of(minus_places(q))

        @pl.when(here)
        def _():
            await_bytes(ym.at[it, q, pl.ds(0, 1)], ym_recv.at[it, q])

        @pl.when(jnp.logical_not(here))
        def _():
            await_bytes(ym.at[it, q], ym_recv.at[it, q])

        spread_rows = jnp.dot(ym[it, q].reshape(2 * FB, 128), spread[...], preferred_element_type=F32)
        row_s = lax.broadcasted_iota(jnp.int32, (2 * FB, 1024), 0)
        lane_s = lax.broadcasted_iota(jnp.int32, (2 * FB, 1024), 1)
        wide[...] = jnp.where(lax.rem(row_s, GF) == lax.rem(lane_s // ML, GF), spread_rows, 0.0)
        for g in range(NG):
            blocks = [wide[c * FB + g * GF : c * FB + (g + 1) * GF, :] for c in range(2)]
            re, im = [
                jnp.concatenate([block[:, i * 256 : (i + 1) * 256] for i in range(4)], axis=0) for block in blocks
            ]
            left = jnp.concatenate([re, im], axis=0).astype(BF16)
            right = jnp.concatenate([im, -re], axis=0).astype(BF16)
            for n in range(4):
                cols = slice(n * 256, (n + 1) * 256)
                out = jnp.dot(left, refl[refl_rows(0, g), cols], preferred_element_type=F32)
                out += jnp.dot(right, refl[refl_rows(1, g), cols], preferred_element_type=F32)
                out = out.astype(BF16)
                psum_snd[it, q, 2 * n, g * ROWS : (g + 1) * ROWS, :] = out[:, :128]
                psum_snd[it, q, 2 * n + 1, g * ROWS : (g + 1) * ROWS, :] = out[:, 128:]
        psum_rcv[it, q, me_r] = psum_snd[it, q, me_r]

        def one(i, _):
            to = lax.rem(me_r + i, NR)
            remote_r(
                psum_snd.at[it, q, to], psum_rcv.at[it, q, me_r], rs_send.at[it], rs_recv.at[it, q], to
            ).start()
            return 0

        lax.fori_loop(1, NR, one, 0)

    def add_up(it, q):
        await_bytes(psum_rcv.at[it, q, pl.ds(0, NR - 1)], rs_recv.at[it, q])
        total = psum_rcv[it, q, 0].astype(F32)
        for r in range(1, NR):
            total += psum_rcv[it, q, r].astype(F32)
        for c in range(2):
            for i in range(4):
                to = PLUS_AT[c][4 * q + i]
                at = c * 4 + i
                block = jnp.concatenate(
                    [total[g * ROWS + at * GF : g * ROWS + (at + 1) * GF] for g in range(NG)], axis=0
                )
                xsnd[it, q, at] = (block * k_scale).astype(BF16)

                @pl.when(me_f == to)
                def _():
                    xp[it, my_rows, :] = xsnd[it, q, at]

                @pl.when(me_f != to)
                def _():
                    remote_f(xsnd.at[it, q, at], xp.at[it, my_rows], xp_send.at[it], xp_recv.at[it], to).start()

    def window_plus(it, q):
        @pl.when(any_of(plus_places(q)))
        def _():
            await_bytes(xp.at[it, pl.ds(0, NK - FB)], xp_recv.at[it])
            point = jnp.int32(0)
            for i in range(1, 4):
                point = jnp.where(any_of([PLUS_AT[c][4 * q + i] for c in range(2)]), i, point)
            onsets = onp_ref[pl.ds(4 * q + point, 1), :]
            send_chunk = scatter(it, ypsnd, wp.at[it, q, part * 4 + point], wp_send.at[it], wp_recv.at[it, q])
            window(xp.at[it], onsets, ypsnd.at[it], send_chunk)

    def update(it, q):
        here = any_of(plus_places(q))

        @pl.when(here)
        def _():
            await_bytes(wp.at[it, q, pl.ds(0, 7)], wp_recv.at[it, q])

        @pl.when(jnp.logical_not(here))
        def _():
            await_bytes(wp.at[it, q], wp_recv.at[it, q])

        @pl.when(it < ITERS - 1)
        def _():
            new = pinit[q] + wp[it, q].astype(F32)
            for g in range(NG):
                rows = new[:, g * GF : (g + 1) * GF, :].reshape(ROWS, SL)
                psnd[it + 1, q, g * ROWS : (g + 1) * ROWS, :] = rows.astype(BF16)
            send_plus(it + 1, q)

        @pl.when(it == ITERS - 1)
        def _():
            change = jnp.concatenate(
                [jnp.concatenate([wp[it, q, c * 4 + i] for i in range(4)], axis=1) for c in range(2)], axis=0
            )
            dims = (((1,), (1,)), ((), ()))
            change = lax.dot_general(
                change, perm[:, q * 4 * SL : (q + 1) * 4 * SL], dims, preferred_element_type=F32
            )
            before = plus_ref if q == 0 else out_plus
            out_plus[...] = before[...] + change

    def finish_minus(it):
        @pl.when(it == ITERS - 1)
        def _():
            minus = jnp.concatenate(
                [jnp.concatenate([ym[it, q, c] for q in range(NQ)], axis=1) for c in range(2)], axis=0
            )
            dims = (((1,), (1,)), ((), ()))
            out_minus[...] = lax.dot_general(minus, perm_m[...], dims, preferred_element_type=F32)

    def iteration(it, _):
        forward(it, 0)
        window_minus(it, 0)
        forward(it, 1)
        window_minus(it, 1)
        forward(it, 2)
        adjoint(it, 0)
        window_minus(it, 2)
        adjoint(it, 1)
        adjoint(it, 2)
        add_up(it, 0)
        finish_minus(it)
        add_up(it, 1)
        window_plus(it, 0)
        add_up(it, 2)
        window_plus(it, 1)
        update(it, 0)
        window_plus(it, 2)
        update(it, 1)
        update(it, 2)
        return 0

    lax.fori_loop(0, ITERS, iteration, 0)

    is_minus = any_of([place for q in range(NQ) for place in minus_places(q)])
    is_plus = any_of([place for q in range(NQ) for place in plus_places(q)])

    def drain(it, _):
        await_bytes(gath.at[it, :, pl.ds(0, NR - 1)], gath_send.at[it])
        await_bytes(gath.at[it, :, pl.ds(0, NR - 1)], rs_send.at[it])

        @pl.when(is_minus)
        def _():
            await_bytes(xm.at[it, pl.ds(0, (WM - 1) * FB)], xm_send.at[it])
            await_bytes(ymsnd.at[it, pl.ds(0, NK - FB)], ym_send.at[it])

        @pl.when(jnp.logical_not(is_minus))
        def _():
            await_bytes(msnd.at[it], xm_send.at[it])

        @pl.when(is_plus)
        def _():
            await_bytes(xp.at[it, pl.ds(0, (WP - 1) * FB)], xp_send.at[it])
            await_bytes(ypsnd.at[it, pl.ds(0, NK - FB)], wp_send.at[it])

        @pl.when(jnp.logical_not(is_plus))
        def _():
            await_bytes(xsnd.at[it], xp_send.at[it])

        return 0

    lax.fori_loop(0, ITERS, drain, 0)


def local(reflection, plus_init, onset_receiver, onset_source):
    onm = jnp.transpose(onset_receiver)
    onp = jnp.transpose(onset_source)
    vmem = pl.BlockSpec(memory_space=pltpu.VMEM)
    hbm = pl.BlockSpec(memory_space=pl.ANY)
    dma = pltpu.SemaphoreType.DMA
    out_minus, out_plus = pl.pallas_call(
        kernel,
        out_shape=(
            jax.ShapeDtypeStruct((2 * FB, ML * PS), F32),
            jax.ShapeDtypeStruct((2 * FB, SL * PS), F32),
        ),
        in_specs=[hbm, hbm, vmem, vmem, vmem],
        out_specs=(vmem, vmem),
        scratch_shapes=[
            pltpu.VMEM((2 * FB * ML, 1024), BF16),
            pltpu.VMEM((NK, NK), F32),
            pltpu.VMEM((2, NK, NK), BF16),
            pltpu.VMEM((SL * PS, SL * PS), BF16),
            pltpu.VMEM((ML * PS, ML * PS), BF16),
            pltpu.VMEM((4 * ML, 4 * GF * ML), BF16),
            pltpu.VMEM((NQ, 8, FB, SL), F32),
            pltpu.VMEM((ITERS, NQ, NG * ROWS, SL), BF16),
            pltpu.VMEM((ITERS, NQ, NR, NG * ROWS, SL), BF16),
            pltpu.VMEM((ITERS, NQ, 2, FB, 128), BF16),
            pltpu.VMEM((ITERS, NK, 128), BF16),
            pltpu.VMEM((ITERS, NK, 128), BF16),
            pltpu.VMEM((ITERS, NQ, 2, FB, 128), BF16),
            pltpu.VMEM((2 * FB, 1024), F32),
            pltpu.VMEM((ITERS, NQ, NR, NG * ROWS, SL), BF16),
            pltpu.VMEM((ITERS, NQ, NR, NG * ROWS, SL), BF16),
            pltpu.VMEM((ITERS, NQ, 8, FB, SL), BF16),
            pltpu.VMEM((ITERS, NK, SL), BF16),
            pltpu.VMEM((ITERS, NK, SL), BF16),
            pltpu.VMEM((ITERS, NQ, 8, FB, SL), BF16),
            pltpu.VMEM((256, TW), BF16),
            dma((2,)),
            dma((ITERS,)), dma((ITERS, NQ)),
            dma((ITERS,)), dma((ITERS,)),
            dma((ITERS,)), dma((ITERS, NQ)),
            dma((ITERS,)), dma((ITERS, NQ)),
            dma((ITERS,)), dma((ITERS,)),
            dma((ITERS,)), dma((ITERS, NQ)),
        ],
        compiler_params=pltpu.CompilerParams(
            collective_id=0, has_side_effects=True, vmem_limit_bytes=56 * 1024 * 1024
        ),
    )(
        reflection.reshape(2 * FB * ML, 1024),
        jnp.asarray(tables()),
        plus_init.reshape(2 * FB, SL * PS),
        onm,
        onp,
    )
    return out_minus.reshape(2, FB, ML * PS), out_plus.reshape(2, FB, SL * PS)


def solution(mesh):
    return jax.shard_map(
        local,
        mesh=mesh,
        in_specs=(
            P(None, "freq", "rcv", None),
            P(None, "freq", "rcv"),
            P("rcv", None),
            P("rcv", None),
        ),
        out_specs=(P(None, "freq", "rcv"), P(None, "freq", "rcv")),
        check_vma=False,
    )
```

```python
import math

import jax
import jax.numpy as jnp
import numpy as np
from jax import lax
from jax.experimental import pallas as pl
from jax.experimental.pallas import tpu as pltpu
from jax.sharding import PartitionSpec as P

MESH = pl.DeviceIdType.MESH
PS = 12
ITERS = 2
FB = 32
NB = 32
NR = 8
NX = 4
GF = 8
NG = FB // GF
ROWS = 2 * 4 * GF
HALF = NG * ROWS // 2
ML = 32
SL = 128
NK = FB * NB
TW = 768
NQ = 3
WM = 2 * NQ
WP = 2 * PS
F32 = jnp.float32
BF16 = jnp.bfloat16


def tables():
    index = np.arange(NK)
    phases = (index[:, None] * index[None, :]) % (2 * NK)
    angles = phases * (2.0 * math.pi / (2 * NK))
    return np.stack([np.cos(angles), np.sin(angles)]).astype(np.float32)


def reorder_rows(start, rows, count):
    index = start + lax.broadcasted_iota(jnp.int32, (rows, 1), 0)
    item = (index * 43691) >> 19
    target = (index - PS * item) * count + item
    lane = lax.broadcasted_iota(jnp.int32, (rows, PS * count), 1)
    return jnp.where(lane == target, 1.0, 0.0).astype(BF16)


def spreading():
    row = lax.broadcasted_iota(jnp.int32, (4 * ML, 4 * GF * ML), 0)
    lane = lax.broadcasted_iota(jnp.int32, (4 * ML, 4 * GF * ML), 1)
    hit = (lane // (GF * ML) == row // ML) & (lax.rem(lane, ML) == lax.rem(row, ML))
    return jnp.where(hit, 1.0, 0.0).astype(BF16)


MINUS_AT = ((3, 11, 5), (25, 17, 31))
PLUS_AT = (
    (0, 4, 8, 12, 2, 6, 10, 14, 1, 7, 9, 15),
    (18, 22, 26, 30, 16, 20, 24, 28, 19, 21, 27, 29),
)


def kernel(
    refl_hbm, tab_hbm, plus_ref, onm_ref, onp_ref,
    out_minus, out_plus,
    refl, tab_full, tab, perm, perm_m, spread, pinit, psnd, gath, msnd, xm, ymsnd, ym, wide,
    part_a, part_b, from_x, from_y, sum_a, sum_b, rest_a, rest_b, xsnd, xp, ypsnd, wp, eo,
    load_sem, gath_send, gath_recv, xm_send, xm_recv, ym_send, ym_recv, rs_send, rs_recv, xp_send, xp_recv,
    wp_send, wp_recv,
):
    me_f = lax.axis_index("freq")
    me_r = lax.axis_index("rcv")
    part = me_f // (NB // 2)
    me_x, me_y = me_r // 2, lax.rem(me_r, 2)
    beside = me_x * 2 + (1 - me_y)

    def along_x(i):
        return lax.rem(me_x + i, NX)


    load_refl = pltpu.make_async_copy(refl_hbm, refl, load_sem.at[0])
    load_tab = pltpu.make_async_copy(tab_hbm.at[part], tab_full, load_sem.at[1])
    load_refl.start()
    load_tab.start()

    barrier = pltpu.get_barrier_semaphore()

    def greet_f(i, _):
        pl.semaphore_signal(
            barrier, inc=1, device_id={"freq": lax.rem(me_f + i, NB), "rcv": me_r}, device_id_type=MESH
        )
        return 0

    def greet_r(i, _):
        pl.semaphore_signal(
            barrier, inc=1, device_id={"freq": me_f, "rcv": lax.rem(me_r + i, NR)}, device_id_type=MESH
        )
        return 0

    lax.fori_loop(1, NB, greet_f, 0)
    lax.fori_loop(1, NR, greet_r, 0)

    row32 = lax.broadcasted_iota(jnp.int32, (FB, 128), 0)
    k_scale = jnp.where((row32 == 0) & (me_f == 0), 0.5, 1.0).astype(F32)
    my_rows = pl.ds(pl.multiple_of(me_f * FB, FB), FB)

    def remote_f(src, dst, send, recv, to):
        return pltpu.make_async_remote_copy(
            src_ref=src, dst_ref=dst, send_sem=send, recv_sem=recv,
            device_id={"freq": to, "rcv": me_r}, device_id_type=MESH,
        )

    def remote_r(src, dst, send, recv, to):
        return pltpu.make_async_remote_copy(
            src_ref=src, dst_ref=dst, send_sem=send, recv_sem=recv,
            device_id={"freq": me_f, "rcv": to}, device_id_type=MESH,
        )

    def await_bytes(ref, sem):
        pltpu.make_async_copy(ref, ref, sem).wait()

    def any_of(places):
        found = me_f == places[0]
        for place in places[1:]:
            found = found | (me_f == place)
        return found

    def minus_places(q):
        return [MINUS_AT[c][q] for c in range(2)]

    def plus_places(q):
        return [PLUS_AT[c][4 * q + i] for c in range(2) for i in range(4)]

    def send_plus(it, q):
        gath[it, q, me_r] = psnd[it, q]
        dst = gath.at[it, q, me_r]
        for i in range(1, NX):
            remote_r(psnd.at[it, q], dst, gath_send.at[it], gath_recv.at[it, q, 0], along_x(i) * 2 + me_y).start()
        remote_r(psnd.at[it, q], dst, gath_send.at[it], gath_recv.at[it, q, 1], beside).start()

    def pass_plus(it, q):
        await_bytes(gath.at[it, q, 0], gath_recv.at[it, q, 1])
        block = gath.at[it, q, beside, pl.ds(0, HALF)]
        for i in range(1, NX):
            remote_r(block, block, gath_send.at[it], gath_recv.at[it, q, 2], along_x(i) * 2 + me_y).start()
        await_bytes(gath.at[it, q, pl.ds(0, NX - 1)], gath_recv.at[it, q, 0])
        for i in range(1, NX):
            block = gath.at[it, q, along_x(i) * 2 + me_y, pl.ds(HALF, HALF)]
            remote_r(block, block, gath_send.at[it], gath_recv.at[it, q, 3], beside).start()

    def fill_perm(i, _):
        perm[pl.ds(pl.multiple_of(i * 128, 128), 128), :] = reorder_rows(i * 128, 128, SL)
        return 0

    lax.fori_loop(0, PS, fill_perm, 0)
    high = plus_ref[...].astype(BF16)
    left = plus_ref[...] - high.astype(F32)
    middle = left.astype(BF16)
    small = (left - middle.astype(F32)).astype(BF16)
    split = jnp.dot(jnp.concatenate([high, middle, small], axis=0), perm[...], preferred_element_type=F32)
    first = split[: 2 * FB]
    for q in range(NQ):
        for g in range(NG):
            parts = [
                first[c * FB + g * GF : c * FB + (g + 1) * GF, p * SL : (p + 1) * SL]
                for c in range(2)
                for p in range(4 * q, 4 * q + 4)
            ]
            psnd[0, q, g * ROWS : (g + 1) * ROWS, :] = jnp.concatenate(parts, axis=0).astype(BF16)
    pl.semaphore_wait(barrier, NB - 1 + NR - 1)
    for q in range(NQ):
        send_plus(0, q)

    exact = first + (split[2 * FB : 4 * FB] + split[4 * FB :])
    for c in range(2):
        for p in range(PS):
            pinit[p // 4, c * 4 + p % 4] = exact[c * FB : (c + 1) * FB, p * SL : (p + 1) * SL]

    spread[...] = spreading()
    perm_m[...] = reorder_rows(0, ML * PS, ML)
    load_tab.wait()

    def split_tab(i, _):
        rows = pl.ds(pl.multiple_of(i * 128, 128), 128)
        values = tab_full[rows, :]
        top = values.astype(BF16)
        tab[0, rows, :] = top
        tab[1, rows, :] = (values - top.astype(F32)).astype(BF16)
        return 0

    lax.fori_loop(0, NK // 128, split_tab, 0)
    load_refl.wait()

    def window(x, onsets, y, send_chunk):
        until = jnp.transpose(jnp.broadcast_to(onsets, (128, 128)))
        until = jnp.concatenate([until, until], axis=1)
        traces = jnp.transpose(x[...])
        for n in range(TW // 256):
            cols = slice(n * 256, (n + 1) * 256)
            in_time = jnp.dot(traces, tab[0, :, cols], preferred_element_type=F32)
            in_time += jnp.dot(traces, tab[1, :, cols], preferred_element_type=F32)
            time = n * 256 + lax.broadcasted_iota(jnp.int32, (128, 256), 1)
            factor = jnp.where(time == 0, 1.0 / NK, 2.0 / NK).astype(F32)
            in_time = jnp.where(time < until, in_time * factor, 0.0)
            top = in_time.astype(BF16)
            eo[:128, cols] = top
            eo[128:, cols] = (in_time - top.astype(F32)).astype(BF16)
        for n in range(NK // 256):
            cols = slice(n * 256, (n + 1) * 256)
            both = jnp.dot(eo[...], tab[0, :TW, cols], preferred_element_type=F32)
            small = jnp.dot(eo[:128, :], tab[1, :TW, cols], preferred_element_type=F32)
            y[cols, :] = jnp.transpose(both[:128] + (both[128:] + small)).astype(BF16)
            send_chunk(n * (256 // FB), 256 // FB)

    half = ROWS // 2
    lane = lax.broadcasted_iota(jnp.int32, (half, GF * ML), 1)
    row = lax.broadcasted_iota(jnp.int32, (half, GF * ML), 0)
    same = lax.rem(row, GF) == lane // ML
    quad_lane = lax.broadcasted_iota(jnp.int32, (GF, 128), 1) // ML

    def refl_rows(c, g):
        return slice(c * FB * ML + g * GF * ML, c * FB * ML + (g + 1) * GF * ML)

    def forward(it, q):
        dims = (((1,), (1,)), ((), ()))
        blocks = ([], [])
        for g in range(NG):
            if g == 0:
                await_bytes(gath.at[it, q, pl.ds(0, NX - 1), pl.ds(0, HALF)], gath_recv.at[it, q, 2])
            if g == NG // 2:
                await_bytes(gath.at[it, q, pl.ds(0, NX - 1), pl.ds(0, HALF)], gath_recv.at[it, q, 3])
            rows = slice(g * ROWS, (g + 1) * ROWS)
            values = jnp.concatenate([gath[it, q, r, rows, :] for r in range(NR)], axis=1)
            a = lax.dot_general(values, refl[refl_rows(0, g), :], dims, preferred_element_type=F32)
            b = lax.dot_general(values, refl[refl_rows(1, g), :], dims, preferred_element_type=F32)
            parts = (a[:half] - b[half:], b[:half] + a[half:])
            for c in range(2):
                own = jnp.where(same, parts[c], 0.0)
                own = own[:, :128] + own[:, 128:]
                own = own + pltpu.roll(own, 64, 1)
                own = own + pltpu.roll(own, 32, 1)
                block = jnp.zeros((GF, 128), F32)
                for i in range(4):
                    block = jnp.where(quad_lane == i, own[i * GF : (i + 1) * GF], block)
                blocks[c].append(block)
        for c in range(2):
            to = MINUS_AT[c][q]
            msnd[it, q, c] = (jnp.concatenate(blocks[c], axis=0) * k_scale).astype(BF16)

            @pl.when(me_f == to)
            def _():
                xm[it, my_rows, :] = msnd[it, q, c]

            @pl.when(me_f != to)
            def _():
                remote_f(msnd.at[it, q, c], xm.at[it, my_rows], xm_send.at[it], xm_recv.at[it], to).start()

    def scatter(it, buffer, dst, send, recv):
        def send_chunk(begin, count):
            def one(i, _):
                to = begin + i
                rows = pl.ds(pl.multiple_of(to * FB, FB), FB)

                @pl.when(to == me_f)
                def _():
                    dst[...] = buffer[it, rows, :]

                @pl.when(to != me_f)
                def _():
                    remote_f(buffer.at[it, rows], dst, send, recv, to).start()

                return 0

            lax.fori_loop(0, count, one, 0)

        return send_chunk

    def window_minus(it, q):
        @pl.when(any_of(minus_places(q)))
        def _():
            await_bytes(xm.at[it, pl.ds(0, NK - FB)], xm_recv.at[it])
            onsets = jnp.concatenate([onm_ref[4 * q + i : 4 * q + i + 1, :] for i in range(4)], axis=1)
            send_chunk = scatter(it, ymsnd, ym.at[it, q, part], ym_send.at[it], ym_recv.at[it, q])
            window(xm.at[it], onsets, ymsnd.at[it], send_chunk)

    def adjoint(it, q):
        here = any_of(minus_places(q))

        @pl.when(here)
        def _():
            await_bytes(ym.at[it, q, pl.ds(0, 1)], ym_recv.at[it, q])

        @pl.when(jnp.logical_not(here))
        def _():
            await_bytes(ym.at[it, q], ym_recv.at[it, q])

        spread_rows = jnp.dot(ym[it, q].reshape(2 * FB, 128), spread[...], preferred_element_type=F32)
        row_s = lax.broadcasted_iota(jnp.int32, (2 * FB, 1024), 0)
        lane_s = lax.broadcasted_iota(jnp.int32, (2 * FB, 1024), 1)
        wide[...] = jnp.where(lax.rem(row_s, GF) == lax.rem(lane_s // ML, GF), spread_rows, 0.0)
        for g in range(NG):
            blocks = [wide[c * FB + g * GF : c * FB + (g + 1) * GF, :] for c in range(2)]
            re, im = [
                jnp.concatenate([block[:, i * 256 : (i + 1) * 256] for i in range(4)], axis=0) for block in blocks
            ]
            left = jnp.concatenate([re, im], axis=0).astype(BF16)
            right = jnp.concatenate([im, -re], axis=0).astype(BF16)
            for n in range(4):
                cols = slice(n * 256, (n + 1) * 256)
                out = jnp.dot(left, refl[refl_rows(0, g), cols], preferred_element_type=F32)
                out += jnp.dot(right, refl[refl_rows(1, g), cols], preferred_element_type=F32)
                out = out.astype(BF16)
                rows = slice(g % 2 * ROWS, (g % 2 + 1) * ROWS)
                for y in range(2):
                    values = out[:, y * SL : (y + 1) * SL]
                    if g < NG // 2:
                        part_a[it, q, n, y, rows, :] = values
                    else:
                        part_b[it, q, y, n, rows, :] = values
            if g == NG // 2 - 1:
                for i in range(1, NX):
                    remote_r(
                        part_a.at[it, q, along_x(i)], from_x.at[it, q, NX - 1 - i], rs_send.at[it],
                        rs_recv.at[it, q, 0], along_x(i) * 2 + me_y,
                    ).start()
        remote_r(
            part_b.at[it, q, 1 - me_y], from_y.at[it, q], rs_send.at[it], rs_recv.at[it, q, 1], beside
        ).start()

    def pass_sums(it, q):
        await_bytes(from_x.at[it, q], rs_recv.at[it, q, 0])
        total = part_a[it, q, me_x, 1 - me_y].astype(F32)
        for i in range(NX - 1):
            total += from_x[it, q, i, 1 - me_y].astype(F32)
        sum_a[it, q] = total.astype(BF16)
        remote_r(sum_a.at[it, q], rest_a.at[it, q], rs_send.at[it], rs_recv.at[it, q, 2], beside).start()
        await_bytes(from_y.at[it, q], rs_recv.at[it, q, 1])
        for i in range(1, NX):
            x = along_x(i)
            total = part_b[it, q, me_y, x].astype(F32) + from_y[it, q, x].astype(F32)
            sum_b[it, q, i - 1] = total.astype(BF16)
            remote_r(
                sum_b.at[it, q, i - 1], rest_b.at[it, q, NX - 1 - i], rs_send.at[it], rs_recv.at[it, q, 3],
                x * 2 + me_y,
            ).start()

    def add_up(it, q):
        await_bytes(rest_a.at[it, q], rs_recv.at[it, q, 2])
        await_bytes(rest_b.at[it, q], rs_recv.at[it, q, 3])
        first = part_a[it, q, me_x, me_y].astype(F32) + rest_a[it, q].astype(F32)
        second = part_b[it, q, me_y, me_x].astype(F32) + from_y[it, q, me_x].astype(F32)
        for i in range(NX - 1):
            first += from_x[it, q, i, me_y].astype(F32)
            second += rest_b[it, q, i].astype(F32)
        total = jnp.concatenate([first, second], axis=0)
        for c in range(2):
            for i in range(4):
                to = PLUS_AT[c][4 * q + i]
                at = c * 4 + i
                block = jnp.concatenate(
                    [total[g * ROWS + at * GF : g * ROWS + (at + 1) * GF] for g in range(NG)], axis=0
                )
                xsnd[it, q, at] = (block * k_scale).astype(BF16)

                @pl.when(me_f == to)
                def _():
                    xp[it, my_rows, :] = xsnd[it, q, at]

                @pl.when(me_f != to)
                def _():
                    remote_f(xsnd.at[it, q, at], xp.at[it, my_rows], xp_send.at[it], xp_recv.at[it], to).start()

    def window_plus(it, q):
        @pl.when(any_of(plus_places(q)))
        def _():
            await_bytes(xp.at[it, pl.ds(0, NK - FB)], xp_recv.at[it])
            point = jnp.int32(0)
            for i in range(1, 4):
                point = jnp.where(any_of([PLUS_AT[c][4 * q + i] for c in range(2)]), i, point)
            onsets = onp_ref[pl.ds(4 * q + point, 1), :]
            send_chunk = scatter(it, ypsnd, wp.at[it, q, part * 4 + point], wp_send.at[it], wp_recv.at[it, q])
            window(xp.at[it], onsets, ypsnd.at[it], send_chunk)

    def update(it, q):
        here = any_of(plus_places(q))

        @pl.when(here)
        def _():
            await_bytes(wp.at[it, q, pl.ds(0, 7)], wp_recv.at[it, q])

        @pl.when(jnp.logical_not(here))
        def _():
            await_bytes(wp.at[it, q], wp_recv.at[it, q])

        @pl.when(it < ITERS - 1)
        def _():
            new = pinit[q] + wp[it, q].astype(F32)
            for g in range(NG):
                rows = new[:, g * GF : (g + 1) * GF, :].reshape(ROWS, SL)
                psnd[it + 1, q, g * ROWS : (g + 1) * ROWS, :] = rows.astype(BF16)
            send_plus(it + 1, q)

        @pl.when(it == ITERS - 1)
        def _():
            change = jnp.concatenate(
                [jnp.concatenate([wp[it, q, c * 4 + i] for i in range(4)], axis=1) for c in range(2)], axis=0
            )
            dims = (((1,), (1,)), ((), ()))
            change = lax.dot_general(
                change, perm[:, q * 4 * SL : (q + 1) * 4 * SL], dims, preferred_element_type=F32
            )
            before = plus_ref if q == 0 else out_plus
            out_plus[...] = before[...] + change

    def finish_minus(it):
        @pl.when(it == ITERS - 1)
        def _():
            minus = jnp.concatenate(
                [jnp.concatenate([ym[it, q, c] for q in range(NQ)], axis=1) for c in range(2)], axis=0
            )
            dims = (((1,), (1,)), ((), ()))
            out_minus[...] = lax.dot_general(minus, perm_m[...], dims, preferred_element_type=F32)

    def iteration(it, _):
        pass_plus(it, 0)
        pass_plus(it, 1)
        pass_plus(it, 2)
        forward(it, 0)
        forward(it, 1)
        forward(it, 2)
        window_minus(it, 0)
        window_minus(it, 1)
        window_minus(it, 2)
        adjoint(it, 0)
        adjoint(it, 1)
        adjoint(it, 2)
        pass_sums(it, 0)
        pass_sums(it, 1)
        pass_sums(it, 2)
        add_up(it, 0)
        add_up(it, 1)
        add_up(it, 2)
        window_plus(it, 0)
        finish_minus(it)
        window_plus(it, 1)
        window_plus(it, 2)
        update(it, 0)
        update(it, 1)
        update(it, 2)
        return 0

    lax.fori_loop(0, ITERS, iteration, 0)

    is_minus = any_of([place for q in range(NQ) for place in minus_places(q)])
    is_plus = any_of([place for q in range(NQ) for place in plus_places(q)])

    def drain(it, _):
        await_bytes(gath.at[it, :, pl.ds(0, NR - 1)], gath_send.at[it])
        await_bytes(gath.at[it, :, pl.ds(0, NR - 1)], rs_send.at[it])

        @pl.when(is_minus)
        def _():
            await_bytes(xm.at[it, pl.ds(0, (WM - 1) * FB)], xm_send.at[it])
            await_bytes(ymsnd.at[it, pl.ds(0, NK - FB)], ym_send.at[it])

        @pl.when(jnp.logical_not(is_minus))
        def _():
            await_bytes(msnd.at[it], xm_send.at[it])

        @pl.when(is_plus)
        def _():
            await_bytes(xp.at[it, pl.ds(0, (WP - 1) * FB)], xp_send.at[it])
            await_bytes(ypsnd.at[it, pl.ds(0, NK - FB)], wp_send.at[it])

        @pl.when(jnp.logical_not(is_plus))
        def _():
            await_bytes(xsnd.at[it], xp_send.at[it])

        return 0

    lax.fori_loop(0, ITERS, drain, 0)


def local(reflection, plus_init, onset_receiver, onset_source):
    onm = jnp.transpose(onset_receiver)
    onp = jnp.transpose(onset_source)
    vmem = pl.BlockSpec(memory_space=pltpu.VMEM)
    hbm = pl.BlockSpec(memory_space=pl.ANY)
    dma = pltpu.SemaphoreType.DMA
    out_minus, out_plus = pl.pallas_call(
        kernel,
        out_shape=(
            jax.ShapeDtypeStruct((2 * FB, ML * PS), F32),
            jax.ShapeDtypeStruct((2 * FB, SL * PS), F32),
        ),
        in_specs=[hbm, hbm, vmem, vmem, vmem],
        out_specs=(vmem, vmem),
        scratch_shapes=[
            pltpu.VMEM((2 * FB * ML, 1024), BF16),
            pltpu.VMEM((NK, NK), F32),
            pltpu.VMEM((2, NK, NK), BF16),
            pltpu.VMEM((SL * PS, SL * PS), BF16),
            pltpu.VMEM((ML * PS, ML * PS), BF16),
            pltpu.VMEM((4 * ML, 4 * GF * ML), BF16),
            pltpu.VMEM((NQ, 8, FB, SL), F32),
            pltpu.VMEM((ITERS, NQ, NG * ROWS, SL), BF16),
            pltpu.VMEM((ITERS, NQ, NR, NG * ROWS, SL), BF16),
            pltpu.VMEM((ITERS, NQ, 2, FB, 128), BF16),
            pltpu.VMEM((ITERS, NK, 128), BF16),
            pltpu.VMEM((ITERS, NK, 128), BF16),
            pltpu.VMEM((ITERS, NQ, 2, FB, 128), BF16),
            pltpu.VMEM((2 * FB, 1024), F32),
            pltpu.VMEM((ITERS, NQ, NX, 2, HALF, SL), BF16),
            pltpu.VMEM((ITERS, NQ, 2, NX, HALF, SL), BF16),
            pltpu.VMEM((ITERS, NQ, NX - 1, 2, HALF, SL), BF16),
            pltpu.VMEM((ITERS, NQ, NX, HALF, SL), BF16),
            pltpu.VMEM((ITERS, NQ, HALF, SL), BF16),
            pltpu.VMEM((ITERS, NQ, NX - 1, HALF, SL), BF16),
            pltpu.VMEM((ITERS, NQ, HALF, SL), BF16),
            pltpu.VMEM((ITERS, NQ, NX - 1, HALF, SL), BF16),
            pltpu.VMEM((ITERS, NQ, 8, FB, SL), BF16),
            pltpu.VMEM((ITERS, NK, SL), BF16),
            pltpu.VMEM((ITERS, NK, SL), BF16),
            pltpu.VMEM((ITERS, NQ, 8, FB, SL), BF16),
            pltpu.VMEM((256, TW), BF16),
            dma((2,)),
            dma((ITERS,)), dma((ITERS, NQ, 4)),
            dma((ITERS,)), dma((ITERS,)),
            dma((ITERS,)), dma((ITERS, NQ)),
            dma((ITERS,)), dma((ITERS, NQ, 4)),
            dma((ITERS,)), dma((ITERS,)),
            dma((ITERS,)), dma((ITERS, NQ)),
        ],
        compiler_params=pltpu.CompilerParams(
            collective_id=0, has_side_effects=True, vmem_limit_bytes=56 * 1024 * 1024
        ),
    )(
        reflection.reshape(2 * FB * ML, 1024),
        jnp.asarray(tables()),
        plus_init.reshape(2 * FB, SL * PS),
        onm,
        onp,
    )
    return out_minus.reshape(2, FB, ML * PS), out_plus.reshape(2, FB, SL * PS)


def solution(mesh):
    return jax.shard_map(
        local,
        mesh=mesh,
        in_specs=(
            P(None, "freq", "rcv", None),
            P(None, "freq", "rcv"),
            P("rcv", None),
            P("rcv", None),
        ),
        out_specs=(P(None, "freq", "rcv"), P(None, "freq", "rcv")),
        check_vma=False,
    )
```

```python
import math

import jax
import jax.numpy as jnp
import numpy as np
from jax import lax
from jax.experimental import pallas as pl
from jax.experimental.pallas import tpu as pltpu
from jax.sharding import PartitionSpec as P

MESH = pl.DeviceIdType.MESH
PS = 12
ITERS = 2
FB = 32
NB = 32
NR = 8
NX = 4
GF = 8
NG = FB // GF
ROWS = 2 * 4 * GF
HALF = NG * ROWS // 2
ML = 32
SL = 128
NK = FB * NB
TW = 768
NQ = 3
WM = 2 * NQ
WP = 2 * PS
F32 = jnp.float32
BF16 = jnp.bfloat16


def tables():
    index = np.arange(NK)
    phases = (index[:, None] * index[None, :]) % (2 * NK)
    angles = phases * (2.0 * math.pi / (2 * NK))
    return np.stack([np.cos(angles), np.sin(angles)]).astype(np.float32)


def reorder_rows(start, rows, count):
    index = start + lax.broadcasted_iota(jnp.int32, (rows, 1), 0)
    item = (index * 43691) >> 19
    target = (index - PS * item) * count + item
    lane = lax.broadcasted_iota(jnp.int32, (rows, PS * count), 1)
    return jnp.where(lane == target, 1.0, 0.0).astype(BF16)


def spreading():
    row = lax.broadcasted_iota(jnp.int32, (4 * ML, 4 * GF * ML), 0)
    lane = lax.broadcasted_iota(jnp.int32, (4 * ML, 4 * GF * ML), 1)
    hit = (lane // (GF * ML) == row // ML) & (lax.rem(lane, ML) == lax.rem(row, ML))
    return jnp.where(hit, 1.0, 0.0).astype(BF16)


MINUS_AT = ((3, 11, 5), (25, 17, 31))
PLUS_AT = (
    (0, 4, 8, 12, 2, 6, 10, 14, 1, 7, 9, 15),
    (18, 22, 26, 30, 16, 20, 24, 28, 19, 21, 27, 29),
)


def kernel(
    refl_hbm, tab_hbm, plus_hbm, onm_ref, onp_ref,
    out_minus, out_plus,
    plus_ref, refl, refl_t, tab_full, tab, perm, perm_m, spread, pinit, psnd, gath, msnd, xm, ymsnd, ym, wide,
    partial, from_far, from_x, from_y, sums, rests, xsnd, xp, ypsnd, wp, eo,
    load_sem, gath_send, gath_recv, xm_send, xm_recv, ym_send, ym_recv, rs_send, rs_recv, xp_send, xp_recv,
    wp_send, wp_recv,
):
    me_f = lax.axis_index("freq")
    me_r = lax.axis_index("rcv")
    part = me_f // (NB // 2)
    me_x, me_y = me_r // 2, lax.rem(me_r, 2)
    beside = me_x * 2 + (1 - me_y)

    def along_x(i):
        return lax.rem(me_x + i, NX)


    load_refl = pltpu.make_async_copy(refl_hbm, refl, load_sem.at[0])
    load_tab = pltpu.make_async_copy(tab_hbm.at[part], tab_full, load_sem.at[1])
    load_plus = pltpu.make_async_copy(plus_hbm, plus_ref, load_sem.at[2])
    load_plus.start()
    load_refl.start()
    load_tab.start()

    barrier = pltpu.get_barrier_semaphore()

    def greet_f(i, _):
        pl.semaphore_signal(
            barrier, inc=1, device_id={"freq": lax.rem(me_f + i, NB), "rcv": me_r}, device_id_type=MESH
        )
        return 0

    def greet_r(i, _):
        pl.semaphore_signal(
            barrier, inc=1, device_id={"freq": me_f, "rcv": lax.rem(me_r + i, NR)}, device_id_type=MESH
        )
        return 0

    lax.fori_loop(1, NB, greet_f, 0)
    lax.fori_loop(1, NR, greet_r, 0)

    row32 = lax.broadcasted_iota(jnp.int32, (FB, 128), 0)
    k_scale = jnp.where((row32 == 0) & (me_f == 0), 0.5, 1.0).astype(F32)
    my_rows = pl.ds(pl.multiple_of(me_f * FB, FB), FB)

    def remote_f(src, dst, send, recv, to):
        return pltpu.make_async_remote_copy(
            src_ref=src, dst_ref=dst, send_sem=send, recv_sem=recv,
            device_id={"freq": to, "rcv": me_r}, device_id_type=MESH,
        )

    def remote_r(src, dst, send, recv, to):
        return pltpu.make_async_remote_copy(
            src_ref=src, dst_ref=dst, send_sem=send, recv_sem=recv,
            device_id={"freq": me_f, "rcv": to}, device_id_type=MESH,
        )

    def await_bytes(ref, sem):
        pltpu.make_async_copy(ref, ref, sem).wait()

    def any_of(places):
        found = me_f == places[0]
        for place in places[1:]:
            found = found | (me_f == place)
        return found

    def minus_places(q):
        return [MINUS_AT[c][q] for c in range(2)]

    def plus_places(q):
        return [PLUS_AT[c][4 * q + i] for c in range(2) for i in range(4)]

    def row_x(i):
        return along_x(i) * 2 + me_y

    def send_plus(it, q):
        gath[it, q, me_r] = psnd[it, q]
        dst = gath.at[it, q, me_r]
        for i in (1, 3):
            remote_r(psnd.at[it, q], dst, gath_send.at[it], gath_recv.at[it, q, 0], row_x(i)).start()
        remote_r(psnd.at[it, q], dst, gath_send.at[it], gath_recv.at[it, q, 1], beside).start()

    def pass_plus(it, q):
        def pass_on(r, start, rows, sem, to):
            block = gath.at[it, q, r, pl.ds(start, rows)]
            remote_r(block, block, gath_send.at[it], gath_recv.at[it, q, sem], to).start()

        await_bytes(gath.at[it, q, 0], gath_recv.at[it, q, 1])
        pass_on(beside, 0, 4 * ROWS, 2, row_x(2))
        pass_on(beside, 0, ROWS, 4, row_x(1))
        pass_on(beside, 0, ROWS, 3, row_x(3))
        await_bytes(gath.at[it, q, pl.ds(0, 2)], gath_recv.at[it, q, 0])
        pass_on(row_x(1), ROWS, 3 * ROWS, 5, beside)
        pass_on(row_x(3), ROWS, 3 * ROWS, 5, beside)
        pass_on(row_x(3), 0, HALF, 4, row_x(1))
        pass_on(row_x(1), HALF, HALF, 3, row_x(3))

    def fill_perm(i, _):
        perm[pl.ds(pl.multiple_of(i * 128, 128), 128), :] = reorder_rows(i * 128, 128, SL)
        return 0

    lax.fori_loop(0, PS, fill_perm, 0)
    load_plus.wait()
    high = plus_ref[...].astype(BF16)
    left = plus_ref[...] - high.astype(F32)
    middle = left.astype(BF16)
    small = (left - middle.astype(F32)).astype(BF16)
    split = jnp.dot(jnp.concatenate([high, middle, small], axis=0), perm[...], preferred_element_type=F32)
    first = split[: 2 * FB]
    for q in range(NQ):
        for g in range(NG):
            parts = [
                first[c * FB + g * GF : c * FB + (g + 1) * GF, p * SL : (p + 1) * SL]
                for c in range(2)
                for p in range(4 * q, 4 * q + 4)
            ]
            psnd[0, q, g * ROWS : (g + 1) * ROWS, :] = jnp.concatenate(parts, axis=0).astype(BF16)
    pl.semaphore_wait(barrier, NB - 1 + NR - 1)
    for q in range(NQ):
        send_plus(0, q)

    exact = first + (split[2 * FB : 4 * FB] + split[4 * FB :])
    for c in range(2):
        for p in range(PS):
            pinit[p // 4, c * 4 + p % 4] = exact[c * FB : (c + 1) * FB, p * SL : (p + 1) * SL]

    spread[...] = spreading()
    perm_m[...] = reorder_rows(0, ML * PS, ML)
    load_tab.wait()

    def split_tab(i, _):
        rows = pl.ds(pl.multiple_of(i * 128, 128), 128)
        values = tab_full[rows, :]
        top = values.astype(BF16)
        tab[0, rows, :] = top
        tab[1, rows, :] = (values - top.astype(F32)).astype(BF16)
        return 0

    lax.fori_loop(0, NK // 128, split_tab, 0)
    load_refl.wait()
    for g in range(NG):
        for c in range(2):
            block = refl[c * FB * ML + g * GF * ML : c * FB * ML + (g + 1) * GF * ML, :]
            refl_t[g, :, c * GF * ML : (c + 1) * GF * ML] = jnp.transpose(block)

    def window(x, onsets, y, send_chunk):
        until = jnp.transpose(jnp.broadcast_to(onsets, (128, 128)))
        until = jnp.concatenate([until, until], axis=1)
        traces = jnp.transpose(x[...])
        for n in range(TW // 256):
            cols = slice(n * 256, (n + 1) * 256)
            in_time = jnp.dot(traces, tab[0, :, cols], preferred_element_type=F32)
            in_time += jnp.dot(traces, tab[1, :, cols], preferred_element_type=F32)
            time = n * 256 + lax.broadcasted_iota(jnp.int32, (128, 256), 1)
            factor = jnp.where(time == 0, 1.0 / NK, 2.0 / NK).astype(F32)
            in_time = jnp.where(time < until, in_time * factor, 0.0)
            top = in_time.astype(BF16)
            eo[:128, cols] = top
            eo[128:, cols] = (in_time - top.astype(F32)).astype(BF16)
        for n in range(NK // 256):
            cols = slice(n * 256, (n + 1) * 256)
            both = jnp.dot(eo[...], tab[0, :TW, cols], preferred_element_type=F32)
            small = jnp.dot(eo[:128, :], tab[1, :TW, cols], preferred_element_type=F32)
            y[cols, :] = jnp.transpose(both[:128] + (both[128:] + small)).astype(BF16)
            send_chunk(n * (256 // FB), 256 // FB)

    half = ROWS // 2
    lane = lax.broadcasted_iota(jnp.int32, (half, GF * ML), 1)
    row = lax.broadcasted_iota(jnp.int32, (half, GF * ML), 0)
    same = lax.rem(row, GF) == lane // ML
    quad_lane = lax.broadcasted_iota(jnp.int32, (GF, 128), 1) // ML

    def refl_rows(c, g):
        return slice(c * FB * ML + g * GF * ML, c * FB * ML + (g + 1) * GF * ML)

    def forward(it, q):
        blocks = ([], [])
        for g in range(NG):
            if g == 0:
                await_bytes(gath.at[it, q, 0, pl.ds(0, 3 * ROWS)], gath_recv.at[it, q, 3])
                await_bytes(gath.at[it, q, 0, pl.ds(0, 3 * ROWS)], gath_recv.at[it, q, 4])
                await_bytes(gath.at[it, q, 0], gath_recv.at[it, q, 2])
            if g == 1:
                await_bytes(gath.at[it, q, pl.ds(0, 2), pl.ds(0, 3 * ROWS)], gath_recv.at[it, q, 5])
            rows = slice(g * ROWS, (g + 1) * ROWS)
            values = jnp.concatenate([gath[it, q, r, rows, :] for r in range(NR)], axis=1)
            both = jnp.dot(values, refl_t[g], preferred_element_type=F32)
            a, b = both[:, : GF * ML], both[:, GF * ML :]
            parts = (a[:half] - b[half:], b[:half] + a[half:])
            for c in range(2):
                own = jnp.where(same, parts[c], 0.0)
                own = own[:, :128] + own[:, 128:]
                own = own + pltpu.roll(own, 64, 1)
                own = own + pltpu.roll(own, 32, 1)
                block = jnp.zeros((GF, 128), F32)
                for i in range(4):
                    block = jnp.where(quad_lane == i, own[i * GF : (i + 1) * GF], block)
                blocks[c].append(block)
        for c in range(2):
            to = MINUS_AT[c][q]
            msnd[it, q, c] = (jnp.concatenate(blocks[c], axis=0) * k_scale).astype(BF16)

            @pl.when(me_f == to)
            def _():
                xm[it, my_rows, :] = msnd[it, q, c]

            @pl.when(me_f != to)
            def _():
                remote_f(msnd.at[it, q, c], xm.at[it, my_rows], xm_send.at[it], xm_recv.at[it], to).start()

    def scatter(it, buffer, dst, send, recv):
        def send_chunk(begin, count):
            def one(i, _):
                to = begin + i
                rows = pl.ds(pl.multiple_of(to * FB, FB), FB)

                @pl.when(to == me_f)
                def _():
                    dst[...] = buffer[it, rows, :]

                @pl.when(to != me_f)
                def _():
                    remote_f(buffer.at[it, rows], dst, send, recv, to).start()

                return 0

            lax.fori_loop(0, count, one, 0)

        return send_chunk

    def window_minus(it, q):
        @pl.when(any_of(minus_places(q)))
        def _():
            await_bytes(xm.at[it, pl.ds(0, NK - FB)], xm_recv.at[it])
            onsets = jnp.concatenate([onm_ref[4 * q + i : 4 * q + i + 1, :] for i in range(4)], axis=1)
            send_chunk = scatter(it, ymsnd, ym.at[it, q, part], ym_send.at[it], ym_recv.at[it, q])
            window(xm.at[it], onsets, ymsnd.at[it], send_chunk)

    def adjoint(it, q):
        here = any_of(minus_places(q))

        @pl.when(here)
        def _():
            await_bytes(ym.at[it, q, pl.ds(0, 1)], ym_recv.at[it, q])

        @pl.when(jnp.logical_not(here))
        def _():
            await_bytes(ym.at[it, q], ym_recv.at[it, q])

        spread_rows = jnp.dot(ym[it, q].reshape(2 * FB, 128), spread[...], preferred_element_type=F32)
        row_s = lax.broadcasted_iota(jnp.int32, (2 * FB, 1024), 0)
        lane_s = lax.broadcasted_iota(jnp.int32, (2 * FB, 1024), 1)
        wide[...] = jnp.where(lax.rem(row_s, GF) == lax.rem(lane_s // ML, GF), spread_rows, 0.0)
        for g in range(NG):
            blocks = [wide[c * FB + g * GF : c * FB + (g + 1) * GF, :] for c in range(2)]
            re, im = [
                jnp.concatenate([block[:, i * 256 : (i + 1) * 256] for i in range(4)], axis=0) for block in blocks
            ]
            left = jnp.concatenate([re, im], axis=0).astype(BF16)
            right = jnp.concatenate([im, -re], axis=0).astype(BF16)
            for n in range(4):
                cols = slice(n * 256, (n + 1) * 256)
                out = jnp.dot(left, refl[refl_rows(0, g), cols], preferred_element_type=F32)
                out += jnp.dot(right, refl[refl_rows(1, g), cols], preferred_element_type=F32)
                out = out.astype(BF16)
                for y in range(2):
                    partial[it, q, n, y, g * ROWS : (g + 1) * ROWS, :] = out[:, y * SL : (y + 1) * SL]

        def send(x, y, start, rows, dst, sem, to):
            src = partial.at[it, q, x, y, pl.ds(start, rows)]
            remote_r(src, dst, rs_send.at[it], rs_recv.at[it, q, sem], to).start()

        send(along_x(2), 1 - me_y, 0, 4 * ROWS, from_far.at[it, q], 0, row_x(2))
        for k, i in enumerate((1, 3)):
            send(along_x(i), 1 - me_y, ROWS, 3 * ROWS, from_y.at[it, q, k], 3, beside)
        for k, i in enumerate((1, 3)):
            there = from_x.at[it, q, 1 - k]
            send(along_x(2), me_y, k * HALF, HALF, there.at[pl.ds(0, HALF)], 2 - k, row_x(i))
            send(along_x(i), 1 - me_y, 0, ROWS, there.at[pl.ds(HALF, ROWS)], 2 - k, row_x(i))

    def pass_sums(it, q):
        def pass_on(total, slot, sem, to):
            sums[it, q, slot] = total.astype(BF16)
            remote_r(
                sums.at[it, q, slot], rests.at[it, q, sem - 4], rs_send.at[it], rs_recv.at[it, q, sem], to
            ).start()

        await_bytes(from_x.at[it, q, 0], rs_recv.at[it, q, 1])
        await_bytes(from_x.at[it, q, 1], rs_recv.at[it, q, 2])
        await_bytes(from_far.at[it, q], rs_recv.at[it, q, 0])
        total = partial[it, q, me_x, 1 - me_y].astype(F32) + from_far[it, q].astype(F32)
        quarter = from_x[it, q, 0, HALF:, :].astype(F32) + from_x[it, q, 1, HALF:, :].astype(F32)
        pass_on(jnp.concatenate([total[:ROWS] + quarter, total[ROWS:]], axis=0), 2, 6, beside)
        await_bytes(from_y.at[it, q], rs_recv.at[it, q, 3])
        for k, i in enumerate((1, 3)):
            total = partial[it, q, along_x(i), me_y].astype(F32)
            more = from_y[it, q, k].astype(F32)
            half = from_x[it, q, 1 - k, :HALF, :].astype(F32)
            if k == 0:
                pieces = [total[:ROWS] + half[:ROWS], total[ROWS:HALF] + half[ROWS:] + more[:ROWS]]
                pieces.append(total[HALF:] + more[ROWS:])
            else:
                pieces = [total[:ROWS], total[ROWS:HALF] + more[:ROWS], total[HALF:] + half + more[ROWS:]]
            pass_on(jnp.concatenate(pieces, axis=0), k, 5 - k, row_x(i))

    def add_up(it, q):
        total = partial[it, q, me_x, me_y].astype(F32)
        for k in range(3):
            await_bytes(rests.at[it, q, k], rs_recv.at[it, q, 4 + k])
            total += rests[it, q, k].astype(F32)
        for c in range(2):
            for i in range(4):
                to = PLUS_AT[c][4 * q + i]
                at = c * 4 + i
                block = jnp.concatenate(
                    [total[g * ROWS + at * GF : g * ROWS + (at + 1) * GF] for g in range(NG)], axis=0
                )
                xsnd[it, q, at] = (block * k_scale).astype(BF16)

                @pl.when(me_f == to)
                def _():
                    xp[it, my_rows, :] = xsnd[it, q, at]

                @pl.when(me_f != to)
                def _():
                    remote_f(xsnd.at[it, q, at], xp.at[it, my_rows], xp_send.at[it], xp_recv.at[it], to).start()

    def window_plus(it, q):
        @pl.when(any_of(plus_places(q)))
        def _():
            await_bytes(xp.at[it, pl.ds(0, NK - FB)], xp_recv.at[it])
            point = jnp.int32(0)
            for i in range(1, 4):
                point = jnp.where(any_of([PLUS_AT[c][4 * q + i] for c in range(2)]), i, point)
            onsets = onp_ref[pl.ds(4 * q + point, 1), :]
            send_chunk = scatter(it, ypsnd, wp.at[it, q, part * 4 + point], wp_send.at[it], wp_recv.at[it, q])
            window(xp.at[it], onsets, ypsnd.at[it], send_chunk)

    def update(it, q):
        here = any_of(plus_places(q))

        @pl.when(here)
        def _():
            await_bytes(wp.at[it, q, pl.ds(0, 7)], wp_recv.at[it, q])

        @pl.when(jnp.logical_not(here))
        def _():
            await_bytes(wp.at[it, q], wp_recv.at[it, q])

        @pl.when(it < ITERS - 1)
        def _():
            new = pinit[q] + wp[it, q].astype(F32)
            for g in range(NG):
                rows = new[:, g * GF : (g + 1) * GF, :].reshape(ROWS, SL)
                psnd[it + 1, q, g * ROWS : (g + 1) * ROWS, :] = rows.astype(BF16)
            send_plus(it + 1, q)

        @pl.when(it == ITERS - 1)
        def _():
            change = jnp.concatenate(
                [jnp.concatenate([wp[it, q, c * 4 + i] for i in range(4)], axis=1) for c in range(2)], axis=0
            )
            dims = (((1,), (1,)), ((), ()))
            change = lax.dot_general(
                change, perm[:, q * 4 * SL : (q + 1) * 4 * SL], dims, preferred_element_type=F32
            )
            before = plus_ref if q == 0 else out_plus
            out_plus[...] = before[...] + change

    def finish_minus(it):
        @pl.when(it == ITERS - 1)
        def _():
            minus = jnp.concatenate(
                [jnp.concatenate([ym[it, q, c] for q in range(NQ)], axis=1) for c in range(2)], axis=0
            )
            dims = (((1,), (1,)), ((), ()))
            out_minus[...] = lax.dot_general(minus, perm_m[...], dims, preferred_element_type=F32)

    def iteration(it, _):
        pass_plus(it, 0)
        pass_plus(it, 1)
        forward(it, 0)
        pass_plus(it, 2)
        forward(it, 1)
        forward(it, 2)
        window_minus(it, 0)
        window_minus(it, 1)
        window_minus(it, 2)
        adjoint(it, 0)
        adjoint(it, 1)
        pass_sums(it, 0)
        adjoint(it, 2)
        pass_sums(it, 1)
        pass_sums(it, 2)
        add_up(it, 0)
        add_up(it, 1)
        add_up(it, 2)
        window_plus(it, 0)
        finish_minus(it)
        window_plus(it, 1)
        window_plus(it, 2)
        update(it, 0)
        update(it, 1)
        update(it, 2)
        return 0

    lax.fori_loop(0, ITERS, iteration, 0)

    is_minus = any_of([place for q in range(NQ) for place in minus_places(q)])
    is_plus = any_of([place for q in range(NQ) for place in plus_places(q)])

    def drain(it, _):
        await_bytes(gath.at[it, :, pl.ds(0, NR - 1)], gath_send.at[it])
        await_bytes(gath.at[it, :, pl.ds(0, NR - 1)], rs_send.at[it])

        @pl.when(is_minus)
        def _():
            await_bytes(xm.at[it, pl.ds(0, (WM - 1) * FB)], xm_send.at[it])
            await_bytes(ymsnd.at[it, pl.ds(0, NK - FB)], ym_send.at[it])

        @pl.when(jnp.logical_not(is_minus))
        def _():
            await_bytes(msnd.at[it], xm_send.at[it])

        @pl.when(is_plus)
        def _():
            await_bytes(xp.at[it, pl.ds(0, (WP - 1) * FB)], xp_send.at[it])
            await_bytes(ypsnd.at[it, pl.ds(0, NK - FB)], wp_send.at[it])

        @pl.when(jnp.logical_not(is_plus))
        def _():
            await_bytes(xsnd.at[it], xp_send.at[it])

        return 0

    lax.fori_loop(0, ITERS, drain, 0)


def local(reflection, plus_init, onset_receiver, onset_source):
    onm = jnp.transpose(onset_receiver)
    onp = jnp.transpose(onset_source)
    vmem = pl.BlockSpec(memory_space=pltpu.VMEM)
    hbm = pl.BlockSpec(memory_space=pl.ANY)
    dma = pltpu.SemaphoreType.DMA
    out_minus, out_plus = pl.pallas_call(
        kernel,
        out_shape=(
            jax.ShapeDtypeStruct((2 * FB, ML * PS), F32),
            jax.ShapeDtypeStruct((2 * FB, SL * PS), F32),
        ),
        in_specs=[hbm, hbm, hbm, vmem, vmem],
        out_specs=(vmem, vmem),
        scratch_shapes=[
            pltpu.VMEM((2 * FB, SL * PS), F32),
            pltpu.VMEM((2 * FB * ML, 1024), BF16),
            pltpu.VMEM((NG, 1024, 2 * GF * ML), BF16),
            pltpu.VMEM((NK, NK), F32),
            pltpu.VMEM((2, NK, NK), BF16),
            pltpu.VMEM((SL * PS, SL * PS), BF16),
            pltpu.VMEM((ML * PS, ML * PS), BF16),
            pltpu.VMEM((4 * ML, 4 * GF * ML), BF16),
            pltpu.VMEM((NQ, 8, FB, SL), F32),
            pltpu.VMEM((ITERS, NQ, NG * ROWS, SL), BF16),
            pltpu.VMEM((ITERS, NQ, NR, NG * ROWS, SL), BF16),
            pltpu.VMEM((ITERS, NQ, 2, FB, 128), BF16),
            pltpu.VMEM((ITERS, NK, 128), BF16),
            pltpu.VMEM((ITERS, NK, 128), BF16),
            pltpu.VMEM((ITERS, NQ, 2, FB, 128), BF16),
            pltpu.VMEM((2 * FB, 1024), F32),
            pltpu.VMEM((ITERS, NQ, NX, 2, 4 * ROWS, SL), BF16),
            pltpu.VMEM((ITERS, NQ, 4 * ROWS, SL), BF16),
            pltpu.VMEM((ITERS, NQ, 2, 3 * ROWS, SL), BF16),
            pltpu.VMEM((ITERS, NQ, 2, 3 * ROWS, SL), BF16),
            pltpu.VMEM((ITERS, NQ, 3, 4 * ROWS, SL), BF16),
            pltpu.VMEM((ITERS, NQ, 3, 4 * ROWS, SL), BF16),
            pltpu.VMEM((ITERS, NQ, 8, FB, SL), BF16),
            pltpu.VMEM((ITERS, NK, SL), BF16),
            pltpu.VMEM((ITERS, NK, SL), BF16),
            pltpu.VMEM((ITERS, NQ, 8, FB, SL), BF16),
            pltpu.VMEM((256, TW), BF16),
            dma((3,)),
            dma((ITERS,)), dma((ITERS, NQ, 6)),
            dma((ITERS,)), dma((ITERS,)),
            dma((ITERS,)), dma((ITERS, NQ)),
            dma((ITERS,)), dma((ITERS, NQ, 7)),
            dma((ITERS,)), dma((ITERS,)),
            dma((ITERS,)), dma((ITERS, NQ)),
        ],
        compiler_params=pltpu.CompilerParams(
            collective_id=0, has_side_effects=True, vmem_limit_bytes=56 * 1024 * 1024
        ),
    )(
        reflection.reshape(2 * FB * ML, 1024),
        jnp.asarray(tables()),
        plus_init.reshape(2 * FB, SL * PS),
        onm,
        onp,
    )
    return out_minus.reshape(2, FB, ML * PS), out_plus.reshape(2, FB, SL * PS)


def solution(mesh):
    return jax.shard_map(
        local,
        mesh=mesh,
        in_specs=(
            P(None, "freq", "rcv", None),
            P(None, "freq", "rcv"),
            P("rcv", None),
            P("rcv", None),
        ),
        out_specs=(P(None, "freq", "rcv"), P(None, "freq", "rcv")),
        check_vma=False,
    )
```

```python
import math

import jax
import jax.numpy as jnp
import numpy as np
from jax import lax
from jax.experimental import pallas as pl
from jax.experimental.pallas import tpu as pltpu
from jax.sharding import PartitionSpec as P

MESH = pl.DeviceIdType.MESH
PS = 12
ITERS = 2
FB = 32
NB = 32
NR = 8
NX = 4
GF = 8
NG = FB // GF
ROWS = 2 * 4 * GF
HALF = NG * ROWS // 2
ML = 32
SL = 128
NK = FB * NB
TW = 768
NQ = 3
WM = 2 * NQ
WP = 2 * PS
F32 = jnp.float32
BF16 = jnp.bfloat16


def tables():
    index = np.arange(NK)
    phases = (index[:, None] * index[None, :]) % (2 * NK)
    angles = phases * (2.0 * math.pi / (2 * NK))
    return np.stack([np.cos(angles), np.sin(angles)]).astype(np.float32)


def reorder_rows(start, rows, count):
    index = start + lax.broadcasted_iota(jnp.int32, (rows, 1), 0)
    item = (index * 43691) >> 19
    target = (index - PS * item) * count + item
    lane = lax.broadcasted_iota(jnp.int32, (rows, PS * count), 1)
    return jnp.where(lane == target, 1.0, 0.0).astype(BF16)


def spreading():
    row = lax.broadcasted_iota(jnp.int32, (4 * ML, 4 * GF * ML), 0)
    lane = lax.broadcasted_iota(jnp.int32, (4 * ML, 4 * GF * ML), 1)
    hit = (lane // (GF * ML) == row // ML) & (lax.rem(lane, ML) == lax.rem(row, ML))
    return jnp.where(hit, 1.0, 0.0).astype(BF16)


MINUS_AT = (((3, 11), (5, 13), (2, 10)), ((19, 27), (21, 29), (18, 26)))
PLUS_AT = (
    (0, 4, 8, 12, 2, 6, 10, 14, 1, 7, 9, 15),
    (18, 22, 26, 30, 16, 20, 24, 28, 19, 21, 27, 29),
)


def kernel(
    refl_hbm, tab_hbm, plus_hbm, onm_ref, onp_ref,
    out_minus, out_plus,
    plus_ref, refl, refl_t, tab_full, tab, perm, perm_m, spread, pinit, psnd, gath, msnd, xm, ymsnd, ym, wide,
    partial, from_far, from_x, from_y, sums, rests, xsnd, xp, ypsnd, wp, eo,
    load_sem, gath_send, gath_recv, xm_send, xm_recv, ym_send, ym_recv, rs_send, rs_recv, xp_send, xp_recv,
    wp_send, wp_recv,
):
    me_f = lax.axis_index("freq")
    me_r = lax.axis_index("rcv")
    part = me_f // (NB // 2)
    z_half = lax.rem(me_f, NB // 2) // 8
    me_x, me_y = me_r // 2, lax.rem(me_r, 2)
    beside = me_x * 2 + (1 - me_y)

    def along_x(i):
        return lax.rem(me_x + i, NX)


    load_refl = pltpu.make_async_copy(refl_hbm, refl, load_sem.at[0])
    load_tab = pltpu.make_async_copy(tab_hbm.at[part], tab_full, load_sem.at[1])
    load_plus = pltpu.make_async_copy(plus_hbm, plus_ref, load_sem.at[2])
    load_plus.start()
    load_refl.start()
    load_tab.start()

    barrier = pltpu.get_barrier_semaphore()

    def greet_f(i, _):
        pl.semaphore_signal(
            barrier, inc=1, device_id={"freq": lax.rem(me_f + i, NB), "rcv": me_r}, device_id_type=MESH
        )
        return 0

    def greet_r(i, _):
        pl.semaphore_signal(
            barrier, inc=1, device_id={"freq": me_f, "rcv": lax.rem(me_r + i, NR)}, device_id_type=MESH
        )
        return 0

    lax.fori_loop(1, NB, greet_f, 0)
    lax.fori_loop(1, NR, greet_r, 0)

    row32 = lax.broadcasted_iota(jnp.int32, (FB, 128), 0)
    k_scale = jnp.where((row32 == 0) & (me_f == 0), 0.5, 1.0).astype(F32)
    my_rows = pl.ds(pl.multiple_of(me_f * FB, FB), FB)

    def remote_f(src, dst, send, recv, to):
        return pltpu.make_async_remote_copy(
            src_ref=src, dst_ref=dst, send_sem=send, recv_sem=recv,
            device_id={"freq": to, "rcv": me_r}, device_id_type=MESH,
        )

    def remote_r(src, dst, send, recv, to):
        return pltpu.make_async_remote_copy(
            src_ref=src, dst_ref=dst, send_sem=send, recv_sem=recv,
            device_id={"freq": me_f, "rcv": to}, device_id_type=MESH,
        )

    def await_bytes(ref, sem):
        pltpu.make_async_copy(ref, ref, sem).wait()

    def any_of(places):
        found = me_f == places[0]
        for place in places[1:]:
            found = found | (me_f == place)
        return found

    def minus_places(q):
        return [place for c in range(2) for place in MINUS_AT[c][q]]

    def plus_places(q):
        return [PLUS_AT[c][4 * q + i] for c in range(2) for i in range(4)]

    def row_x(i):
        return along_x(i) * 2 + me_y

    def send_plus(it, q):
        gath[it, q, me_r] = psnd[it, q]
        dst = gath.at[it, q, me_r]
        for i in (1, 3):
            remote_r(psnd.at[it, q], dst, gath_send.at[it], gath_recv.at[it, q, 0], row_x(i)).start()
        remote_r(psnd.at[it, q], dst, gath_send.at[it], gath_recv.at[it, q, 1], beside).start()

    def pass_plus(it, q):
        def pass_on(r, start, rows, sem, to):
            block = gath.at[it, q, r, pl.ds(start, rows)]
            remote_r(block, block, gath_send.at[it], gath_recv.at[it, q, sem], to).start()

        await_bytes(gath.at[it, q, 0], gath_recv.at[it, q, 1])
        pass_on(beside, 0, 4 * ROWS, 2, row_x(2))
        pass_on(beside, 0, ROWS, 4, row_x(1))
        pass_on(beside, 0, ROWS, 3, row_x(3))
        await_bytes(gath.at[it, q, pl.ds(0, 2)], gath_recv.at[it, q, 0])
        pass_on(row_x(1), ROWS, 3 * ROWS, 5, beside)
        pass_on(row_x(3), ROWS, 3 * ROWS, 5, beside)
        pass_on(row_x(3), 0, HALF, 4, row_x(1))
        pass_on(row_x(1), HALF, HALF, 3, row_x(3))

    def fill_perm(i, _):
        perm[pl.ds(pl.multiple_of(i * 128, 128), 128), :] = reorder_rows(i * 128, 128, SL)
        return 0

    lax.fori_loop(0, PS, fill_perm, 0)
    load_plus.wait()
    high = plus_ref[...].astype(BF16)
    left = plus_ref[...] - high.astype(F32)
    middle = left.astype(BF16)
    small = (left - middle.astype(F32)).astype(BF16)
    split = jnp.dot(jnp.concatenate([high, middle, small], axis=0), perm[...], preferred_element_type=F32)
    first = split[: 2 * FB]
    for q in range(NQ):
        for g in range(NG):
            parts = [
                first[c * FB + g * GF : c * FB + (g + 1) * GF, p * SL : (p + 1) * SL]
                for c in range(2)
                for p in range(4 * q, 4 * q + 4)
            ]
            psnd[0, q, g * ROWS : (g + 1) * ROWS, :] = jnp.concatenate(parts, axis=0).astype(BF16)
    pl.semaphore_wait(barrier, NB - 1 + NR - 1)
    for q in range(NQ):
        send_plus(0, q)

    exact = first + (split[2 * FB : 4 * FB] + split[4 * FB :])
    for c in range(2):
        for p in range(PS):
            pinit[p // 4, c * 4 + p % 4] = exact[c * FB : (c + 1) * FB, p * SL : (p + 1) * SL]

    spread[...] = spreading()
    perm_m[...] = reorder_rows(0, ML * PS, ML)
    load_tab.wait()

    def split_tab(i, _):
        rows = pl.ds(pl.multiple_of(i * 128, 128), 128)
        values = tab_full[rows, :]
        top = values.astype(BF16)
        tab[0, rows, :] = top
        tab[1, rows, :] = (values - top.astype(F32)).astype(BF16)
        return 0

    lax.fori_loop(0, NK // 128, split_tab, 0)
    load_refl.wait()
    for g in range(NG):
        for c in range(2):
            block = refl[c * FB * ML + g * GF * ML : c * FB * ML + (g + 1) * GF * ML, :]
            refl_t[g, :, c * GF * ML : (c + 1) * GF * ML] = jnp.transpose(block)

    def window(x, onsets, y, send_chunk, chunks):
        until = jnp.transpose(jnp.broadcast_to(onsets, (128, 128)))
        until = jnp.concatenate([until, until], axis=1)
        traces = jnp.transpose(x[...])
        for n in range(TW // 256):
            cols = slice(n * 256, (n + 1) * 256)
            in_time = jnp.dot(traces, tab[0, :, cols], preferred_element_type=F32)
            in_time += jnp.dot(traces, tab[1, :, cols], preferred_element_type=F32)
            time = n * 256 + lax.broadcasted_iota(jnp.int32, (128, 256), 1)
            factor = jnp.where(time == 0, 1.0 / NK, 2.0 / NK).astype(F32)
            in_time = jnp.where(time < until, in_time * factor, 0.0)
            top = in_time.astype(BF16)
            eo[:128, cols] = top
            eo[128:, cols] = (in_time - top.astype(F32)).astype(BF16)
        for n in chunks:
            cols = pl.ds(pl.multiple_of(n * 256, 256), 256)
            both = jnp.dot(eo[...], tab[0, :TW, cols], preferred_element_type=F32)
            small = jnp.dot(eo[:128, :], tab[1, :TW, cols], preferred_element_type=F32)
            y[cols, :] = jnp.transpose(both[:128] + (both[128:] + small)).astype(BF16)
            send_chunk(n * (256 // FB), 256 // FB)

    half = ROWS // 2
    lane = lax.broadcasted_iota(jnp.int32, (half, GF * ML), 1)
    row = lax.broadcasted_iota(jnp.int32, (half, GF * ML), 0)
    same = lax.rem(row, GF) == lane // ML
    quad_lane = lax.broadcasted_iota(jnp.int32, (GF, 128), 1) // ML

    def refl_rows(c, g):
        return slice(c * FB * ML + g * GF * ML, c * FB * ML + (g + 1) * GF * ML)

    def forward(it, q):
        blocks = ([], [])
        for g in range(NG):
            if g == 0:
                await_bytes(gath.at[it, q, 0, pl.ds(0, 3 * ROWS)], gath_recv.at[it, q, 3])
                await_bytes(gath.at[it, q, 0, pl.ds(0, 3 * ROWS)], gath_recv.at[it, q, 4])
                await_bytes(gath.at[it, q, 0], gath_recv.at[it, q, 2])
            if g == 1:
                await_bytes(gath.at[it, q, pl.ds(0, 2), pl.ds(0, 3 * ROWS)], gath_recv.at[it, q, 5])
            rows = slice(g * ROWS, (g + 1) * ROWS)
            values = jnp.concatenate([gath[it, q, r, rows, :] for r in range(NR)], axis=1)
            both = jnp.dot(values, refl_t[g], preferred_element_type=F32)
            a, b = both[:, : GF * ML], both[:, GF * ML :]
            parts = (a[:half] - b[half:], b[:half] + a[half:])
            for c in range(2):
                own = jnp.where(same, parts[c], 0.0)
                own = own[:, :128] + own[:, 128:]
                own = own + pltpu.roll(own, 64, 1)
                own = own + pltpu.roll(own, 32, 1)
                block = jnp.zeros((GF, 128), F32)
                for i in range(4):
                    block = jnp.where(quad_lane == i, own[i * GF : (i + 1) * GF], block)
                blocks[c].append(block)
        for c in range(2):
            msnd[it, q, c] = (jnp.concatenate(blocks[c], axis=0) * k_scale).astype(BF16)
            for to in MINUS_AT[c][q]:

                @pl.when(me_f == to)
                def _():
                    xm[it, my_rows, :] = msnd[it, q, c]

                @pl.when(me_f != to)
                def _():
                    remote_f(msnd.at[it, q, c], xm.at[it, my_rows], xm_send.at[it], xm_recv.at[it], to).start()

    def scatter(it, buffer, dst, send, recv):
        def send_chunk(begin, count):
            def one(i, _):
                to = begin + i
                rows = pl.ds(pl.multiple_of(to * FB, FB), FB)

                @pl.when(to == me_f)
                def _():
                    dst[...] = buffer[it, rows, :]

                @pl.when(to != me_f)
                def _():
                    remote_f(buffer.at[it, rows], dst, send, recv, to).start()

                return 0

            lax.fori_loop(0, count, one, 0)

        return send_chunk

    def window_minus(it, q):
        @pl.when(any_of(minus_places(q)))
        def _():
            await_bytes(xm.at[it, pl.ds(0, NK - FB)], xm_recv.at[it])
            onsets = jnp.concatenate([onm_ref[4 * q + i : 4 * q + i + 1, :] for i in range(4)], axis=1)
            send_chunk = scatter(it, ymsnd, ym.at[it, q, part], ym_send.at[it], ym_recv.at[it, q])
            window(xm.at[it], onsets, ymsnd.at[it], send_chunk, (z_half, z_half + 2))

    def adjoint(it, q):
        here = any_of(minus_places(q))

        @pl.when(here)
        def _():
            await_bytes(ym.at[it, q, pl.ds(0, 1)], ym_recv.at[it, q])

        @pl.when(jnp.logical_not(here))
        def _():
            await_bytes(ym.at[it, q], ym_recv.at[it, q])

        spread_rows = jnp.dot(ym[it, q].reshape(2 * FB, 128), spread[...], preferred_element_type=F32)
        row_s = lax.broadcasted_iota(jnp.int32, (2 * FB, 1024), 0)
        lane_s = lax.broadcasted_iota(jnp.int32, (2 * FB, 1024), 1)
        wide[...] = jnp.where(lax.rem(row_s, GF) == lax.rem(lane_s // ML, GF), spread_rows, 0.0)
        for g in range(NG):
            blocks = [wide[c * FB + g * GF : c * FB + (g + 1) * GF, :] for c in range(2)]
            re, im = [
                jnp.concatenate([block[:, i * 256 : (i + 1) * 256] for i in range(4)], axis=0) for block in blocks
            ]
            left = jnp.concatenate([re, im], axis=0).astype(BF16)
            right = jnp.concatenate([im, -re], axis=0).astype(BF16)
            for n in range(4):
                cols = slice(n * 256, (n + 1) * 256)
                out = jnp.dot(left, refl[refl_rows(0, g), cols], preferred_element_type=F32)
                out += jnp.dot(right, refl[refl_rows(1, g), cols], preferred_element_type=F32)
                out = out.astype(BF16)
                for y in range(2):
                    partial[it, q, n, y, g * ROWS : (g + 1) * ROWS, :] = out[:, y * SL : (y + 1) * SL]

        def send(x, y, start, rows, dst, sem, to):
            src = partial.at[it, q, x, y, pl.ds(start, rows)]
            remote_r(src, dst, rs_send.at[it], rs_recv.at[it, q, sem], to).start()

        send(along_x(2), 1 - me_y, 0, 4 * ROWS, from_far.at[it, q], 0, row_x(2))
        for k, i in enumerate((1, 3)):
            send(along_x(i), 1 - me_y, ROWS, 3 * ROWS, from_y.at[it, q, k], 3, beside)
        for k, i in enumerate((1, 3)):
            there = from_x.at[it, q, 1 - k]
            send(along_x(2), me_y, k * HALF, HALF, there.at[pl.ds(0, HALF)], 2 - k, row_x(i))
            send(along_x(i), 1 - me_y, 0, ROWS, there.at[pl.ds(HALF, ROWS)], 2 - k, row_x(i))

    def pass_sums(it, q):
        def pass_on(total, slot, sem, to):
            sums[it, q, slot] = total.astype(BF16)
            remote_r(
                sums.at[it, q, slot], rests.at[it, q, sem - 4], rs_send.at[it], rs_recv.at[it, q, sem], to
            ).start()

        await_bytes(from_x.at[it, q, 0], rs_recv.at[it, q, 1])
        await_bytes(from_x.at[it, q, 1], rs_recv.at[it, q, 2])
        await_bytes(from_far.at[it, q], rs_recv.at[it, q, 0])
        total = partial[it, q, me_x, 1 - me_y].astype(F32) + from_far[it, q].astype(F32)
        quarter = from_x[it, q, 0, HALF:, :].astype(F32) + from_x[it, q, 1, HALF:, :].astype(F32)
        pass_on(jnp.concatenate([total[:ROWS] + quarter, total[ROWS:]], axis=0), 2, 6, beside)
        await_bytes(from_y.at[it, q], rs_recv.at[it, q, 3])
        for k, i in enumerate((1, 3)):
            total = partial[it, q, along_x(i), me_y].astype(F32)
            more = from_y[it, q, k].astype(F32)
            half = from_x[it, q, 1 - k, :HALF, :].astype(F32)
            if k == 0:
                pieces = [total[:ROWS] + half[:ROWS], total[ROWS:HALF] + half[ROWS:] + more[:ROWS]]
                pieces.append(total[HALF:] + more[ROWS:])
            else:
                pieces = [total[:ROWS], total[ROWS:HALF] + more[:ROWS], total[HALF:] + half + more[ROWS:]]
            pass_on(jnp.concatenate(pieces, axis=0), k, 5 - k, row_x(i))

    def add_up(it, q):
        total = partial[it, q, me_x, me_y].astype(F32)
        for k in range(3):
            await_bytes(rests.at[it, q, k], rs_recv.at[it, q, 4 + k])
            total += rests[it, q, k].astype(F32)
        for c in range(2):
            for i in range(4):
                to = PLUS_AT[c][4 * q + i]
                at = c * 4 + i
                block = jnp.concatenate(
                    [total[g * ROWS + at * GF : g * ROWS + (at + 1) * GF] for g in range(NG)], axis=0
                )
                xsnd[it, q, at] = (block * k_scale).astype(BF16)

                @pl.when(me_f == to)
                def _():
                    xp[it, my_rows, :] = xsnd[it, q, at]

                @pl.when(me_f != to)
                def _():
                    remote_f(xsnd.at[it, q, at], xp.at[it, my_rows], xp_send.at[it], xp_recv.at[it], to).start()

    def window_plus(it, q):
        @pl.when(any_of(plus_places(q)))
        def _():
            await_bytes(xp.at[it, pl.ds(0, NK - FB)], xp_recv.at[it])
            point = jnp.int32(0)
            for i in range(1, 4):
                point = jnp.where(any_of([PLUS_AT[c][4 * q + i] for c in range(2)]), i, point)
            onsets = onp_ref[pl.ds(4 * q + point, 1), :]
            send_chunk = scatter(it, ypsnd, wp.at[it, q, part * 4 + point], wp_send.at[it], wp_recv.at[it, q])
            window(xp.at[it], onsets, ypsnd.at[it], send_chunk, range(NK // 256))

    def update(it, q):
        here = any_of(plus_places(q))

        @pl.when(here)
        def _():
            await_bytes(wp.at[it, q, pl.ds(0, 7)], wp_recv.at[it, q])

        @pl.when(jnp.logical_not(here))
        def _():
            await_bytes(wp.at[it, q], wp_recv.at[it, q])

        @pl.when(it < ITERS - 1)
        def _():
            new = pinit[q] + wp[it, q].astype(F32)
            for g in range(NG):
                rows = new[:, g * GF : (g + 1) * GF, :].reshape(ROWS, SL)
                psnd[it + 1, q, g * ROWS : (g + 1) * ROWS, :] = rows.astype(BF16)
            send_plus(it + 1, q)

        @pl.when(it == ITERS - 1)
        def _():
            change = jnp.concatenate(
                [jnp.concatenate([wp[it, q, c * 4 + i] for i in range(4)], axis=1) for c in range(2)], axis=0
            )
            dims = (((1,), (1,)), ((), ()))
            change = lax.dot_general(
                change, perm[:, q * 4 * SL : (q + 1) * 4 * SL], dims, preferred_element_type=F32
            )
            if q < NQ - 1:
                plus_ref[...] = change if q == 0 else plus_ref[...] + change
            else:
                out_plus[...] = (plus_ref[...] + change).astype(BF16)

    def finish_minus(it):
        @pl.when(it == ITERS - 1)
        def _():
            minus = jnp.concatenate(
                [jnp.concatenate([ym[it, q, c] for q in range(NQ)], axis=1) for c in range(2)], axis=0
            )
            dims = (((1,), (1,)), ((), ()))
            minus = lax.dot_general(minus, perm_m[...], dims, preferred_element_type=F32)
            out_minus[...] = minus.astype(BF16)

    def iteration(it, _):
        pass_plus(it, 0)
        pass_plus(it, 1)
        pass_plus(it, 2)
        forward(it, 0)
        forward(it, 1)
        forward(it, 2)
        window_minus(it, 0)
        window_minus(it, 1)
        window_minus(it, 2)
        adjoint(it, 0)
        adjoint(it, 1)
        adjoint(it, 2)
        pass_sums(it, 0)
        pass_sums(it, 1)
        pass_sums(it, 2)
        add_up(it, 0)
        add_up(it, 1)
        add_up(it, 2)
        window_plus(it, 0)
        finish_minus(it)
        window_plus(it, 1)
        window_plus(it, 2)
        update(it, 0)
        update(it, 1)
        update(it, 2)
        return 0

    lax.fori_loop(0, ITERS, iteration, 0)

    is_minus = any_of([place for q in range(NQ) for place in minus_places(q)])
    is_plus = any_of([place for q in range(NQ) for place in plus_places(q)])

    def drain(it, _):
        await_bytes(gath.at[it, :, pl.ds(0, NR - 1)], gath_send.at[it])
        await_bytes(gath.at[it, :, pl.ds(0, NR - 1)], rs_send.at[it])

        @pl.when(is_minus)
        def _():
            await_bytes(xm.at[it, pl.ds(0, (2 * WM - 1) * FB)], xm_send.at[it])
            await_bytes(ymsnd.at[it, pl.ds(0, NK // 2 - FB)], ym_send.at[it])

        @pl.when(jnp.logical_not(is_minus))
        def _():
            await_bytes(xm.at[it, pl.ds(0, 2 * WM * FB)], xm_send.at[it])

        @pl.when(is_plus)
        def _():
            await_bytes(xp.at[it, pl.ds(0, (WP - 1) * FB)], xp_send.at[it])
            await_bytes(ypsnd.at[it, pl.ds(0, NK - FB)], wp_send.at[it])

        @pl.when(jnp.logical_not(is_plus))
        def _():
            await_bytes(xsnd.at[it], xp_send.at[it])

        return 0

    lax.fori_loop(0, ITERS, drain, 0)


def widen(minus_ref, change_ref, plus_ref, out_minus, out_plus):
    out_minus[...] = minus_ref[...].astype(F32)
    out_plus[...] = plus_ref[...] + change_ref[...].astype(F32)


def local(reflection, plus_init, onset_receiver, onset_source):
    onm = jnp.transpose(onset_receiver)
    onp = jnp.transpose(onset_source)
    vmem = pl.BlockSpec(memory_space=pltpu.VMEM)
    hbm = pl.BlockSpec(memory_space=pl.ANY)
    dma = pltpu.SemaphoreType.DMA
    plus_rows = plus_init.reshape(2 * FB, SL * PS)
    minus, change = pl.pallas_call(
        kernel,
        out_shape=(
            jax.ShapeDtypeStruct((2 * FB, ML * PS), BF16),
            jax.ShapeDtypeStruct((2 * FB, SL * PS), BF16),
        ),
        in_specs=[hbm, hbm, hbm, vmem, vmem],
        out_specs=(vmem, vmem),
        scratch_shapes=[
            pltpu.VMEM((2 * FB, SL * PS), F32),
            pltpu.VMEM((2 * FB * ML, 1024), BF16),
            pltpu.VMEM((NG, 1024, 2 * GF * ML), BF16),
            pltpu.VMEM((NK, NK), F32),
            pltpu.VMEM((2, NK, NK), BF16),
            pltpu.VMEM((SL * PS, SL * PS), BF16),
            pltpu.VMEM((ML * PS, ML * PS), BF16),
            pltpu.VMEM((4 * ML, 4 * GF * ML), BF16),
            pltpu.VMEM((NQ, 8, FB, SL), F32),
            pltpu.VMEM((ITERS, NQ, NG * ROWS, SL), BF16),
            pltpu.VMEM((ITERS, NQ, NR, NG * ROWS, SL), BF16),
            pltpu.VMEM((ITERS, NQ, 2, FB, 128), BF16),
            pltpu.VMEM((ITERS, NK, 128), BF16),
            pltpu.VMEM((ITERS, NK, 128), BF16),
            pltpu.VMEM((ITERS, NQ, 2, FB, 128), BF16),
            pltpu.VMEM((2 * FB, 1024), F32),
            pltpu.VMEM((ITERS, NQ, NX, 2, 4 * ROWS, SL), BF16),
            pltpu.VMEM((ITERS, NQ, 4 * ROWS, SL), BF16),
            pltpu.VMEM((ITERS, NQ, 2, 3 * ROWS, SL), BF16),
            pltpu.VMEM((ITERS, NQ, 2, 3 * ROWS, SL), BF16),
            pltpu.VMEM((ITERS, NQ, 3, 4 * ROWS, SL), BF16),
            pltpu.VMEM((ITERS, NQ, 3, 4 * ROWS, SL), BF16),
            pltpu.VMEM((ITERS, NQ, 8, FB, SL), BF16),
            pltpu.VMEM((ITERS, NK, SL), BF16),
            pltpu.VMEM((ITERS, NK, SL), BF16),
            pltpu.VMEM((ITERS, NQ, 8, FB, SL), BF16),
            pltpu.VMEM((256, TW), BF16),
            dma((3,)),
            dma((ITERS,)), dma((ITERS, NQ, 6)),
            dma((ITERS,)), dma((ITERS,)),
            dma((ITERS,)), dma((ITERS, NQ)),
            dma((ITERS,)), dma((ITERS, NQ, 7)),
            dma((ITERS,)), dma((ITERS,)),
            dma((ITERS,)), dma((ITERS, NQ)),
        ],
        compiler_params=pltpu.CompilerParams(
            collective_id=0, has_side_effects=True, vmem_limit_bytes=56 * 1024 * 1024
        ),
    )(
        reflection.reshape(2 * FB * ML, 1024),
        jnp.asarray(tables()),
        plus_rows,
        onm,
        onp,
    )
    out_minus, out_plus = pl.pallas_call(
        widen,
        out_shape=(
            jax.ShapeDtypeStruct((2 * FB, ML * PS), F32),
            jax.ShapeDtypeStruct((2 * FB, SL * PS), F32),
        ),
        in_specs=[vmem, vmem, vmem],
        out_specs=(vmem, vmem),
    )(minus, change, plus_rows)
    return out_minus.reshape(2, FB, ML * PS), out_plus.reshape(2, FB, SL * PS)


def solution(mesh):
    return jax.shard_map(
        local,
        mesh=mesh,
        in_specs=(
            P(None, "freq", "rcv", None),
            P(None, "freq", "rcv"),
            P("rcv", None),
            P("rcv", None),
        ),
        out_specs=(P(None, "freq", "rcv"), P(None, "freq", "rcv")),
        check_vma=False,
    )
```

```python
import math

import jax
import jax.numpy as jnp
import numpy as np
from jax import lax
from jax.experimental import pallas as pl
from jax.experimental.pallas import tpu as pltpu
from jax.sharding import PartitionSpec as P

MESH = pl.DeviceIdType.MESH
PS = 12
ITERS = 2
FB = 32
NB = 32
NR = 8
NX = 4
GF = 8
NG = FB // GF
ROWS = 2 * 4 * GF
HALF = NG * ROWS // 2
ML = 32
SL = 128
NK = FB * NB
TW = 768
NQ = 3
WM = 2 * NQ
WP = 2 * PS
F32 = jnp.float32
BF16 = jnp.bfloat16


def tables():
    index = np.arange(NK)
    phases = (index[:, None] * index[None, :]) % (2 * NK)
    angles = phases * (2.0 * math.pi / (2 * NK))
    return np.stack([np.cos(angles), np.sin(angles)]).astype(np.float32)


def reorder_rows(start, rows, count):
    index = start + lax.broadcasted_iota(jnp.int32, (rows, 1), 0)
    item = (index * 43691) >> 19
    target = (index - PS * item) * count + item
    lane = lax.broadcasted_iota(jnp.int32, (rows, PS * count), 1)
    return jnp.where(lane == target, 1.0, 0.0).astype(BF16)


def reorder_back_rows(start, rows, count):
    index = start + lax.broadcasted_iota(jnp.int32, (rows, 1), 0)
    point = index // count
    target = (index - point * count) * PS + point
    lane = lax.broadcasted_iota(jnp.int32, (rows, PS * count), 1)
    return jnp.where(lane == target, 1.0, 0.0).astype(BF16)


def spreading():
    row = lax.broadcasted_iota(jnp.int32, (4 * ML, 4 * GF * ML), 0)
    lane = lax.broadcasted_iota(jnp.int32, (4 * ML, 4 * GF * ML), 1)
    hit = (lane // (GF * ML) == row // ML) & (lax.rem(lane, ML) == lax.rem(row, ML))
    return jnp.where(hit, 1.0, 0.0).astype(BF16)


MINUS_AT = (((3, 11), (5, 13), (2, 10)), ((19, 27), (21, 29), (18, 26)))
PLUS_AT = (
    (0, 4, 8, 12, 2, 6, 10, 14, 1, 7, 9, 15),
    (18, 22, 26, 30, 16, 20, 24, 28, 19, 21, 27, 29),
)


def kernel(
    refl_hbm, tab_hbm, plus_hbm, onm_ref, onp_ref,
    out_minus, out_plus,
    plus_ref, refl, refl_t, tab_full, tab, perm, perm_back, perm_m, spread, pinit, psnd, gath, msnd, xm, ymsnd, ym, wide,
    partial, from_far, from_x, from_y, sums, rests, xsnd, xp, ypsnd, wp, eo,
    load_sem, gath_send, gath_recv, xm_send, xm_recv, ym_send, ym_recv, rs_send, rs_recv, xp_send, xp_recv,
    wp_send, wp_recv,
):
    me_f = lax.axis_index("freq")
    me_r = lax.axis_index("rcv")
    part = me_f // (NB // 2)
    z_half = lax.rem(me_f, NB // 2) // 8
    far_first = [2 * y + z for z in (1 - z_half, z_half) for y in (1 - part, part)]
    me_x, me_y = me_r // 2, lax.rem(me_r, 2)
    beside = me_x * 2 + (1 - me_y)

    def along_x(i):
        return lax.rem(me_x + i, NX)


    load_refl = pltpu.make_async_copy(refl_hbm, refl, load_sem.at[0])
    load_tab = pltpu.make_async_copy(tab_hbm.at[part], tab_full, load_sem.at[1])
    load_plus = pltpu.make_async_copy(plus_hbm, plus_ref, load_sem.at[2])
    load_plus.start()
    load_refl.start()
    load_tab.start()

    barrier = pltpu.get_barrier_semaphore()

    def greet_f(i, _):
        pl.semaphore_signal(
            barrier, inc=1, device_id={"freq": lax.rem(me_f + i, NB), "rcv": me_r}, device_id_type=MESH
        )
        return 0

    def greet_r(i, _):
        pl.semaphore_signal(
            barrier, inc=1, device_id={"freq": me_f, "rcv": lax.rem(me_r + i, NR)}, device_id_type=MESH
        )
        return 0

    lax.fori_loop(1, NR, greet_r, 0)
    lax.fori_loop(NB // 2 + 1, NB, greet_f, 0)
    lax.fori_loop(1, NB // 2 + 1, greet_f, 0)

    row32 = lax.broadcasted_iota(jnp.int32, (FB, 128), 0)
    k_scale = jnp.where((row32 == 0) & (me_f == 0), 0.5, 1.0).astype(F32)
    my_rows = pl.ds(pl.multiple_of(me_f * FB, FB), FB)

    def remote_f(src, dst, send, recv, to):
        return pltpu.make_async_remote_copy(
            src_ref=src, dst_ref=dst, send_sem=send, recv_sem=recv,
            device_id={"freq": to, "rcv": me_r}, device_id_type=MESH,
        )

    def remote_r(src, dst, send, recv, to):
        return pltpu.make_async_remote_copy(
            src_ref=src, dst_ref=dst, send_sem=send, recv_sem=recv,
            device_id={"freq": me_f, "rcv": to}, device_id_type=MESH,
        )

    def await_bytes(ref, sem):
        pltpu.make_async_copy(ref, ref, sem).wait()

    def any_of(places):
        found = me_f == places[0]
        for place in places[1:]:
            found = found | (me_f == place)
        return found

    def minus_places(q):
        return [place for c in range(2) for place in MINUS_AT[c][q]]

    def plus_places(q):
        return [PLUS_AT[c][4 * q + i] for c in range(2) for i in range(4)]

    def row_x(i):
        return along_x(i) * 2 + me_y

    def send_plus(it, q):
        gath[it, q, me_r] = psnd[it, q]
        dst = gath.at[it, q, me_r]
        for i in (1, 3):
            remote_r(psnd.at[it, q], dst, gath_send.at[it], gath_recv.at[it, q, 0], row_x(i)).start()
        remote_r(psnd.at[it, q], dst, gath_send.at[it], gath_recv.at[it, q, 1], beside).start()

    def pass_plus(it, q):
        def pass_on(r, start, rows, sem, to):
            block = gath.at[it, q, r, pl.ds(start, rows)]
            remote_r(block, block, gath_send.at[it], gath_recv.at[it, q, sem], to).start()

        await_bytes(gath.at[it, q, pl.ds(0, 2)], gath_recv.at[it, q, 0])
        pass_on(row_x(1), ROWS, 3 * ROWS, 5, beside)
        pass_on(row_x(3), ROWS, 3 * ROWS, 5, beside)
        pass_on(row_x(3), 0, HALF, 4, row_x(1))
        pass_on(row_x(1), HALF, HALF, 3, row_x(3))
        await_bytes(gath.at[it, q, 0], gath_recv.at[it, q, 1])
        pass_on(beside, 0, 4 * ROWS, 2, row_x(2))
        pass_on(beside, 0, ROWS, 4, row_x(1))
        pass_on(beside, 0, ROWS, 3, row_x(3))

    def fill_perm(i, _):
        perm[pl.ds(pl.multiple_of(i * 128, 128), 128), :] = reorder_rows(i * 128, 128, SL)
        return 0

    lax.fori_loop(0, PS, fill_perm, 0)
    load_plus.wait()
    high = plus_ref[...].astype(BF16)
    left = plus_ref[...] - high.astype(F32)
    middle = left.astype(BF16)
    small = (left - middle.astype(F32)).astype(BF16)
    split = jnp.dot(jnp.concatenate([high, middle, small], axis=0), perm[...], preferred_element_type=F32)
    first = split[: 2 * FB]
    for q in range(NQ):
        for g in range(NG):
            parts = [
                first[c * FB + g * GF : c * FB + (g + 1) * GF, p * SL : (p + 1) * SL]
                for c in range(2)
                for p in range(4 * q, 4 * q + 4)
            ]
            psnd[0, q, g * ROWS : (g + 1) * ROWS, :] = jnp.concatenate(parts, axis=0).astype(BF16)
    pl.semaphore_wait(barrier, NB - 1 + NR - 1)
    for q in range(NQ):
        send_plus(0, q)

    exact = first + (split[2 * FB : 4 * FB] + split[4 * FB :])
    for c in range(2):
        for p in range(PS):
            pinit[p // 4, c * 4 + p % 4] = exact[c * FB : (c + 1) * FB, p * SL : (p + 1) * SL]

    spread[...] = spreading()
    perm_m[...] = reorder_back_rows(0, ML * PS, ML)

    def fill_back(i, _):
        perm_back[pl.ds(pl.multiple_of(i * 128, 128), 128), :] = reorder_back_rows(i * 128, 128, SL)
        return 0

    lax.fori_loop(0, PS, fill_back, 0)
    load_tab.wait()

    def round_tab(i, _):
        rows = pl.ds(pl.multiple_of(i * 128, 128), 128)
        tab[rows, :] = tab_full[rows, :].astype(BF16)
        return 0

    lax.fori_loop(0, NK // 128, round_tab, 0)
    load_refl.wait()
    for g in range(NG):
        for c in range(2):
            block = refl[c * FB * ML + g * GF * ML : c * FB * ML + (g + 1) * GF * ML, :]
            refl_t[g, :, c * GF * ML : (c + 1) * GF * ML] = jnp.transpose(block)

    def window(x, onsets, y, send_chunk, chunks):
        until = jnp.transpose(jnp.broadcast_to(onsets, (128, 128)))
        until = jnp.concatenate([until, until], axis=1)
        traces = jnp.transpose(x[...])
        for n in range(TW // 256):
            cols = slice(n * 256, (n + 1) * 256)
            in_time = jnp.dot(traces, tab[:, cols], preferred_element_type=F32)
            time = n * 256 + lax.broadcasted_iota(jnp.int32, (128, 256), 1)
            factor = jnp.where(time == 0, 1.0 / NK, 2.0 / NK).astype(F32)
            in_time = jnp.where(time < until, in_time * factor, 0.0)
            top = in_time.astype(BF16)
            eo[:128, cols] = top
            eo[128:, cols] = (in_time - top.astype(F32)).astype(BF16)
        for n in chunks:
            cols = pl.ds(pl.multiple_of(n * 256, 256), 256)
            both = jnp.dot(eo[...], tab[:TW, cols], preferred_element_type=F32)
            y[cols, :] = jnp.transpose(both[:128] + both[128:]).astype(BF16)
            send_chunk(n * (256 // FB), 256 // FB)

    half = ROWS // 2
    lane = lax.broadcasted_iota(jnp.int32, (half, GF * ML), 1)
    row = lax.broadcasted_iota(jnp.int32, (half, GF * ML), 0)
    same = lax.rem(row, GF) == lane // ML
    quad_lane = lax.broadcasted_iota(jnp.int32, (GF, 128), 1) // ML

    def refl_rows(c, g):
        return slice(c * FB * ML + g * GF * ML, c * FB * ML + (g + 1) * GF * ML)

    def forward(it, q):
        blocks = ([], [])
        for g in range(NG):
            if g == 0:
                await_bytes(gath.at[it, q, 0, pl.ds(0, 3 * ROWS)], gath_recv.at[it, q, 3])
                await_bytes(gath.at[it, q, 0, pl.ds(0, 3 * ROWS)], gath_recv.at[it, q, 4])
                await_bytes(gath.at[it, q, 0], gath_recv.at[it, q, 2])
            if g == 1:
                await_bytes(gath.at[it, q, pl.ds(0, 2), pl.ds(0, 3 * ROWS)], gath_recv.at[it, q, 5])
            rows = slice(g * ROWS, (g + 1) * ROWS)
            values = jnp.concatenate([gath[it, q, r, rows, :] for r in range(NR)], axis=1)
            both = jnp.dot(values, refl_t[g], preferred_element_type=F32)
            a, b = both[:, : GF * ML], both[:, GF * ML :]
            parts = (a[:half] - b[half:], b[:half] + a[half:])
            for c in range(2):
                own = jnp.where(same, parts[c], 0.0)
                own = own[:, :128] + own[:, 128:]
                own = own + pltpu.roll(own, 64, 1)
                own = own + pltpu.roll(own, 32, 1)
                block = jnp.zeros((GF, 128), F32)
                for i in range(4):
                    block = jnp.where(quad_lane == i, own[i * GF : (i + 1) * GF], block)
                blocks[c].append(block)
        for c in range(2):
            msnd[it, q, c] = (jnp.concatenate(blocks[c], axis=0) * k_scale).astype(BF16)
            for to in MINUS_AT[c][q]:

                @pl.when(me_f == to)
                def _():
                    xm[it, my_rows, :] = msnd[it, q, c]

                @pl.when(me_f != to)
                def _():
                    remote_f(msnd.at[it, q, c], xm.at[it, my_rows], xm_send.at[it], xm_recv.at[it], to).start()

    def scatter(it, buffer, dst, send, recv):
        def send_chunk(begin, count):
            def one(i, _):
                to = begin + i
                rows = pl.ds(pl.multiple_of(to * FB, FB), FB)

                @pl.when(to == me_f)
                def _():
                    dst[...] = buffer[it, rows, :]

                @pl.when(to != me_f)
                def _():
                    remote_f(buffer.at[it, rows], dst, send, recv, to).start()

                return 0

            lax.fori_loop(0, count, one, 0)

        return send_chunk

    def window_minus(it, q):
        @pl.when(any_of(minus_places(q)))
        def _():
            await_bytes(xm.at[it, pl.ds(0, NK - FB)], xm_recv.at[it])
            onsets = jnp.concatenate([onm_ref[4 * q + i : 4 * q + i + 1, :] for i in range(4)], axis=1)
            send_chunk = scatter(it, ymsnd, ym.at[it, q, part], ym_send.at[it], ym_recv.at[it, q])
            window(xm.at[it], onsets, ymsnd.at[it], send_chunk, far_first[2:])

    def adjoint(it, q):
        here = any_of(minus_places(q))

        @pl.when(here)
        def _():
            await_bytes(ym.at[it, q, pl.ds(0, 1)], ym_recv.at[it, q])

        @pl.when(jnp.logical_not(here))
        def _():
            await_bytes(ym.at[it, q], ym_recv.at[it, q])

        spread_rows = jnp.dot(ym[it, q].reshape(2 * FB, 128), spread[...], preferred_element_type=F32)
        row_s = lax.broadcasted_iota(jnp.int32, (2 * FB, 1024), 0)
        lane_s = lax.broadcasted_iota(jnp.int32, (2 * FB, 1024), 1)
        wide[...] = jnp.where(lax.rem(row_s, GF) == lax.rem(lane_s // ML, GF), spread_rows, 0.0)
        for g in range(NG):
            blocks = [wide[c * FB + g * GF : c * FB + (g + 1) * GF, :] for c in range(2)]
            re, im = [
                jnp.concatenate([block[:, i * 256 : (i + 1) * 256] for i in range(4)], axis=0) for block in blocks
            ]
            left = jnp.concatenate([re, im], axis=0).astype(BF16)
            right = jnp.concatenate([im, -re], axis=0).astype(BF16)
            for n in range(4):
                cols = slice(n * 256, (n + 1) * 256)
                out = jnp.dot(left, refl[refl_rows(0, g), cols], preferred_element_type=F32)
                out += jnp.dot(right, refl[refl_rows(1, g), cols], preferred_element_type=F32)
                out = out.astype(BF16)
                for y in range(2):
                    partial[it, q, n, y, g * ROWS : (g + 1) * ROWS, :] = out[:, y * SL : (y + 1) * SL]

        def send(x, y, start, rows, dst, sem, to):
            src = partial.at[it, q, x, y, pl.ds(start, rows)]
            remote_r(src, dst, rs_send.at[it], rs_recv.at[it, q, sem], to).start()

        send(along_x(2), 1 - me_y, 0, 4 * ROWS, from_far.at[it, q], 0, row_x(2))
        for k, i in enumerate((1, 3)):
            send(along_x(i), 1 - me_y, ROWS, 3 * ROWS, from_y.at[it, q, k], 3, beside)
        for k, i in enumerate((1, 3)):
            there = from_x.at[it, q, 1 - k]
            send(along_x(2), me_y, k * HALF, HALF, there.at[pl.ds(0, HALF)], 2 - k, row_x(i))
            send(along_x(i), 1 - me_y, 0, ROWS, there.at[pl.ds(HALF, ROWS)], 2 - k, row_x(i))

    def pass_sums(it, q):
        def pass_on(total, slot, sem, to):
            sums[it, q, slot] = total.astype(BF16)
            remote_r(
                sums.at[it, q, slot], rests.at[it, q, sem - 4], rs_send.at[it], rs_recv.at[it, q, sem], to
            ).start()

        await_bytes(from_x.at[it, q, 0], rs_recv.at[it, q, 1])
        await_bytes(from_x.at[it, q, 1], rs_recv.at[it, q, 2])
        await_bytes(from_far.at[it, q], rs_recv.at[it, q, 0])
        total = partial[it, q, me_x, 1 - me_y].astype(F32) + from_far[it, q].astype(F32)
        quarter = from_x[it, q, 0, HALF:, :].astype(F32) + from_x[it, q, 1, HALF:, :].astype(F32)
        pass_on(jnp.concatenate([total[:ROWS] + quarter, total[ROWS:]], axis=0), 2, 6, beside)
        await_bytes(from_y.at[it, q], rs_recv.at[it, q, 3])
        for k, i in enumerate((1, 3)):
            total = partial[it, q, along_x(i), me_y].astype(F32)
            more = from_y[it, q, k].astype(F32)
            half = from_x[it, q, 1 - k, :HALF, :].astype(F32)
            if k == 0:
                pieces = [total[:ROWS] + half[:ROWS], total[ROWS:HALF] + half[ROWS:] + more[:ROWS]]
                pieces.append(total[HALF:] + more[ROWS:])
            else:
                pieces = [total[:ROWS], total[ROWS:HALF] + more[:ROWS], total[HALF:] + half + more[ROWS:]]
            pass_on(jnp.concatenate(pieces, axis=0), k, 5 - k, row_x(i))

    def add_up(it, q):
        total = partial[it, q, me_x, me_y].astype(F32)
        for k in range(3):
            await_bytes(rests.at[it, q, k], rs_recv.at[it, q, 4 + k])
            total += rests[it, q, k].astype(F32)
        for c in range(2):
            for i in range(4):
                to = PLUS_AT[c][4 * q + i]
                at = c * 4 + i
                block = jnp.concatenate(
                    [total[g * ROWS + at * GF : g * ROWS + (at + 1) * GF] for g in range(NG)], axis=0
                )
                xsnd[it, q, at] = (block * k_scale).astype(BF16)

                @pl.when(me_f == to)
                def _():
                    xp[it, my_rows, :] = xsnd[it, q, at]

                @pl.when(me_f != to)
                def _():
                    remote_f(xsnd.at[it, q, at], xp.at[it, my_rows], xp_send.at[it], xp_recv.at[it], to).start()

    def window_plus(it, q):
        @pl.when(any_of(plus_places(q)))
        def _():
            await_bytes(xp.at[it, pl.ds(0, NK - FB)], xp_recv.at[it])
            point = jnp.int32(0)
            for i in range(1, 4):
                point = jnp.where(any_of([PLUS_AT[c][4 * q + i] for c in range(2)]), i, point)
            onsets = onp_ref[pl.ds(4 * q + point, 1), :]
            send_chunk = scatter(it, ypsnd, wp.at[it, q, part * 4 + point], wp_send.at[it], wp_recv.at[it, q])
            window(xp.at[it], onsets, ypsnd.at[it], send_chunk, far_first)

    def update(it, q):
        here = any_of(plus_places(q))

        @pl.when(here)
        def _():
            await_bytes(wp.at[it, q, pl.ds(0, 7)], wp_recv.at[it, q])

        @pl.when(jnp.logical_not(here))
        def _():
            await_bytes(wp.at[it, q], wp_recv.at[it, q])

        @pl.when(it < ITERS - 1)
        def _():
            new = pinit[q] + wp[it, q].astype(F32)
            for g in range(NG):
                rows = new[:, g * GF : (g + 1) * GF, :].reshape(ROWS, SL)
                psnd[it + 1, q, g * ROWS : (g + 1) * ROWS, :] = rows.astype(BF16)
            send_plus(it + 1, q)

        @pl.when(it == ITERS - 1)
        def _():
            change = jnp.concatenate(
                [jnp.concatenate([wp[it, q, c * 4 + i] for i in range(4)], axis=1) for c in range(2)], axis=0
            )
            change = jnp.dot(
                change, perm_back[q * 4 * SL : (q + 1) * 4 * SL, :], preferred_element_type=F32
            )
            if q < NQ - 1:
                plus_ref[...] = change if q == 0 else plus_ref[...] + change
            else:
                out_plus[...] = (plus_ref[...] + change).astype(BF16)

    def finish_minus(it):
        @pl.when(it == ITERS - 1)
        def _():
            minus = jnp.concatenate(
                [jnp.concatenate([ym[it, q, c] for q in range(NQ)], axis=1) for c in range(2)], axis=0
            )
            minus = jnp.dot(minus, perm_m[...], preferred_element_type=F32)
            out_minus[...] = minus.astype(BF16)

    def iteration(it, _):
        pass_plus(it, 0)
        pass_plus(it, 1)
        pass_plus(it, 2)
        forward(it, 0)
        forward(it, 1)
        forward(it, 2)
        window_minus(it, 0)
        window_minus(it, 1)
        window_minus(it, 2)
        adjoint(it, 0)
        adjoint(it, 1)
        adjoint(it, 2)
        pass_sums(it, 0)
        pass_sums(it, 1)
        pass_sums(it, 2)
        add_up(it, 0)
        add_up(it, 1)
        add_up(it, 2)
        window_plus(it, 0)
        window_plus(it, 1)
        window_plus(it, 2)
        finish_minus(it)
        update(it, 0)
        update(it, 1)
        update(it, 2)
        return 0

    lax.fori_loop(0, ITERS, iteration, 0)

    is_minus = any_of([place for q in range(NQ) for place in minus_places(q)])
    is_plus = any_of([place for q in range(NQ) for place in plus_places(q)])

    def drain(it, _):
        await_bytes(gath.at[it, :, pl.ds(0, NR - 1)], gath_send.at[it])
        await_bytes(gath.at[it, :, pl.ds(0, NR - 1)], rs_send.at[it])

        @pl.when(is_minus)
        def _():
            await_bytes(xm.at[it, pl.ds(0, (2 * WM - 1) * FB)], xm_send.at[it])
            await_bytes(ymsnd.at[it, pl.ds(0, NK // 2 - FB)], ym_send.at[it])

        @pl.when(jnp.logical_not(is_minus))
        def _():
            await_bytes(xm.at[it, pl.ds(0, 2 * WM * FB)], xm_send.at[it])

        @pl.when(is_plus)
        def _():
            await_bytes(xp.at[it, pl.ds(0, (WP - 1) * FB)], xp_send.at[it])
            await_bytes(ypsnd.at[it, pl.ds(0, NK - FB)], wp_send.at[it])

        @pl.when(jnp.logical_not(is_plus))
        def _():
            await_bytes(xsnd.at[it], xp_send.at[it])

        return 0

    lax.fori_loop(0, ITERS, drain, 0)


def widen(minus_ref, change_ref, plus_ref, out_minus, out_plus):
    out_minus[...] = minus_ref[...].astype(F32)
    out_plus[...] = plus_ref[...] + change_ref[...].astype(F32)


def local(reflection, plus_init, onset_receiver, onset_source):
    onm = jnp.transpose(onset_receiver)
    onp = jnp.transpose(onset_source)
    vmem = pl.BlockSpec(memory_space=pltpu.VMEM)
    hbm = pl.BlockSpec(memory_space=pl.ANY)
    dma = pltpu.SemaphoreType.DMA
    plus_rows = plus_init.reshape(2 * FB, SL * PS)
    minus, change = pl.pallas_call(
        kernel,
        out_shape=(
            jax.ShapeDtypeStruct((2 * FB, ML * PS), BF16),
            jax.ShapeDtypeStruct((2 * FB, SL * PS), BF16),
        ),
        in_specs=[hbm, hbm, hbm, vmem, vmem],
        out_specs=(vmem, vmem),
        scratch_shapes=[
            pltpu.VMEM((2 * FB, SL * PS), F32),
            pltpu.VMEM((2 * FB * ML, 1024), BF16),
            pltpu.VMEM((NG, 1024, 2 * GF * ML), BF16),
            pltpu.VMEM((NK, NK), F32),
            pltpu.VMEM((NK, NK), BF16),
            pltpu.VMEM((SL * PS, SL * PS), BF16),
            pltpu.VMEM((SL * PS, SL * PS), BF16),
            pltpu.VMEM((ML * PS, ML * PS), BF16),
            pltpu.VMEM((4 * ML, 4 * GF * ML), BF16),
            pltpu.VMEM((NQ, 8, FB, SL), F32),
            pltpu.VMEM((ITERS, NQ, NG * ROWS, SL), BF16),
            pltpu.VMEM((ITERS, NQ, NR, NG * ROWS, SL), BF16),
            pltpu.VMEM((ITERS, NQ, 2, FB, 128), BF16),
            pltpu.VMEM((ITERS, NK, 128), BF16),
            pltpu.VMEM((ITERS, NK, 128), BF16),
            pltpu.VMEM((ITERS, NQ, 2, FB, 128), BF16),
            pltpu.VMEM((2 * FB, 1024), F32),
            pltpu.VMEM((ITERS, NQ, NX, 2, 4 * ROWS, SL), BF16),
            pltpu.VMEM((ITERS, NQ, 4 * ROWS, SL), BF16),
            pltpu.VMEM((ITERS, NQ, 2, 3 * ROWS, SL), BF16),
            pltpu.VMEM((ITERS, NQ, 2, 3 * ROWS, SL), BF16),
            pltpu.VMEM((ITERS, NQ, 3, 4 * ROWS, SL), BF16),
            pltpu.VMEM((ITERS, NQ, 3, 4 * ROWS, SL), BF16),
            pltpu.VMEM((ITERS, NQ, 8, FB, SL), BF16),
            pltpu.VMEM((ITERS, NK, SL), BF16),
            pltpu.VMEM((ITERS, NK, SL), BF16),
            pltpu.VMEM((ITERS, NQ, 8, FB, SL), BF16),
            pltpu.VMEM((256, TW), BF16),
            dma((3,)),
            dma((ITERS,)), dma((ITERS, NQ, 6)),
            dma((ITERS,)), dma((ITERS,)),
            dma((ITERS,)), dma((ITERS, NQ)),
            dma((ITERS,)), dma((ITERS, NQ, 7)),
            dma((ITERS,)), dma((ITERS,)),
            dma((ITERS,)), dma((ITERS, NQ)),
        ],
        compiler_params=pltpu.CompilerParams(
            collective_id=0, has_side_effects=True, vmem_limit_bytes=56 * 1024 * 1024
        ),
    )(
        reflection.reshape(2 * FB * ML, 1024),
        jnp.asarray(tables()),
        plus_rows,
        onm,
        onp,
    )
    out_minus, out_plus = pl.pallas_call(
        widen,
        out_shape=(
            jax.ShapeDtypeStruct((2 * FB, ML * PS), F32),
            jax.ShapeDtypeStruct((2 * FB, SL * PS), F32),
        ),
        in_specs=[vmem, vmem, vmem],
        out_specs=(vmem, vmem),
    )(minus, change, plus_rows)
    return out_minus.reshape(2, FB, ML * PS), out_plus.reshape(2, FB, SL * PS)


def solution(mesh):
    return jax.shard_map(
        local,
        mesh=mesh,
        in_specs=(
            P(None, "freq", "rcv", None),
            P(None, "freq", "rcv"),
            P("rcv", None),
            P("rcv", None),
        ),
        out_specs=(P(None, "freq", "rcv"), P(None, "freq", "rcv")),
        check_vma=False,
    )
```

```python
import math

import jax
import jax.numpy as jnp
import numpy as np
from jax import lax
from jax.experimental import pallas as pl
from jax.experimental.pallas import tpu as pltpu
from jax.sharding import PartitionSpec as P

MESH = pl.DeviceIdType.MESH
PS = 12
ITERS = 2
FB = 32
NB = 32
NR = 8
NX = 4
GF = 8
NG = FB // GF
ROWS = 2 * 4 * GF
HALF = NG * ROWS // 2
ML = 32
SL = 128
NK = FB * NB
TW = 768
NQ = 3
WM = 2 * NQ
WP = 2 * PS
F32 = jnp.float32
BF16 = jnp.bfloat16


def tables():
    index = np.arange(NK)
    phases = (index[:, None] * index[None, :]) % (2 * NK)
    angles = phases * (2.0 * math.pi / (2 * NK))
    return np.stack([np.cos(angles), np.sin(angles)]).astype(np.float32)


def reorder_rows(start, rows, count):
    index = start + lax.broadcasted_iota(jnp.int32, (rows, 1), 0)
    item = (index * 43691) >> 19
    target = (index - PS * item) * count + item
    lane = lax.broadcasted_iota(jnp.int32, (rows, PS * count), 1)
    return jnp.where(lane == target, 1.0, 0.0).astype(BF16)


def reorder_back_rows(start, rows, count):
    index = start + lax.broadcasted_iota(jnp.int32, (rows, 1), 0)
    point = index // count
    target = (index - point * count) * PS + point
    lane = lax.broadcasted_iota(jnp.int32, (rows, PS * count), 1)
    return jnp.where(lane == target, 1.0, 0.0).astype(BF16)


def spreading():
    row = lax.broadcasted_iota(jnp.int32, (4 * ML, 4 * GF * ML), 0)
    lane = lax.broadcasted_iota(jnp.int32, (4 * ML, 4 * GF * ML), 1)
    hit = (lane // (GF * ML) == row // ML) & (lax.rem(lane, ML) == lax.rem(row, ML))
    return jnp.where(hit, 1.0, 0.0).astype(BF16)


MINUS_AT = (((3, 11), (5, 13), (2, 10)), ((19, 27), (21, 29), (18, 26)))
PLUS_AT = (
    (0, 4, 8, 12, 2, 6, 10, 14, 1, 7, 9, 15),
    (18, 22, 26, 30, 16, 20, 24, 28, 19, 21, 27, 29),
)


def kernel(
    refl_hbm, tab_hbm, plus_hbm, onm_ref, onp_ref,
    out_minus, out_plus,
    plus_ref, refl, refl_t, tab_full, tab, perm, perm_back, perm_m, spread, pinit, psnd, gath, msnd, xm, ymsnd, ym, wide,
    partial, from_far, from_x, from_y, sums, rests, xsnd, xp, ypsnd, wp, eo,
    load_sem, gath_send, gath_recv, xm_send, xm_recv, ym_send, ym_recv, rs_send, rs_recv, xp_send, xp_recv,
    wp_send, wp_recv,
):
    me_f = lax.axis_index("freq")
    me_r = lax.axis_index("rcv")
    part = me_f // (NB // 2)
    z_half = lax.rem(me_f, NB // 2) // 8
    far_first = [2 * y + z for z in (1 - z_half, z_half) for y in (1 - part, part)]
    me_x, me_y = me_r // 2, lax.rem(me_r, 2)
    beside = me_x * 2 + (1 - me_y)

    def along_x(i):
        return lax.rem(me_x + i, NX)


    load_refl = pltpu.make_async_copy(refl_hbm, refl, load_sem.at[0])
    load_tab = pltpu.make_async_copy(tab_hbm.at[part], tab_full, load_sem.at[1])
    load_plus = pltpu.make_async_copy(plus_hbm, plus_ref, load_sem.at[2])
    load_plus.start()
    load_refl.start()
    load_tab.start()

    barrier = pltpu.get_barrier_semaphore()

    def greet_f(i, _):
        pl.semaphore_signal(
            barrier, inc=1, device_id={"freq": lax.rem(me_f + i, NB), "rcv": me_r}, device_id_type=MESH
        )
        return 0

    def greet_r(i, _):
        pl.semaphore_signal(
            barrier, inc=1, device_id={"freq": me_f, "rcv": lax.rem(me_r + i, NR)}, device_id_type=MESH
        )
        return 0

    lax.fori_loop(1, NR, greet_r, 0)
    lax.fori_loop(NB // 2 + 1, NB, greet_f, 0)
    lax.fori_loop(1, NB // 2 + 1, greet_f, 0)

    row32 = lax.broadcasted_iota(jnp.int32, (FB, 128), 0)
    k_scale = jnp.where((row32 == 0) & (me_f == 0), 0.5, 1.0).astype(F32)
    my_rows = pl.ds(pl.multiple_of(me_f * FB, FB), FB)

    def remote_f(src, dst, send, recv, to):
        return pltpu.make_async_remote_copy(
            src_ref=src, dst_ref=dst, send_sem=send, recv_sem=recv,
            device_id={"freq": to, "rcv": me_r}, device_id_type=MESH,
        )

    def remote_r(src, dst, send, recv, to):
        return pltpu.make_async_remote_copy(
            src_ref=src, dst_ref=dst, send_sem=send, recv_sem=recv,
            device_id={"freq": me_f, "rcv": to}, device_id_type=MESH,
        )

    def await_bytes(ref, sem):
        pltpu.make_async_copy(ref, ref, sem).wait()

    def any_of(places):
        found = me_f == places[0]
        for place in places[1:]:
            found = found | (me_f == place)
        return found

    def minus_places(q):
        return [place for c in range(2) for place in MINUS_AT[c][q]]

    def plus_places(q):
        return [PLUS_AT[c][4 * q + i] for c in range(2) for i in range(4)]

    def row_x(i):
        return along_x(i) * 2 + me_y

    def send_plus(it, q):
        gath[it, q, me_r] = psnd[it, q]
        dst = gath.at[it, q, me_r]
        for i in (1, 3):
            remote_r(psnd.at[it, q], dst, gath_send.at[it], gath_recv.at[it, q, 0], row_x(i)).start()
        remote_r(psnd.at[it, q], dst, gath_send.at[it], gath_recv.at[it, q, 1], beside).start()

    def pass_plus(it, q):
        def pass_on(r, start, rows, sem, to):
            block = gath.at[it, q, r, pl.ds(start, rows)]
            remote_r(block, block, gath_send.at[it], gath_recv.at[it, q, sem], to).start()

        await_bytes(gath.at[it, q, pl.ds(0, 2)], gath_recv.at[it, q, 0])
        pass_on(row_x(1), ROWS, 3 * ROWS, 5, beside)
        pass_on(row_x(3), ROWS, 3 * ROWS, 5, beside)
        pass_on(row_x(3), 0, HALF, 4, row_x(1))
        pass_on(row_x(1), HALF, HALF, 3, row_x(3))
        await_bytes(gath.at[it, q, 0], gath_recv.at[it, q, 1])
        pass_on(beside, 0, 4 * ROWS, 2, row_x(2))
        pass_on(beside, 0, ROWS, 4, row_x(1))
        pass_on(beside, 0, ROWS, 3, row_x(3))

    def fill_perm(i, _):
        perm[pl.ds(pl.multiple_of(i * 128, 128), 128), :] = reorder_rows(i * 128, 128, SL)
        return 0

    lax.fori_loop(0, PS, fill_perm, 0)
    load_plus.wait()
    high = plus_ref[...].astype(BF16)
    left = plus_ref[...] - high.astype(F32)
    middle = left.astype(BF16)
    small = (left - middle.astype(F32)).astype(BF16)
    split = jnp.dot(jnp.concatenate([high, middle, small], axis=0), perm[...], preferred_element_type=F32)
    first = split[: 2 * FB]
    for q in range(NQ):
        for g in range(NG):
            parts = [
                first[c * FB + g * GF : c * FB + (g + 1) * GF, p * SL : (p + 1) * SL]
                for c in range(2)
                for p in range(4 * q, 4 * q + 4)
            ]
            psnd[0, q, g * ROWS : (g + 1) * ROWS, :] = jnp.concatenate(parts, axis=0).astype(BF16)
    pl.semaphore_wait(barrier, NB - 1 + NR - 1)
    for q in range(NQ):
        send_plus(0, q)

    exact = first + (split[2 * FB : 4 * FB] + split[4 * FB :])
    for c in range(2):
        for p in range(PS):
            pinit[p // 4, c * 4 + p % 4] = exact[c * FB : (c + 1) * FB, p * SL : (p + 1) * SL]

    spread[...] = spreading()
    perm_m[...] = reorder_back_rows(0, ML * PS, ML)

    def fill_back(i, _):
        perm_back[pl.ds(pl.multiple_of(i * 128, 128), 128), :] = reorder_back_rows(i * 128, 128, SL)
        return 0

    lax.fori_loop(0, PS, fill_back, 0)
    load_tab.wait()

    def round_tab(i, _):
        rows = pl.ds(pl.multiple_of(i * 128, 128), 128)
        tab[rows, :] = tab_full[rows, :].astype(BF16)
        return 0

    lax.fori_loop(0, NK // 128, round_tab, 0)
    load_refl.wait()
    for g in range(NG):
        for c in range(2):
            block = refl[c * FB * ML + g * GF * ML : c * FB * ML + (g + 1) * GF * ML, :]
            refl_t[g, :, c * GF * ML : (c + 1) * GF * ML] = jnp.transpose(block)

    def window(x, onsets, y, send_chunk, chunks, arrival):
        until = jnp.transpose(jnp.broadcast_to(onsets, (128, 128)))
        until = jnp.concatenate([until, until], axis=1)
        await_bytes(x.at[pl.ds(0, NK - FB)], arrival)
        traces = jnp.transpose(x[...])
        for n in range(TW // 256):
            cols = slice(n * 256, (n + 1) * 256)
            in_time = jnp.dot(traces, tab[:, cols], preferred_element_type=F32)
            time = n * 256 + lax.broadcasted_iota(jnp.int32, (128, 256), 1)
            factor = jnp.where(time == 0, 1.0 / NK, 2.0 / NK).astype(F32)
            in_time = jnp.where(time < until, in_time * factor, 0.0)
            top = in_time.astype(BF16)
            eo[:128, cols] = top
            eo[128:, cols] = (in_time - top.astype(F32)).astype(BF16)
        for n in chunks:
            cols = pl.ds(pl.multiple_of(n * 256, 256), 256)
            both = jnp.dot(eo[...], tab[:TW, cols], preferred_element_type=F32)
            y[cols, :] = jnp.transpose(both[:128] + both[128:]).astype(BF16)
            send_chunk(n * (256 // FB), 256 // FB)

    half = ROWS // 2
    lane = lax.broadcasted_iota(jnp.int32, (half, GF * ML), 1)
    row = lax.broadcasted_iota(jnp.int32, (half, GF * ML), 0)
    same = lax.rem(row, GF) == lane // ML
    quad_lane = lax.broadcasted_iota(jnp.int32, (GF, 128), 1) // ML

    def refl_rows(c, g):
        return slice(c * FB * ML + g * GF * ML, c * FB * ML + (g + 1) * GF * ML)

    def forward(it, q):
        blocks = ([], [])
        for g in range(NG):
            if g == 0:
                await_bytes(gath.at[it, q, 0, pl.ds(0, 3 * ROWS)], gath_recv.at[it, q, 3])
                await_bytes(gath.at[it, q, 0, pl.ds(0, 3 * ROWS)], gath_recv.at[it, q, 4])
                await_bytes(gath.at[it, q, 0], gath_recv.at[it, q, 2])
            if g == 1:
                await_bytes(gath.at[it, q, pl.ds(0, 2), pl.ds(0, 3 * ROWS)], gath_recv.at[it, q, 5])
            rows = slice(g * ROWS, (g + 1) * ROWS)
            values = jnp.concatenate([gath[it, q, r, rows, :] for r in range(NR)], axis=1)
            both = jnp.dot(values, refl_t[g], preferred_element_type=F32)
            a, b = both[:, : GF * ML], both[:, GF * ML :]
            parts = (a[:half] - b[half:], b[:half] + a[half:])
            for c in range(2):
                own = jnp.where(same, parts[c], 0.0)
                own = own[:, :128] + own[:, 128:]
                own = own + pltpu.roll(own, 64, 1)
                own = own + pltpu.roll(own, 32, 1)
                block = jnp.zeros((GF, 128), F32)
                for i in range(4):
                    block = jnp.where(quad_lane == i, own[i * GF : (i + 1) * GF], block)
                blocks[c].append(block)
        for c in range(2):
            msnd[it, q, c] = (jnp.concatenate(blocks[c], axis=0) * k_scale).astype(BF16)
            for to in MINUS_AT[c][q]:

                @pl.when(me_f == to)
                def _():
                    xm[it, my_rows, :] = msnd[it, q, c]

                @pl.when(me_f != to)
                def _():
                    remote_f(msnd.at[it, q, c], xm.at[it, my_rows], xm_send.at[it], xm_recv.at[it], to).start()

    def scatter(it, buffer, dst, send, recv):
        def send_chunk(begin, count):
            def one(i, _):
                to = begin + i
                rows = pl.ds(pl.multiple_of(to * FB, FB), FB)

                @pl.when(to == me_f)
                def _():
                    dst[...] = buffer[it, rows, :]

                @pl.when(to != me_f)
                def _():
                    remote_f(buffer.at[it, rows], dst, send, recv, to).start()

                return 0

            lax.fori_loop(0, count, one, 0)

        return send_chunk

    def window_minus(it, q):
        @pl.when(any_of(minus_places(q)))
        def _():
            onsets = jnp.concatenate([onm_ref[4 * q + i : 4 * q + i + 1, :] for i in range(4)], axis=1)
            send_chunk = scatter(it, ymsnd, ym.at[it, q, part], ym_send.at[it], ym_recv.at[it, q])
            window(xm.at[it], onsets, ymsnd.at[it], send_chunk, far_first[2:], xm_recv.at[it])

    def adjoint(it, q):
        here = any_of(minus_places(q))

        @pl.when(here)
        def _():
            await_bytes(ym.at[it, q, pl.ds(0, 1)], ym_recv.at[it, q])

        @pl.when(jnp.logical_not(here))
        def _():
            await_bytes(ym.at[it, q], ym_recv.at[it, q])

        spread_rows = jnp.dot(ym[it, q].reshape(2 * FB, 128), spread[...], preferred_element_type=F32)
        row_s = lax.broadcasted_iota(jnp.int32, (2 * FB, 1024), 0)
        lane_s = lax.broadcasted_iota(jnp.int32, (2 * FB, 1024), 1)
        wide[...] = jnp.where(lax.rem(row_s, GF) == lax.rem(lane_s // ML, GF), spread_rows, 0.0)
        for g in range(NG):
            blocks = [wide[c * FB + g * GF : c * FB + (g + 1) * GF, :] for c in range(2)]
            re, im = [
                jnp.concatenate([block[:, i * 256 : (i + 1) * 256] for i in range(4)], axis=0) for block in blocks
            ]
            left = jnp.concatenate([re, im], axis=0).astype(BF16)
            right = jnp.concatenate([im, -re], axis=0).astype(BF16)
            for n in range(4):
                cols = slice(n * 256, (n + 1) * 256)
                out = jnp.dot(left, refl[refl_rows(0, g), cols], preferred_element_type=F32)
                out += jnp.dot(right, refl[refl_rows(1, g), cols], preferred_element_type=F32)
                out = out.astype(BF16)
                for y in range(2):
                    partial[it, q, n, y, g * ROWS : (g + 1) * ROWS, :] = out[:, y * SL : (y + 1) * SL]

        def send(x, y, start, rows, dst, sem, to):
            src = partial.at[it, q, x, y, pl.ds(start, rows)]
            remote_r(src, dst, rs_send.at[it], rs_recv.at[it, q, sem], to).start()

        for k, i in enumerate((1, 3)):
            send(along_x(i), 1 - me_y, ROWS, 3 * ROWS, from_y.at[it, q, k], 3, beside)
        send(along_x(2), 1 - me_y, 0, 4 * ROWS, from_far.at[it, q], 0, row_x(2))
        for k, i in enumerate((1, 3)):
            there = from_x.at[it, q, 1 - k]
            send(along_x(2), me_y, k * HALF, HALF, there.at[pl.ds(0, HALF)], 2 - k, row_x(i))
            send(along_x(i), 1 - me_y, 0, ROWS, there.at[pl.ds(HALF, ROWS)], 2 - k, row_x(i))

    def pass_sums(it, q):
        def pass_on(total, slot, sem, to):
            sums[it, q, slot] = total.astype(BF16)
            remote_r(
                sums.at[it, q, slot], rests.at[it, q, sem - 4], rs_send.at[it], rs_recv.at[it, q, sem], to
            ).start()

        await_bytes(from_x.at[it, q, 0], rs_recv.at[it, q, 1])
        await_bytes(from_x.at[it, q, 1], rs_recv.at[it, q, 2])
        await_bytes(from_far.at[it, q], rs_recv.at[it, q, 0])
        total = partial[it, q, me_x, 1 - me_y].astype(F32) + from_far[it, q].astype(F32)
        quarter = from_x[it, q, 0, HALF:, :].astype(F32) + from_x[it, q, 1, HALF:, :].astype(F32)
        pass_on(jnp.concatenate([total[:ROWS] + quarter, total[ROWS:]], axis=0), 2, 6, beside)
        await_bytes(from_y.at[it, q], rs_recv.at[it, q, 3])
        for k, i in enumerate((1, 3)):
            total = partial[it, q, along_x(i), me_y].astype(F32)
            more = from_y[it, q, k].astype(F32)
            half = from_x[it, q, 1 - k, :HALF, :].astype(F32)
            if k == 0:
                pieces = [total[:ROWS] + half[:ROWS], total[ROWS:HALF] + half[ROWS:] + more[:ROWS]]
                pieces.append(total[HALF:] + more[ROWS:])
            else:
                pieces = [total[:ROWS], total[ROWS:HALF] + more[:ROWS], total[HALF:] + half + more[ROWS:]]
            pass_on(jnp.concatenate(pieces, axis=0), k, 5 - k, row_x(i))

    def add_up(it, q):
        total = partial[it, q, me_x, me_y].astype(F32)
        for k in range(3):
            await_bytes(rests.at[it, q, k], rs_recv.at[it, q, 4 + k])
            total += rests[it, q, k].astype(F32)
        for c in range(2):
            for i in range(4):
                to = PLUS_AT[c][4 * q + i]
                at = c * 4 + i
                block = jnp.concatenate(
                    [total[g * ROWS + at * GF : g * ROWS + (at + 1) * GF] for g in range(NG)], axis=0
                )
                xsnd[it, q, at] = (block * k_scale).astype(BF16)

                @pl.when(me_f == to)
                def _():
                    xp[it, my_rows, :] = xsnd[it, q, at]

                @pl.when(me_f != to)
                def _():
                    remote_f(xsnd.at[it, q, at], xp.at[it, my_rows], xp_send.at[it], xp_recv.at[it], to).start()

    def window_plus(it, q):
        @pl.when(any_of(plus_places(q)))
        def _():
            point = jnp.int32(0)
            for i in range(1, 4):
                point = jnp.where(any_of([PLUS_AT[c][4 * q + i] for c in range(2)]), i, point)
            onsets = onp_ref[pl.ds(4 * q + point, 1), :]
            send_chunk = scatter(it, ypsnd, wp.at[it, q, part * 4 + point], wp_send.at[it], wp_recv.at[it, q])
            window(xp.at[it], onsets, ypsnd.at[it], send_chunk, far_first, xp_recv.at[it])

    def update(it, q):
        here = any_of(plus_places(q))

        @pl.when(here)
        def _():
            await_bytes(wp.at[it, q, pl.ds(0, 7)], wp_recv.at[it, q])

        @pl.when(jnp.logical_not(here))
        def _():
            await_bytes(wp.at[it, q], wp_recv.at[it, q])

        @pl.when(it < ITERS - 1)
        def _():
            new = pinit[q] + wp[it, q].astype(F32)
            for g in range(NG):
                rows = new[:, g * GF : (g + 1) * GF, :].reshape(ROWS, SL)
                psnd[it + 1, q, g * ROWS : (g + 1) * ROWS, :] = rows.astype(BF16)
            send_plus(it + 1, q)

        @pl.when(it == ITERS - 1)
        def _():
            change = jnp.concatenate(
                [jnp.concatenate([wp[it, q, c * 4 + i] for i in range(4)], axis=1) for c in range(2)], axis=0
            )
            change = jnp.dot(
                change, perm_back[q * 4 * SL : (q + 1) * 4 * SL, :], preferred_element_type=F32
            )
            if q < NQ - 1:
                plus_ref[...] = change if q == 0 else plus_ref[...] + change
            else:
                out_plus[...] = (plus_ref[...] + change).astype(BF16)

    def finish_minus(it):
        @pl.when(it == ITERS - 1)
        def _():
            minus = jnp.concatenate(
                [jnp.concatenate([ym[it, q, c] for q in range(NQ)], axis=1) for c in range(2)], axis=0
            )
            minus = jnp.dot(minus, perm_m[...], preferred_element_type=F32)
            out_minus[...] = minus.astype(BF16)

    def iteration(it, _):
        pass_plus(it, 0)
        pass_plus(it, 1)
        pass_plus(it, 2)
        forward(it, 0)
        forward(it, 1)
        forward(it, 2)
        window_minus(it, 0)
        window_minus(it, 1)
        window_minus(it, 2)
        adjoint(it, 0)
        adjoint(it, 1)
        adjoint(it, 2)
        pass_sums(it, 0)
        pass_sums(it, 1)
        pass_sums(it, 2)
        add_up(it, 0)
        add_up(it, 1)
        add_up(it, 2)
        window_plus(it, 0)
        window_plus(it, 1)
        window_plus(it, 2)
        finish_minus(it)
        update(it, 0)
        update(it, 1)
        update(it, 2)
        return 0

    lax.fori_loop(0, ITERS, iteration, 0)

    is_minus = any_of([place for q in range(NQ) for place in minus_places(q)])
    is_plus = any_of([place for q in range(NQ) for place in plus_places(q)])

    def drain(it, _):
        await_bytes(gath.at[it, :, pl.ds(0, NR - 1)], gath_send.at[it])
        await_bytes(gath.at[it, :, pl.ds(0, NR - 1)], rs_send.at[it])

        @pl.when(is_minus)
        def _():
            await_bytes(xm.at[it, pl.ds(0, (2 * WM - 1) * FB)], xm_send.at[it])
            await_bytes(ymsnd.at[it, pl.ds(0, NK // 2 - FB)], ym_send.at[it])

        @pl.when(jnp.logical_not(is_minus))
        def _():
            await_bytes(xm.at[it, pl.ds(0, 2 * WM * FB)], xm_send.at[it])

        @pl.when(is_plus)
        def _():
            await_bytes(xp.at[it, pl.ds(0, (WP - 1) * FB)], xp_send.at[it])
            await_bytes(ypsnd.at[it, pl.ds(0, NK - FB)], wp_send.at[it])

        @pl.when(jnp.logical_not(is_plus))
        def _():
            await_bytes(xsnd.at[it], xp_send.at[it])

        return 0

    lax.fori_loop(0, ITERS, drain, 0)


def widen(minus_ref, change_ref, plus_ref, out_minus, out_plus):
    out_minus[...] = minus_ref[...].astype(F32)
    out_plus[...] = plus_ref[...] + change_ref[...].astype(F32)


def local(reflection, plus_init, onset_receiver, onset_source):
    onm = jnp.transpose(onset_receiver)
    onp = jnp.transpose(onset_source)
    vmem = pl.BlockSpec(memory_space=pltpu.VMEM)
    hbm = pl.BlockSpec(memory_space=pl.ANY)
    dma = pltpu.SemaphoreType.DMA
    plus_rows = plus_init.reshape(2 * FB, SL * PS)
    minus, change = pl.pallas_call(
        kernel,
        out_shape=(
            jax.ShapeDtypeStruct((2 * FB, ML * PS), BF16),
            jax.ShapeDtypeStruct((2 * FB, SL * PS), BF16),
        ),
        in_specs=[hbm, hbm, hbm, vmem, vmem],
        out_specs=(vmem, vmem),
        scratch_shapes=[
            pltpu.VMEM((2 * FB, SL * PS), F32),
            pltpu.VMEM((2 * FB * ML, 1024), BF16),
            pltpu.VMEM((NG, 1024, 2 * GF * ML), BF16),
            pltpu.VMEM((NK, NK), F32),
            pltpu.VMEM((NK, NK), BF16),
            pltpu.VMEM((SL * PS, SL * PS), BF16),
            pltpu.VMEM((SL * PS, SL * PS), BF16),
            pltpu.VMEM((ML * PS, ML * PS), BF16),
            pltpu.VMEM((4 * ML, 4 * GF * ML), BF16),
            pltpu.VMEM((NQ, 8, FB, SL), F32),
            pltpu.VMEM((ITERS, NQ, NG * ROWS, SL), BF16),
            pltpu.VMEM((ITERS, NQ, NR, NG * ROWS, SL), BF16),
            pltpu.VMEM((ITERS, NQ, 2, FB, 128), BF16),
            pltpu.VMEM((ITERS, NK, 128), BF16),
            pltpu.VMEM((ITERS, NK, 128), BF16),
            pltpu.VMEM((ITERS, NQ, 2, FB, 128), BF16),
            pltpu.VMEM((2 * FB, 1024), F32),
            pltpu.VMEM((ITERS, NQ, NX, 2, 4 * ROWS, SL), BF16),
            pltpu.VMEM((ITERS, NQ, 4 * ROWS, SL), BF16),
            pltpu.VMEM((ITERS, NQ, 2, 3 * ROWS, SL), BF16),
            pltpu.VMEM((ITERS, NQ, 2, 3 * ROWS, SL), BF16),
            pltpu.VMEM((ITERS, NQ, 3, 4 * ROWS, SL), BF16),
            pltpu.VMEM((ITERS, NQ, 3, 4 * ROWS, SL), BF16),
            pltpu.VMEM((ITERS, NQ, 8, FB, SL), BF16),
            pltpu.VMEM((ITERS, NK, SL), BF16),
            pltpu.VMEM((ITERS, NK, SL), BF16),
            pltpu.VMEM((ITERS, NQ, 8, FB, SL), BF16),
            pltpu.VMEM((256, TW), BF16),
            dma((3,)),
            dma((ITERS,)), dma((ITERS, NQ, 6)),
            dma((ITERS,)), dma((ITERS,)),
            dma((ITERS,)), dma((ITERS, NQ)),
            dma((ITERS,)), dma((ITERS, NQ, 7)),
            dma((ITERS,)), dma((ITERS,)),
            dma((ITERS,)), dma((ITERS, NQ)),
        ],
        compiler_params=pltpu.CompilerParams(
            collective_id=0, has_side_effects=True, vmem_limit_bytes=56 * 1024 * 1024
        ),
    )(
        reflection.reshape(2 * FB * ML, 1024),
        jnp.asarray(tables()),
        plus_rows,
        onm,
        onp,
    )
    out_minus, out_plus = pl.pallas_call(
        widen,
        out_shape=(
            jax.ShapeDtypeStruct((2 * FB, ML * PS), F32),
            jax.ShapeDtypeStruct((2 * FB, SL * PS), F32),
        ),
        in_specs=[vmem, vmem, vmem],
        out_specs=(vmem, vmem),
    )(minus, change, plus_rows)
    return out_minus.reshape(2, FB, ML * PS), out_plus.reshape(2, FB, SL * PS)


def solution(mesh):
    return jax.shard_map(
        local,
        mesh=mesh,
        in_specs=(
            P(None, "freq", "rcv", None),
            P(None, "freq", "rcv"),
            P("rcv", None),
            P("rcv", None),
        ),
        out_specs=(P(None, "freq", "rcv"), P(None, "freq", "rcv")),
        check_vma=False,
    )
```

```python
import math

import jax
import jax.numpy as jnp
import numpy as np
from jax import lax
from jax.experimental import pallas as pl
from jax.experimental.pallas import tpu as pltpu
from jax.sharding import PartitionSpec as P

MESH = pl.DeviceIdType.MESH
PS = 12
ITERS = 2
FB = 32
NB = 32
NR = 8
NX = 4
GF = 8
NG = FB // GF
ROWS = 2 * 4 * GF
HALF = NG * ROWS // 2
ML = 32
SL = 128
NK = FB * NB
TW = 768
NQ = 3
WM = 2 * NQ
WP = 2 * PS
F32 = jnp.float32
BF16 = jnp.bfloat16


def tables():
    index = np.arange(NK)
    phases = (index[:, None] * index[None, :]) % (2 * NK)
    angles = phases * (2.0 * math.pi / (2 * NK))
    return np.stack([np.cos(angles), np.sin(angles)]).astype(np.float32)


def reorder_rows(start, rows, count):
    index = start + lax.broadcasted_iota(jnp.int32, (rows, 1), 0)
    item = (index * 43691) >> 19
    target = (index - PS * item) * count + item
    lane = lax.broadcasted_iota(jnp.int32, (rows, PS * count), 1)
    return jnp.where(lane == target, 1.0, 0.0).astype(BF16)


def reorder_back_rows(start, rows, count):
    index = start + lax.broadcasted_iota(jnp.int32, (rows, 1), 0)
    point = index // count
    target = (index - point * count) * PS + point
    lane = lax.broadcasted_iota(jnp.int32, (rows, PS * count), 1)
    return jnp.where(lane == target, 1.0, 0.0).astype(BF16)


def spreading():
    row = lax.broadcasted_iota(jnp.int32, (4 * ML, 4 * GF * ML), 0)
    lane = lax.broadcasted_iota(jnp.int32, (4 * ML, 4 * GF * ML), 1)
    hit = (lane // (GF * ML) == row // ML) & (lax.rem(lane, ML) == lax.rem(row, ML))
    return jnp.where(hit, 1.0, 0.0).astype(BF16)


MINUS_AT = (((3, 11), (5, 13), (2, 10)), ((19, 27), (21, 29), (18, 26)))
PLUS_AT = (
    (0, 4, 8, 12, 2, 6, 10, 14, 1, 7, 9, 15),
    (18, 22, 26, 30, 16, 20, 24, 28, 19, 21, 27, 29),
)


def kernel(
    refl_hbm, tab_hbm, plus_hbm, onm_ref, onp_ref,
    out_minus, out_plus,
    plus_ref, refl, refl_t, tab_full, tab, perm, perm_back, perm_m, spread, pinit, psnd, gath, msnd, xm, ymsnd, ym, wide,
    partial, from_far, from_x, from_y, sums, rests, xsnd, xp, ypsnd, wp, eo,
    load_sem, gath_send, gath_recv, xm_send, xm_recv, ym_send, ym_recv, rs_send, rs_recv, xp_send, xp_recv,
    wp_send, wp_recv,
):
    me_f = lax.axis_index("freq")
    me_r = lax.axis_index("rcv")
    part = me_f // (NB // 2)
    z_half = lax.rem(me_f, NB // 2) // 8
    far_first = [2 * y + z for z in (1 - z_half, z_half) for y in (1 - part, part)]
    me_x, me_y = me_r // 2, lax.rem(me_r, 2)
    beside = me_x * 2 + (1 - me_y)

    def along_x(i):
        return lax.rem(me_x + i, NX)


    load_refl = pltpu.make_async_copy(refl_hbm, refl, load_sem.at[0])
    load_tab = pltpu.make_async_copy(tab_hbm.at[part], tab_full, load_sem.at[1])
    load_plus = pltpu.make_async_copy(plus_hbm, plus_ref, load_sem.at[2])
    load_plus.start()
    load_refl.start()
    load_tab.start()

    barrier = pltpu.get_barrier_semaphore()

    def greet_f(i, _):
        pl.semaphore_signal(
            barrier, inc=1, device_id={"freq": lax.rem(me_f + i, NB), "rcv": me_r}, device_id_type=MESH
        )
        return 0

    def greet_r(i, _):
        pl.semaphore_signal(
            barrier, inc=1, device_id={"freq": me_f, "rcv": lax.rem(me_r + i, NR)}, device_id_type=MESH
        )
        return 0

    lax.fori_loop(1, NR, greet_r, 0)
    lax.fori_loop(NB // 2 + 1, NB, greet_f, 0)
    lax.fori_loop(1, NB // 2 + 1, greet_f, 0)

    row32 = lax.broadcasted_iota(jnp.int32, (FB, 128), 0)
    k_scale = jnp.where((row32 == 0) & (me_f == 0), 0.5, 1.0).astype(F32)
    my_rows = pl.ds(pl.multiple_of(me_f * FB, FB), FB)

    def remote_f(src, dst, send, recv, to):
        return pltpu.make_async_remote_copy(
            src_ref=src, dst_ref=dst, send_sem=send, recv_sem=recv,
            device_id={"freq": to, "rcv": me_r}, device_id_type=MESH,
        )

    def remote_r(src, dst, send, recv, to):
        return pltpu.make_async_remote_copy(
            src_ref=src, dst_ref=dst, send_sem=send, recv_sem=recv,
            device_id={"freq": me_f, "rcv": to}, device_id_type=MESH,
        )

    def await_bytes(ref, sem):
        pltpu.make_async_copy(ref, ref, sem).wait()

    def any_of(places):
        found = me_f == places[0]
        for place in places[1:]:
            found = found | (me_f == place)
        return found

    def minus_places(q):
        return [place for c in range(2) for place in MINUS_AT[c][q]]

    def plus_places(q):
        return [PLUS_AT[c][4 * q + i] for c in range(2) for i in range(4)]

    def row_x(i):
        return along_x(i) * 2 + me_y

    def send_plus(it, q):
        gath[it, q, me_r] = psnd[it, q]
        dst = gath.at[it, q, me_r]
        for i in (1, 3):
            remote_r(psnd.at[it, q], dst, gath_send.at[it], gath_recv.at[it, q, 0], row_x(i)).start()
        remote_r(psnd.at[it, q], dst, gath_send.at[it], gath_recv.at[it, q, 1], beside).start()

    def pass_plus(it, q):
        def pass_on(r, start, rows, sem, to):
            block = gath.at[it, q, r, pl.ds(start, rows)]
            remote_r(block, block, gath_send.at[it], gath_recv.at[it, q, sem], to).start()

        await_bytes(gath.at[it, q, pl.ds(0, 2)], gath_recv.at[it, q, 0])
        pass_on(row_x(1), ROWS, 3 * ROWS, 5, beside)
        pass_on(row_x(3), ROWS, 3 * ROWS, 5, beside)
        pass_on(row_x(3), 0, HALF, 4, row_x(1))
        pass_on(row_x(1), HALF, HALF, 3, row_x(3))
        await_bytes(gath.at[it, q, 0], gath_recv.at[it, q, 1])
        pass_on(beside, 0, 4 * ROWS, 2, row_x(2))
        pass_on(beside, 0, ROWS, 4, row_x(1))
        pass_on(beside, 0, ROWS, 3, row_x(3))

    def fill_perm(i, _):
        perm[pl.ds(pl.multiple_of(i * 128, 128), 128), :] = reorder_rows(i * 128, 128, SL)
        return 0

    lax.fori_loop(0, PS, fill_perm, 0)
    load_plus.wait()
    high = plus_ref[...].astype(BF16)
    left = plus_ref[...] - high.astype(F32)
    middle = left.astype(BF16)
    small = (left - middle.astype(F32)).astype(BF16)
    split = jnp.dot(jnp.concatenate([high, middle, small], axis=0), perm[...], preferred_element_type=F32)
    first = split[: 2 * FB]
    for q in range(NQ):
        for g in range(NG):
            parts = [
                first[c * FB + g * GF : c * FB + (g + 1) * GF, p * SL : (p + 1) * SL]
                for c in range(2)
                for p in range(4 * q, 4 * q + 4)
            ]
            psnd[0, q, g * ROWS : (g + 1) * ROWS, :] = jnp.concatenate(parts, axis=0).astype(BF16)
    pl.semaphore_wait(barrier, NB - 1 + NR - 1)
    for q in range(NQ):
        send_plus(0, q)

    exact = first + (split[2 * FB : 4 * FB] + split[4 * FB :])
    for c in range(2):
        for p in range(PS):
            pinit[p // 4, c * 4 + p % 4] = exact[c * FB : (c + 1) * FB, p * SL : (p + 1) * SL]

    spread[...] = spreading()
    perm_m[...] = reorder_back_rows(0, ML * PS, ML)

    def fill_back(i, _):
        perm_back[pl.ds(pl.multiple_of(i * 128, 128), 128), :] = reorder_back_rows(i * 128, 128, SL)
        return 0

    lax.fori_loop(0, PS, fill_back, 0)
    load_tab.wait()

    def round_tab(i, _):
        rows = pl.ds(pl.multiple_of(i * 128, 128), 128)
        tab[rows, :] = tab_full[rows, :].astype(BF16)
        return 0

    lax.fori_loop(0, NK // 128, round_tab, 0)
    load_refl.wait()
    for g in range(NG):
        for c in range(2):
            block = refl[c * FB * ML + g * GF * ML : c * FB * ML + (g + 1) * GF * ML, :]
            refl_t[g, :, c * GF * ML : (c + 1) * GF * ML] = jnp.transpose(block)

    def window(x, onsets, y, send_chunk, chunks, arrival):
        until = jnp.transpose(jnp.broadcast_to(onsets, (128, 128)))
        until = jnp.concatenate([until, until], axis=1)
        await_bytes(x.at[pl.ds(0, NK - FB)], arrival)
        traces = jnp.transpose(x[...])
        for n in range(TW // 256):
            cols = slice(n * 256, (n + 1) * 256)
            in_time = jnp.dot(traces, tab[:, cols], preferred_element_type=F32)
            time = n * 256 + lax.broadcasted_iota(jnp.int32, (128, 256), 1)
            factor = jnp.where(time == 0, 1.0 / NK, 2.0 / NK).astype(F32)
            in_time = jnp.where(time < until, in_time * factor, 0.0)
            top = in_time.astype(BF16)
            eo[:128, cols] = top
            eo[128:, cols] = (in_time - top.astype(F32)).astype(BF16)
        for n in chunks:
            cols = pl.ds(pl.multiple_of(n * 256, 256), 256)
            both = jnp.dot(eo[...], tab[:TW, cols], preferred_element_type=F32)
            y[cols, :] = jnp.transpose(both[:128] + both[128:]).astype(BF16)
            send_chunk(n * (256 // FB), 256 // FB)

    half = ROWS // 2
    lane = lax.broadcasted_iota(jnp.int32, (half, GF * ML), 1)
    row = lax.broadcasted_iota(jnp.int32, (half, GF * ML), 0)
    same = lax.rem(row, GF) == lane // ML
    quad_lane = lax.broadcasted_iota(jnp.int32, (GF, 128), 1) // ML

    def refl_rows(c, g):
        return slice(c * FB * ML + g * GF * ML, c * FB * ML + (g + 1) * GF * ML)

    def forward(it, q):
        blocks = ([], [])
        for g in range(NG):
            if g == 0:
                await_bytes(gath.at[it, q, 0, pl.ds(0, 3 * ROWS)], gath_recv.at[it, q, 3])
                await_bytes(gath.at[it, q, 0, pl.ds(0, 3 * ROWS)], gath_recv.at[it, q, 4])
                await_bytes(gath.at[it, q, 0], gath_recv.at[it, q, 2])
            if g == 1:
                await_bytes(gath.at[it, q, pl.ds(0, 2), pl.ds(0, 3 * ROWS)], gath_recv.at[it, q, 5])
            rows = slice(g * ROWS, (g + 1) * ROWS)
            values = jnp.concatenate([gath[it, q, r, rows, :] for r in range(NR)], axis=1)
            both = jnp.dot(values, refl_t[g], preferred_element_type=F32)
            a, b = both[:, : GF * ML], both[:, GF * ML :]
            parts = (a[:half] - b[half:], b[:half] + a[half:])
            for c in range(2):
                own = jnp.where(same, parts[c], 0.0)
                own = own[:, :128] + own[:, 128:]
                own = own + pltpu.roll(own, 64, 1)
                own = own + pltpu.roll(own, 32, 1)
                block = jnp.zeros((GF, 128), F32)
                for i in range(4):
                    block = jnp.where(quad_lane == i, own[i * GF : (i + 1) * GF], block)
                blocks[c].append(block)
        for c in range(2):
            msnd[it, q, c] = (jnp.concatenate(blocks[c], axis=0) * k_scale).astype(BF16)
            for to in MINUS_AT[c][q]:

                @pl.when(me_f == to)
                def _():
                    xm[it, my_rows, :] = msnd[it, q, c]

                @pl.when(me_f != to)
                def _():
                    remote_f(msnd.at[it, q, c], xm.at[it, my_rows], xm_send.at[it], xm_recv.at[it], to).start()

    def scatter(it, buffer, dst, send, recv):
        def send_chunk(begin, count):
            def one(i, _):
                to = begin + i
                rows = pl.ds(pl.multiple_of(to * FB, FB), FB)

                @pl.when(to == me_f)
                def _():
                    dst[...] = buffer[it, rows, :]

                @pl.when(to != me_f)
                def _():
                    remote_f(buffer.at[it, rows], dst, send, recv, to).start()

                return 0

            lax.fori_loop(0, count, one, 0)

        return send_chunk

    def window_minus(it, q):
        @pl.when(any_of(minus_places(q)))
        def _():
            onsets = jnp.concatenate([onm_ref[4 * q + i : 4 * q + i + 1, :] for i in range(4)], axis=1)
            send_chunk = scatter(it, ymsnd, ym.at[it, q, part], ym_send.at[it], ym_recv.at[it, q])
            window(xm.at[it], onsets, ymsnd.at[it], send_chunk, far_first[2:], xm_recv.at[it])

    def adjoint(it, q):
        here = any_of(minus_places(q))

        @pl.when(here)
        def _():
            await_bytes(ym.at[it, q, pl.ds(0, 1)], ym_recv.at[it, q])

        @pl.when(jnp.logical_not(here))
        def _():
            await_bytes(ym.at[it, q], ym_recv.at[it, q])

        spread_rows = jnp.dot(ym[it, q].reshape(2 * FB, 128), spread[...], preferred_element_type=F32)
        row_s = lax.broadcasted_iota(jnp.int32, (2 * FB, 1024), 0)
        lane_s = lax.broadcasted_iota(jnp.int32, (2 * FB, 1024), 1)
        wide[...] = jnp.where(lax.rem(row_s, GF) == lax.rem(lane_s // ML, GF), spread_rows, 0.0)
        def send(x, y, start, rows, dst, sem, to):
            src = partial.at[it, q, x, y, pl.ds(start, rows)]
            remote_r(src, dst, rs_send.at[it], rs_recv.at[it, q, sem], to).start()

        def send_half(k, i):
            there = from_x.at[it, q, 1 - k, pl.ds(0, HALF)]
            send(along_x(2), me_y, k * HALF, HALF, there, 2 - k, row_x(i))

        for g in range(NG):
            blocks = [wide[c * FB + g * GF : c * FB + (g + 1) * GF, :] for c in range(2)]
            re, im = [
                jnp.concatenate([block[:, i * 256 : (i + 1) * 256] for i in range(4)], axis=0) for block in blocks
            ]
            left = jnp.concatenate([re, im], axis=0).astype(BF16)
            right = jnp.concatenate([im, -re], axis=0).astype(BF16)
            for n in range(4):
                cols = slice(n * 256, (n + 1) * 256)
                out = jnp.dot(left, refl[refl_rows(0, g), cols], preferred_element_type=F32)
                out += jnp.dot(right, refl[refl_rows(1, g), cols], preferred_element_type=F32)
                out = out.astype(BF16)
                for y in range(2):
                    partial[it, q, n, y, g * ROWS : (g + 1) * ROWS, :] = out[:, y * SL : (y + 1) * SL]
            if g == 0:
                for k, i in enumerate((1, 3)):
                    there = from_x.at[it, q, 1 - k, pl.ds(HALF, ROWS)]
                    send(along_x(i), 1 - me_y, 0, ROWS, there, 2 - k, row_x(i))
            if g == 1:
                send_half(0, 1)

        for k, i in enumerate((1, 3)):
            send(along_x(i), 1 - me_y, ROWS, 3 * ROWS, from_y.at[it, q, k], 3, beside)
        send(along_x(2), 1 - me_y, 0, 4 * ROWS, from_far.at[it, q], 0, row_x(2))
        send_half(1, 3)

    def pass_sums(it, q):
        def pass_on(total, slot, sem, to):
            sums[it, q, slot] = total.astype(BF16)
            remote_r(
                sums.at[it, q, slot], rests.at[it, q, sem - 4], rs_send.at[it], rs_recv.at[it, q, sem], to
            ).start()

        await_bytes(from_x.at[it, q, 0], rs_recv.at[it, q, 1])
        await_bytes(from_x.at[it, q, 1], rs_recv.at[it, q, 2])
        await_bytes(from_far.at[it, q], rs_recv.at[it, q, 0])
        total = partial[it, q, me_x, 1 - me_y].astype(F32) + from_far[it, q].astype(F32)
        quarter = from_x[it, q, 0, HALF:, :].astype(F32) + from_x[it, q, 1, HALF:, :].astype(F32)
        pass_on(jnp.concatenate([total[:ROWS] + quarter, total[ROWS:]], axis=0), 2, 6, beside)
        await_bytes(from_y.at[it, q], rs_recv.at[it, q, 3])
        for k, i in enumerate((1, 3)):
            total = partial[it, q, along_x(i), me_y].astype(F32)
            more = from_y[it, q, k].astype(F32)
            half = from_x[it, q, 1 - k, :HALF, :].astype(F32)
            if k == 0:
                pieces = [total[:ROWS] + half[:ROWS], total[ROWS:HALF] + half[ROWS:] + more[:ROWS]]
                pieces.append(total[HALF:] + more[ROWS:])
            else:
                pieces = [total[:ROWS], total[ROWS:HALF] + more[:ROWS], total[HALF:] + half + more[ROWS:]]
            pass_on(jnp.concatenate(pieces, axis=0), k, 5 - k, row_x(i))

    def add_up(it, q):
        total = partial[it, q, me_x, me_y].astype(F32)
        for k in range(3):
            await_bytes(rests.at[it, q, k], rs_recv.at[it, q, 4 + k])
            total += rests[it, q, k].astype(F32)
        for c in range(2):
            for i in range(4):
                to = PLUS_AT[c][4 * q + i]
                at = c * 4 + i
                block = jnp.concatenate(
                    [total[g * ROWS + at * GF : g * ROWS + (at + 1) * GF] for g in range(NG)], axis=0
                )
                xsnd[it, q, at] = (block * k_scale).astype(BF16)

                @pl.when(me_f == to)
                def _():
                    xp[it, my_rows, :] = xsnd[it, q, at]

                @pl.when(me_f != to)
                def _():
                    remote_f(xsnd.at[it, q, at], xp.at[it, my_rows], xp_send.at[it], xp_recv.at[it], to).start()

    def window_plus(it, q):
        @pl.when(any_of(plus_places(q)))
        def _():
            point = jnp.int32(0)
            for i in range(1, 4):
                point = jnp.where(any_of([PLUS_AT[c][4 * q + i] for c in range(2)]), i, point)
            onsets = onp_ref[pl.ds(4 * q + point, 1), :]
            send_chunk = scatter(it, ypsnd, wp.at[it, q, part * 4 + point], wp_send.at[it], wp_recv.at[it, q])
            window(xp.at[it], onsets, ypsnd.at[it], send_chunk, far_first, xp_recv.at[it])

    def update(it, q):
        here = any_of(plus_places(q))

        @pl.when(here)
        def _():
            await_bytes(wp.at[it, q, pl.ds(0, 7)], wp_recv.at[it, q])

        @pl.when(jnp.logical_not(here))
        def _():
            await_bytes(wp.at[it, q], wp_recv.at[it, q])

        @pl.when(it < ITERS - 1)
        def _():
            new = pinit[q] + wp[it, q].astype(F32)
            for g in range(NG):
                rows = new[:, g * GF : (g + 1) * GF, :].reshape(ROWS, SL)
                psnd[it + 1, q, g * ROWS : (g + 1) * ROWS, :] = rows.astype(BF16)
            send_plus(it + 1, q)

        @pl.when(it == ITERS - 1)
        def _():
            change = jnp.concatenate(
                [jnp.concatenate([wp[it, q, c * 4 + i] for i in range(4)], axis=1) for c in range(2)], axis=0
            )
            change = jnp.dot(
                change, perm_back[q * 4 * SL : (q + 1) * 4 * SL, :], preferred_element_type=F32
            )
            if q < NQ - 1:
                plus_ref[...] = change if q == 0 else plus_ref[...] + change
            else:
                out_plus[...] = (plus_ref[...] + change).astype(BF16)

    def finish_minus(it):
        @pl.when(it == ITERS - 1)
        def _():
            minus = jnp.concatenate(
                [jnp.concatenate([ym[it, q, c] for q in range(NQ)], axis=1) for c in range(2)], axis=0
            )
            minus = jnp.dot(minus, perm_m[...], preferred_element_type=F32)
            out_minus[...] = minus.astype(BF16)

    def iteration(it, _):
        pass_plus(it, 0)
        pass_plus(it, 1)
        pass_plus(it, 2)
        forward(it, 0)
        forward(it, 1)
        forward(it, 2)
        window_minus(it, 0)
        window_minus(it, 1)
        window_minus(it, 2)
        adjoint(it, 0)
        adjoint(it, 1)
        adjoint(it, 2)
        pass_sums(it, 0)
        pass_sums(it, 1)
        pass_sums(it, 2)
        add_up(it, 0)
        add_up(it, 1)
        add_up(it, 2)
        window_plus(it, 0)
        window_plus(it, 1)
        window_plus(it, 2)
        finish_minus(it)
        update(it, 0)
        update(it, 1)
        update(it, 2)
        return 0

    lax.fori_loop(0, ITERS, iteration, 0)

    is_minus = any_of([place for q in range(NQ) for place in minus_places(q)])
    is_plus = any_of([place for q in range(NQ) for place in plus_places(q)])

    def drain(it, _):
        await_bytes(gath.at[it, :, pl.ds(0, NR - 1)], gath_send.at[it])
        await_bytes(gath.at[it, :, pl.ds(0, NR - 1)], rs_send.at[it])

        @pl.when(is_minus)
        def _():
            await_bytes(xm.at[it, pl.ds(0, (2 * WM - 1) * FB)], xm_send.at[it])
            await_bytes(ymsnd.at[it, pl.ds(0, NK // 2 - FB)], ym_send.at[it])

        @pl.when(jnp.logical_not(is_minus))
        def _():
            await_bytes(xm.at[it, pl.ds(0, 2 * WM * FB)], xm_send.at[it])

        @pl.when(is_plus)
        def _():
            await_bytes(xp.at[it, pl.ds(0, (WP - 1) * FB)], xp_send.at[it])
            await_bytes(ypsnd.at[it, pl.ds(0, NK - FB)], wp_send.at[it])

        @pl.when(jnp.logical_not(is_plus))
        def _():
            await_bytes(xsnd.at[it], xp_send.at[it])

        return 0

    lax.fori_loop(0, ITERS, drain, 0)


def widen(minus_ref, change_ref, plus_ref, out_minus, out_plus):
    out_minus[...] = minus_ref[...].astype(F32)
    out_plus[...] = plus_ref[...] + change_ref[...].astype(F32)


def local(reflection, plus_init, onset_receiver, onset_source):
    onm = jnp.transpose(onset_receiver)
    onp = jnp.transpose(onset_source)
    vmem = pl.BlockSpec(memory_space=pltpu.VMEM)
    hbm = pl.BlockSpec(memory_space=pl.ANY)
    dma = pltpu.SemaphoreType.DMA
    plus_rows = plus_init.reshape(2 * FB, SL * PS)
    minus, change = pl.pallas_call(
        kernel,
        out_shape=(
            jax.ShapeDtypeStruct((2 * FB, ML * PS), BF16),
            jax.ShapeDtypeStruct((2 * FB, SL * PS), BF16),
        ),
        in_specs=[hbm, hbm, hbm, vmem, vmem],
        out_specs=(vmem, vmem),
        scratch_shapes=[
            pltpu.VMEM((2 * FB, SL * PS), F32),
            pltpu.VMEM((2 * FB * ML, 1024), BF16),
            pltpu.VMEM((NG, 1024, 2 * GF * ML), BF16),
            pltpu.VMEM((NK, NK), F32),
            pltpu.VMEM((NK, NK), BF16),
            pltpu.VMEM((SL * PS, SL * PS), BF16),
            pltpu.VMEM((SL * PS, SL * PS), BF16),
            pltpu.VMEM((ML * PS, ML * PS), BF16),
            pltpu.VMEM((4 * ML, 4 * GF * ML), BF16),
            pltpu.VMEM((NQ, 8, FB, SL), F32),
            pltpu.VMEM((ITERS, NQ, NG * ROWS, SL), BF16),
            pltpu.VMEM((ITERS, NQ, NR, NG * ROWS, SL), BF16),
            pltpu.VMEM((ITERS, NQ, 2, FB, 128), BF16),
            pltpu.VMEM((ITERS, NK, 128), BF16),
            pltpu.VMEM((ITERS, NK, 128), BF16),
            pltpu.VMEM((ITERS, NQ, 2, FB, 128), BF16),
            pltpu.VMEM((2 * FB, 1024), F32),
            pltpu.VMEM((ITERS, NQ, NX, 2, 4 * ROWS, SL), BF16),
            pltpu.VMEM((ITERS, NQ, 4 * ROWS, SL), BF16),
            pltpu.VMEM((ITERS, NQ, 2, 3 * ROWS, SL), BF16),
            pltpu.VMEM((ITERS, NQ, 2, 3 * ROWS, SL), BF16),
            pltpu.VMEM((ITERS, NQ, 3, 4 * ROWS, SL), BF16),
            pltpu.VMEM((ITERS, NQ, 3, 4 * ROWS, SL), BF16),
            pltpu.VMEM((ITERS, NQ, 8, FB, SL), BF16),
            pltpu.VMEM((ITERS, NK, SL), BF16),
            pltpu.VMEM((ITERS, NK, SL), BF16),
            pltpu.VMEM((ITERS, NQ, 8, FB, SL), BF16),
            pltpu.VMEM((256, TW), BF16),
            dma((3,)),
            dma((ITERS,)), dma((ITERS, NQ, 6)),
            dma((ITERS,)), dma((ITERS,)),
            dma((ITERS,)), dma((ITERS, NQ)),
            dma((ITERS,)), dma((ITERS, NQ, 7)),
            dma((ITERS,)), dma((ITERS,)),
            dma((ITERS,)), dma((ITERS, NQ)),
        ],
        compiler_params=pltpu.CompilerParams(
            collective_id=0, has_side_effects=True, vmem_limit_bytes=56 * 1024 * 1024
        ),
    )(
        reflection.reshape(2 * FB * ML, 1024),
        jnp.asarray(tables()),
        plus_rows,
        onm,
        onp,
    )
    out_minus, out_plus = pl.pallas_call(
        widen,
        out_shape=(
            jax.ShapeDtypeStruct((2 * FB, ML * PS), F32),
            jax.ShapeDtypeStruct((2 * FB, SL * PS), F32),
        ),
        in_specs=[vmem, vmem, vmem],
        out_specs=(vmem, vmem),
    )(minus, change, plus_rows)
    return out_minus.reshape(2, FB, ML * PS), out_plus.reshape(2, FB, SL * PS)


def solution(mesh):
    return jax.shard_map(
        local,
        mesh=mesh,
        in_specs=(
            P(None, "freq", "rcv", None),
            P(None, "freq", "rcv"),
            P("rcv", None),
            P("rcv", None),
        ),
        out_specs=(P(None, "freq", "rcv"), P(None, "freq", "rcv")),
        check_vma=False,
    )
```
